512 devices in a mesh: blk: 8 (over z_hi, y), grp: 64 (over x, z_lo, core).
Axes of the slice: x: 4, y: 4, z: 16 (z_hi: 2, z_lo: 8; z = z_hi * 8 + z_lo), core: 2. Of those that a mesh axis runs over, the one named last changes fastest.
Arguments:
- image_emb: bfloat16 [12288, 1152], P('grp'), may hold values from -0.19921875 to 0.19921875
- text_emb: bfloat16 [12288, 1152], P(('blk', 'grp')), may hold values from -0.19921875 to 0.19921875
- log_temp: float32 [1], replicated, may hold values from 0.5 to 1.5
- bias: float32 [1], replicated, may hold values from -3 to -1
Outputs:
- loss: float32 [1], replicated
- grad_image: float32 [12288, 1152], P('grp', 'blk')
- grad_text: float32 [12288, 1152], P(('blk', 'grp'))
- grad_log_temp: float32 [1], replicated
- grad_bias: float32 [1], replicated
The draws below stay inside these ranges and needn't reach their ends.
All inputs are finite; a program needn't handle non-finite values.
Results may differ from the reference program's by a relative error of at most 0.0038.
The reference program's roundings to bfloat16 on the way count: a program that leaves them out, or rounds other values in their place, can miss the bound.
Values may be sent and summed in bfloat16 or wider, within the bound.
A program may use at most 64 MiB of HBM per device.

```python
import jax
import jax.numpy as jnp
from jax import lax

D = 1152
ROWS = 192
BATCH = 12288


def shard_levels(own_key, extent, cuts, least, high):
    factor_of = 1.0
    for axis_at, shards_of in cuts:
        heights = jax.random.uniform(jax.random.fold_in(jax.random.fold_in(own_key, 6), axis_at), (shards_of,), jnp.float32, least / len(cuts), high / len(cuts))
        factor_of = factor_of * jnp.repeat(jnp.exp(heights), extent[axis_at] // shards_of).reshape((-1,) + (1,) * (len(extent) - 1 - axis_at))
    return factor_of


def normal_values(stream_key, shape, deviation, most, split=(), kind=jnp.bfloat16):
    factor_of = shard_levels(stream_key, shape, split, -0.22, 0.18) if split else 1.0
    array = jax.random.normal(stream_key, shape, jnp.float32) * deviation * factor_of
    return jnp.minimum(jnp.maximum(array, -most), most).astype(kind)


def setup_inputs(seed: int = 0) -> dict:
    splits = jax.random.split(jax.random.key(seed), 5)
    return {
        "image_emb": normal_values(splits[0], (BATCH, D), 0.03, 0.19921875, ((0, 64),)),
        "text_emb": normal_values(splits[1], (BATCH, D), 0.03, 0.19921875, ((0, 512),)),
        "log_temp": jnp.clip(jax.random.uniform(splits[2], (1,), jnp.float32, 0.5, 1.5), 0.5, 1.5),
        "bias": jnp.clip(jax.random.uniform(splits[3], (1,), jnp.float32, -3.0, -1.0), -3.0, -1.0),
    }


epsilon = 1e-06

def unit_rows(embedded):
    values = embedded.astype(jnp.float32)
    inverse = lax.rsqrt(lax.optimization_barrier(jnp.sum(values * values, axis=1, keepdims=True)) + epsilon)
    return (values * inverse, inverse)

def norm_back(grad_unit, unit, inverse):
    return (grad_unit - unit * lax.optimization_barrier(jnp.sum(unit * grad_unit, axis=1, keepdims=True))) * inverse

def reference(image_emb, text_emb, log_temp, bias):
    image_unit, image_inverse = unit_rows(image_emb)
    text_unit, text_inverse = unit_rows(text_emb)
    image_bf = image_unit.astype(jnp.bfloat16)
    text_bf = text_unit.astype(jnp.bfloat16)
    scale_now = jnp.exp(log_temp[0])
    shift_now = bias[0]
    block_count = BATCH // ROWS
    image_blocks = jnp.reshape(image_bf, (block_count, ROWS, D))
    column_ids = jnp.arange(BATCH, dtype=jnp.int32)

    def scan_block(carry, inputs):
        text_total, loss_sum, dlogit_sum, weighted_sum = carry
        image_block, block_index = inputs
        similar = lax.dot_general(image_block, text_bf, (((1,), (1,)), ((), ())), preferred_element_type=jnp.float32)
        row_ids = block_index * ROWS + jnp.arange(ROWS, dtype=jnp.int32)
        labels = jnp.where(row_ids[:, None] == column_ids[None, :], jnp.float32(1.0), jnp.float32(-1.0))
        margin = -labels * (scale_now * similar + shift_now)
        dlogit = -labels * jax.nn.sigmoid(margin)
        weights_bf = (scale_now * dlogit).astype(jnp.bfloat16)
        image_part = jnp.dot(weights_bf, text_bf, preferred_element_type=jnp.float32)
        text_total = text_total + lax.dot_general(weights_bf, image_block, (((0,), (0,)), ((), ())), preferred_element_type=jnp.float32)
        loss_sum = loss_sum + jnp.sum(jax.nn.softplus(margin))
        dlogit_sum = dlogit_sum + jnp.sum(dlogit)
        weighted_sum = weighted_sum + jnp.sum(dlogit * similar)
        return ((text_total, loss_sum, dlogit_sum, weighted_sum), image_part)
    zero_scalar = jnp.zeros((), jnp.float32)
    start = (jnp.zeros((BATCH, D), jnp.float32), zero_scalar, zero_scalar, zero_scalar)
    final, image_parts = lax.scan(scan_block, start, (image_blocks, jnp.arange(block_count, dtype=jnp.int32)))
    text_unit_grad, loss_sum, dlogit_sum, weighted_sum = final
    image_unit_grad = jnp.reshape(image_parts, (BATCH, D))
    loss = loss_sum / BATCH
    grad_log_temp = scale_now * weighted_sum
    grad_image = norm_back(image_unit_grad, image_unit, image_inverse)
    grad_text = norm_back(text_unit_grad, text_unit, text_inverse)
    return (jnp.reshape(loss, (1,)), grad_image, grad_text, jnp.reshape(grad_log_temp, (1,)), jnp.reshape(dlogit_sum, (1,)))
```

```python
import functools

import jax
import jax.numpy as jnp
from jax import lax
from jax.experimental import pallas as pl
from jax.experimental.pallas import tpu as pltpu
from jax.sharding import PartitionSpec as P

MESH = pl.DeviceIdType.MESH
epsilon = 1e-06

NX, NY, NZ, ZLO = 4, 4, 16, 8
D = 1152
ROWS = 192
HALF = ROWS // 2
TEXTS = 24
COLUMNS = NZ * TEXTS
LANES = 128
TILES = D // LANES
PACKED = 224
SLOT = D // 8
BATCH = 12288
STRIDE = 2
Z_SIDES = ((-1, 8), (1, 7))
F32, BF16 = jnp.float32, jnp.bfloat16
VMEM_LIMIT = 48 * 1024 * 1024


def place():
    blk, grp = lax.axis_index("blk"), lax.axis_index("grp")
    z_hi, y = blk // NY, blk % NY
    core, z_lo, x = grp % 2, (grp // 2) % ZLO, grp // (2 * ZLO)
    return x, y, z_hi * ZLO + z_lo, core


def device(x, y, z, core):
    return ((z // ZLO) * NY + y, (x * ZLO + z % ZLO) * 2 + core)


class Peers:
    def __init__(self):
        self.x, self.y, self.z, self.core = place()

    def other_core(self):
        return device(self.x, self.y, self.z, 1 - self.core)

    def along_x(self, step):
        return device((self.x + step) % NX, self.y, self.z, self.core)

    def along_y(self, step):
        return device(self.x, (self.y + step) % NY, self.z, self.core)

    def along_z(self, step):
        return device(self.x, self.y, (self.z + step + NZ) % NZ, self.core)


class Copies:
    def __init__(self, send_sem, recv_sem):
        self.send_sem, self.recv_sem, self.made = send_sem, recv_sem, []

    def start(self, source, target, device_id):
        at = len(self.made)
        copy = pltpu.make_async_remote_copy(
            src_ref=source,
            dst_ref=target,
            send_sem=self.send_sem.at[at],
            recv_sem=self.recv_sem.at[at],
            device_id=device_id,
            device_id_type=MESH,
        )
        copy.start()
        self.made.append(copy)
        return copy

    def finish(self):
        for copy in self.made:
            copy.wait_send()


def meet(devices):
    barrier = pltpu.get_barrier_semaphore()
    for device_id in devices:
        pl.semaphore_signal(barrier, inc=1, device_id=device_id, device_id_type=MESH)
    pl.semaphore_wait(barrier, len(devices))


def hop(distance):
    return distance % STRIDE or STRIDE


def pack(rows):
    pieces = [rows[:, k * LANES : (k + 1) * LANES] for k in range(TILES)]
    pieces.append(jnp.zeros((PACKED - TILES * TEXTS, LANES), F32))
    return jnp.concatenate(pieces, axis=0)


def unpack(packed):
    return jnp.concatenate(
        [packed[k * TEXTS : (k + 1) * TEXTS, :] for k in range(TILES)], axis=1
    )


GATHER_COPIES = 3 + NX + 15


def gather_kernel(image, text, images, texts, send_sem, recv_sem, local_sem):
    peers = Peers()
    copies = Copies(send_sem, recv_sem)
    steps = sorted({step for step in range(-STRIDE, STRIDE + 1) if step})
    meet(
        [peers.other_core()]
        + [peers.along_x(step) for step in range(1, NX)]
        + [peers.along_z(step) for step in steps]
    )
    half = image.at[pl.ds(pl.multiple_of((peers.z // ZLO) * HALF, HALF), HALF)]
    own = pltpu.make_async_copy(half, images.at[0, 0], local_sem)
    own.start()
    texts[0] = pack(text[...].astype(F32)).astype(BF16)
    arriving = {}

    def spread(side, most, base):
        for far in range(min(base + STRIDE, most), base, -1):
            arriving[side, far] = copies.start(
                texts.at[(-side * base) % NZ],
                texts.at[(-side * far) % NZ],
                peers.along_z(side * (far - base)),
            )

    for side, most in Z_SIDES:
        spread(side, most, 0)
    over_x = {}
    for step in (2, 1, 3):
        over_x[NX - step] = copies.start(half, images.at[NX - step, 0], peers.along_x(step))
    over_core = [copies.start(half, images.at[0, 1], peers.other_core())]
    done = set()
    pending = [1, 3, 2]
    for base in range(STRIDE, 8, STRIDE):
        for side, most in Z_SIDES:
            if base < most:
                arriving[side, base].wait_recv()
                done.add((side, base))
                spread(side, most, base)
        if pending:
            slot = pending.pop(0)
            over_x[slot].wait_recv()
            over_core.append(
                copies.start(images.at[slot, 0], images.at[slot, 1], peers.other_core())
            )
    for slot in pending:
        over_x[slot].wait_recv()
        over_core.append(
            copies.start(images.at[slot, 0], images.at[slot, 1], peers.other_core())
        )
    for key, copy in arriving.items():
        if key not in done:
            copy.wait_recv()
    for copy in over_core:
        copy.wait_recv()
    own.wait()
    copies.finish()


def row_inverse(values):
    return lax.rsqrt(jnp.sum(values * values, axis=1, keepdims=True) + epsilon)


def compute_kernel(
    where,
    log_temp,
    bias,
    images,
    texts,
    own_grad,
    other_grad,
    text_grad,
    sums,
    text_bf,
    image_bf,
    weights,
    text_part,
):
    x, y, z, core = where[0], where[1], where[2], where[3]
    z_hi, z_lo = z // ZLO, z % ZLO
    scale = jnp.exp(jnp.full((1, 1), log_temp[0], F32))
    shift = bias[0]

    @pl.loop(0, NZ // 2)
    def _(pair):
        both = [unpack(texts[2 * pair + k].astype(F32)) for k in range(2)]
        rows = jnp.concatenate(both, axis=0)
        text_bf[pl.ds(pl.multiple_of(pair * 2 * TEXTS, 16), 2 * TEXTS), :] = (
            rows * row_inverse(rows)
        ).astype(BF16)

    column = lax.broadcasted_iota(jnp.int32, (1, COLUMNS), 1)
    block = (column * 171) >> 12
    text_z = (block + z) & (NZ - 1)
    text_ids = (
        (text_z >> 3) * (NY * BATCH // 8)
        + y * (BATCH // 8)
        + x * (ZLO * 2 * TEXTS)
        + (text_z & (ZLO - 1)) * (2 * TEXTS)
        + core * TEXTS
        + column
        - block * TEXTS
    )

    def chunk(at, carry):
        losses, dlogits, weighted = carry
        image_x = (x + at) % NX
        for k in range(2):
            raw = images[at, k].astype(F32)
            unit = raw * row_inverse(raw)
            unit_bf = unit.astype(BF16)
            rows = pl.ds(pl.multiple_of((at * 2 + k) * HALF, HALF), HALF)
            image_bf[rows, :] = unit_bf
            similar = lax.dot_general(
                unit_bf, text_bf[...], (((1,), (1,)), ((), ())), preferred_element_type=F32
            )
            image_core = core if k == 0 else 1 - core
            first = ((image_x * ZLO + z_lo) * 2 + image_core) * ROWS + z_hi * HALF
            image_ids = first + lax.broadcasted_iota(jnp.int32, (HALF, 1), 0)
            same = image_ids == text_ids
            logits = scale * similar + shift
            power = jnp.exp(jnp.where(same, -logits, logits))
            above = 1.0 + power
            chance = power / above
            dlogit = jnp.where(same, -chance, chance)
            weight = (scale * dlogit).astype(BF16)
            weights[rows, :] = weight
            grad = jnp.dot(weight, text_bf[...], preferred_element_type=F32)
            grad = grad - unit * jnp.sum(unit * grad, axis=1, keepdims=True)
            if k == 0:
                own_grad[at] = grad
            else:
                other_grad[at] = grad.astype(BF16)
            losses = losses + jnp.sum(jnp.log(above), axis=0, keepdims=True)
            dlogits = dlogits + jnp.sum(dlogit, axis=0, keepdims=True)
            weighted = weighted + jnp.sum(dlogit * similar, axis=0, keepdims=True)
        return losses, dlogits, weighted

    zero = jnp.zeros((1, COLUMNS), F32)
    parts = lax.fori_loop(0, NX, chunk, (zero, zero, zero))
    row = lax.broadcasted_iota(jnp.int32, (8, LANES), 0)
    total = jnp.zeros((8, LANES), F32)
    for k in range(3):
        part = jnp.sum(parts[k], axis=1, keepdims=True)
        total = jnp.where(row == k, part, total)
    sums[...] = total

    @pl.loop(0, COLUMNS // LANES)
    def _(at):
        lanes = pl.ds(pl.multiple_of(at * LANES, LANES), LANES)
        text_part[lanes, :] = lax.dot_general(
            weights[:, lanes],
            image_bf[...],
            (((0,), (0,)), ((), ())),
            preferred_element_type=F32,
        )

    @pl.loop(0, NZ)
    def _(j):
        text_grad[j] = pack(text_part[pl.ds(pl.multiple_of(j * TEXTS, 8), TEXTS), :])


REDUCE_COPIES = NX + 15 + 3 + 3 + 1 + 13


def reduce_kernel(
    own_grad,
    other_grad,
    text_grad,
    sums,
    image,
    text,
    grad_image,
    grad_text,
    totals,
    core_land,
    x_send,
    x_land,
    y_own,
    y_send,
    y_land,
    z_send,
    z_land,
    t_send,
    t_land,
    s_send,
    s_land,
    send_sem,
    recv_sem,
):
    peers = Peers()
    copies = Copies(send_sem, recv_sem)
    steps = sorted({s * k for s in (-1, 1) for k in (*range(1, STRIDE + 1), 1, 2, 3, 4)}) + [8]
    meet(
        [peers.other_core()]
        + [peers.along_x(step) for step in range(1, NX)]
        + [peers.along_y(step) for step in range(1, NY)]
        + [peers.along_z(step) for step in steps]
    )

    scalar = {"stage": 0, "slot": 0, "value": None}

    def scalar_send(value, to):
        stage = scalar["stage"]
        scalar["value"] = value
        s_send[stage] = value
        made = []
        for peer in to:
            slot = scalar["slot"]
            made.append((copies.start(s_send.at[stage], s_land.at[slot], peer), slot))
            scalar["slot"] += 1
        scalar["stage"] += 1
        return made

    def scalar_sum(made):
        value = scalar["value"]
        for copy, slot in made:
            copy.wait_recv()
            value = value + s_land[slot]
        return value

    index = {}
    for side, most in Z_SIDES:
        for far in range(most, 0, -1):
            index[side, far] = len(index)
    flying = {}

    def inbound(side, most, to):
        return [(side, far) for far in range(to + 1, min(to + STRIDE, most) + 1)]

    def gathered(side, most, to, value):
        for key in inbound(side, most, to):
            flying[key].wait_recv()
            value = value + t_land[index[key]].astype(F32)
        return value

    def text_send(side, far, value):
        at = index[side, far]
        t_send[at] = value.astype(BF16)
        flying[side, far] = copies.start(
            t_send.at[at], t_land.at[at], peers.along_z(side * hop(far))
        )

    def text_own(side, far):
        return text_grad[(side * far) % NZ]

    waiting = []
    for side, most in Z_SIDES:
        for far in range(most, 0, -1):
            if far % STRIDE or far == most:
                text_send(side, far, text_own(side, far))
            else:
                waiting.append((far, side, most))
    waiting.sort(key=lambda item: -item[0])
    stages = sorted({item[0] for item in waiting}, reverse=True)

    def text_stage():
        if not stages:
            return
        now = stages.pop(0)
        for far, side, most in waiting:
            if far == now:
                text_send(side, far, gathered(side, most, far, text_own(side, far)))

    over_core = {
        d: copies.start(other_grad.at[d], core_land.at[d], peers.other_core())
        for d in (2, 1, 3, 0)
    }
    made = scalar_send(sums[...], [peers.other_core()])

    over_x = []
    for d in (2, 1, 3):
        over_core[d].wait_recv()
        x_send[d - 1] = (own_grad[d] + core_land[d].astype(F32)).astype(BF16)
        over_x.append(
            (copies.start(x_send.at[d - 1], x_land.at[NX - d - 1], peers.along_x(d)), NX - d - 1)
        )
    made = scalar_send(scalar_sum(made), [peers.along_x(step) for step in range(1, NX)])
    text_stage()
    over_core[0].wait_recv()
    grad = own_grad[0] + core_land[0].astype(F32)
    made = scalar_send(scalar_sum(made), [peers.along_y(step) for step in range(1, NY)])
    for copy, slot in over_x:
        copy.wait_recv()
        grad = grad + x_land[slot].astype(F32)
    for k in range(NY):
        slots = [grad[:, (h * NY + k) * SLOT : (h * NY + k + 1) * SLOT] for h in range(2)]
        group = jnp.concatenate(slots, axis=1)
        y_own[k] = group
        y_send[k] = group.astype(BF16)
    over_y = []
    for step in (2, 1, 3):
        over_y.append(
            (
                copies.start(
                    y_send.at[(peers.y + step) % NY],
                    y_land.at[NY - step - 1],
                    peers.along_y(step),
                ),
                NY - step - 1,
            )
        )
    text_stage()
    made = scalar_send(scalar_sum(made), [peers.along_z(step) for step in (4, 8, -4)])
    grad = y_own[peers.y]
    for copy, slot in over_y:
        copy.wait_recv()
        grad = grad + y_land[slot].astype(F32)
    low, high = grad[:, :SLOT], grad[:, SLOT:]
    first = peers.z < ZLO
    z_send[...] = jnp.where(first, high, low).astype(BF16)
    over_z = copies.start(z_send, z_land, peers.along_z(ZLO))
    kept = jnp.where(first, low, high)
    text_stage()
    made = scalar_send(scalar_sum(made), [peers.along_z(step) for step in (1, 2, 3)])
    while stages:
        text_stage()

    here = pl.ds(pl.multiple_of((peers.z // ZLO) * HALF, HALF), HALF)
    there = pl.ds(pl.multiple_of((1 - peers.z // ZLO) * HALF, HALF), HALF)
    grad_image[here, :] = kept * row_inverse(image[here, :].astype(F32))
    there_inverse = row_inverse(image[there, :].astype(F32))
    text_values = text[...].astype(F32)
    text_inverse = row_inverse(text_values)
    text_unit = text_values * text_inverse

    packed = text_grad[0]
    for side, most in Z_SIDES:
        packed = gathered(side, most, 0, packed)
    text_total = unpack(packed)
    inner = jnp.sum(text_unit * text_total, axis=1, keepdims=True)
    grad_text[...] = (text_total - text_unit * inner) * text_inverse
    over_z.wait_recv()
    grad_image[there, :] = z_land[...].astype(F32) * there_inverse
    totals[...] = scalar_sum(made)
    copies.finish()


def vmem():
    return pl.BlockSpec(memory_space=pltpu.VMEM)


def smem():
    return pl.BlockSpec(memory_space=pltpu.SMEM)


def shards(image_emb, text_emb, log_temp, bias):
    images, texts = pl.pallas_call(
        gather_kernel,
        out_shape=(
            jax.ShapeDtypeStruct((NX, 2, HALF, D), BF16),
            jax.ShapeDtypeStruct((NZ, PACKED, LANES), BF16),
        ),
        in_specs=[vmem(), vmem()],
        out_specs=(vmem(), vmem()),
        scratch_shapes=[
            pltpu.SemaphoreType.DMA((GATHER_COPIES,)),
            pltpu.SemaphoreType.DMA((GATHER_COPIES,)),
            pltpu.SemaphoreType.DMA(()),
        ],
        compiler_params=pltpu.CompilerParams(
            collective_id=0, has_side_effects=True, vmem_limit_bytes=VMEM_LIMIT
        ),
    )(image_emb, text_emb)

    where = jnp.stack([jnp.int32(value) for value in place()])
    own_grad, other_grad, text_grad, sums = pl.pallas_call(
        compute_kernel,
        out_shape=(
            jax.ShapeDtypeStruct((NX, HALF, D), F32),
            jax.ShapeDtypeStruct((NX, HALF, D), BF16),
            jax.ShapeDtypeStruct((NZ, PACKED, LANES), F32),
            jax.ShapeDtypeStruct((8, LANES), F32),
        ),
        in_specs=[smem(), smem(), smem(), vmem(), vmem()],
        out_specs=(vmem(),) * 4,
        scratch_shapes=[
            pltpu.VMEM((COLUMNS, D), BF16),
            pltpu.VMEM((NX * ROWS, D), BF16),
            pltpu.VMEM((NX * ROWS, COLUMNS), BF16),
            pltpu.VMEM((COLUMNS, D), F32),
        ],
        compiler_params=pltpu.CompilerParams(vmem_limit_bytes=VMEM_LIMIT),
    )(where, log_temp, bias, images, texts)

    grad_image, grad_text, totals = pl.pallas_call(
        reduce_kernel,
        out_shape=(
            jax.ShapeDtypeStruct((ROWS, SLOT), F32),
            jax.ShapeDtypeStruct((TEXTS, D), F32),
            jax.ShapeDtypeStruct((8, LANES), F32),
        ),
        in_specs=[vmem()] * 6,
        out_specs=(vmem(),) * 3,
        scratch_shapes=[
            pltpu.VMEM((NX, HALF, D), BF16),
            pltpu.VMEM((NX - 1, HALF, D), BF16),
            pltpu.VMEM((NX - 1, HALF, D), BF16),
            pltpu.VMEM((NY, HALF, 2 * SLOT), F32),
            pltpu.VMEM((NY, HALF, 2 * SLOT), BF16),
            pltpu.VMEM((NY - 1, HALF, 2 * SLOT), BF16),
            pltpu.VMEM((HALF, SLOT), BF16),
            pltpu.VMEM((HALF, SLOT), BF16),
            pltpu.VMEM((15, PACKED, LANES), BF16),
            pltpu.VMEM((15, PACKED, LANES), BF16),
            pltpu.VMEM((5, 8, LANES), F32),
            pltpu.VMEM((13, 8, LANES), F32),
            pltpu.SemaphoreType.DMA((REDUCE_COPIES,)),
            pltpu.SemaphoreType.DMA((REDUCE_COPIES,)),
        ],
        compiler_params=pltpu.CompilerParams(
            collective_id=1, has_side_effects=True, vmem_limit_bytes=VMEM_LIMIT
        ),
    )(own_grad, other_grad, text_grad, sums, image_emb, text_emb)
    loss = totals[0, :1] / BATCH
    grad_bias = totals[1, :1]
    grad_log_temp = jnp.exp(log_temp) * totals[2, :1]
    return (loss, grad_image, grad_text, grad_log_temp, grad_bias)


def solution(mesh):
    return jax.shard_map(
        shards,
        mesh=mesh,
        in_specs=(P("grp", None), P(("blk", "grp"), None), P(), P()),
        out_specs=(P(), P("grp", "blk"), P(("blk", "grp"), None), P(), P()),
        check_vma=False,
    )
```

```python
import jax
import jax.numpy as jnp
from jax import lax
from jax.experimental import pallas as pl
from jax.experimental.pallas import tpu as pltpu
from jax.sharding import PartitionSpec as P

MESH = pl.DeviceIdType.MESH
epsilon = 1e-06

NX, NY, NZ, ZLO = 4, 4, 16, 8
D = 1152
ROWS = 192
QUARTER = ROWS // NY
IMAGES = ZLO * QUARTER
TEXTS = 24
SLOTS = NX * NY
OWN = SLOTS * TEXTS
COLUMNS = 2 * OWN
GROUP = 4 * TEXTS
LANES = 128
TILES = D // LANES
PACKED = 224
WIDE = D // 2
SLOT = D // 8
BATCH = 12288
STRIDE = 2
Z_SIDES = ((-1, 8), (1, 7))
ORDER = (0, 1, 7, 2, 6, 3, 5, 4)
NEAR = 3
COPIES = 3 + 16 + 12 + 7 + 15 + 4 + 3 + 3 + 3 + 13
F32, BF16 = jnp.float32, jnp.bfloat16
VMEM_LIMIT = 48 * 1024 * 1024


class Peers:
    def __init__(self):
        blk, grp = lax.axis_index("blk"), lax.axis_index("grp")
        z_hi, self.y = blk // NY, blk % NY
        self.core, z_lo, self.x = grp % 2, (grp // 2) % ZLO, grp // (2 * ZLO)
        self.z = z_hi * ZLO + z_lo
        self.sign = 1 - 2 * self.core

    def at(self, x, y, z, core):
        return ((z // ZLO) * NY + y, (x * ZLO + z % ZLO) * 2 + core)

    def other_core(self):
        return self.at(self.x, self.y, self.z, 1 - self.core)

    def along_x(self, step):
        return self.at((self.x + step) % NX, self.y, self.z, self.core)

    def along_y(self, step):
        return self.at(self.x, (self.y + step) % NY, self.z, self.core)

    def first_axis(self, step):
        return self.at(
            (self.x + step * (1 - self.core)) % NX,
            (self.y + step * self.core) % NY,
            self.z,
            self.core,
        )

    def second_axis(self, step):
        return self.at(
            (self.x + step * self.core) % NX,
            (self.y + step * (1 - self.core)) % NY,
            self.z,
            self.core,
        )

    def z_of(self, step):
        return (self.z + self.sign * step + NZ) % NZ

    def along_z(self, step):
        return self.at(self.x, self.y, self.z_of(step), self.core)


class Copies:
    def __init__(self, send_sem, recv_sem):
        self.send_sem, self.recv_sem, self.made = send_sem, recv_sem, []

    def start(self, source, target, device_id):
        at = len(self.made)
        copy = pltpu.make_async_remote_copy(
            src_ref=source,
            dst_ref=target,
            send_sem=self.send_sem.at[at],
            recv_sem=self.recv_sem.at[at],
            device_id=device_id,
            device_id_type=MESH,
        )
        copy.start()
        self.made.append(copy)
        return copy

    def finish(self):
        for copy in self.made:
            copy.wait_send()


def pack(rows):
    pieces = [rows[:, k * LANES : (k + 1) * LANES] for k in range(TILES)]
    pieces.append(jnp.zeros((PACKED - TILES * TEXTS, LANES), F32))
    return jnp.concatenate(pieces, axis=0)


def unpack(packed):
    return jnp.concatenate(
        [packed[k * TEXTS : (k + 1) * TEXTS, :] for k in range(TILES)], axis=1
    )


def row_inverse(values):
    return lax.rsqrt(jnp.sum(values * values, axis=1, keepdims=True) + epsilon)


def hop(distance):
    return distance % STRIDE or STRIDE


def aligned(start, size):
    return pl.ds(pl.multiple_of(start, size), size)


def kernel(
    log_temp,
    bias,
    image_in,
    text_in,
    grad_image,
    grad_text,
    totals,
    image,
    text,
    images,
    own_texts,
    other_texts,
    text_bf,
    image_bf,
    similar,
    weights,
    grads,
    halves,
    text_part,
    core_send,
    core_land,
    b_send,
    b_land,
    a_send,
    a_land,
    z_send,
    z_land,
    y_send,
    y_land,
    s_send,
    s_land,
    send_sem,
    recv_sem,
    local_sem,
):
    peers = Peers()
    copies = Copies(send_sem, recv_sem)
    x, y, z, core = peers.x, peers.y, peers.z, peers.core

    image_copy = pltpu.make_async_copy(image_in, image, local_sem.at[0])
    text_copy = pltpu.make_async_copy(text_in, text, local_sem.at[1])
    image_copy.start()
    text_copy.start()
    barrier = pltpu.get_barrier_semaphore()
    met = (
        [peers.other_core()]
        + [peers.along_x(step) for step in range(1, NX)]
        + [peers.along_y(step) for step in range(1, NY)]
        + [peers.along_z(step) for step in (-4, -3, -2, -1, 1, 2, 3, 4, 8)]
    )
    for device_id in met:
        pl.semaphore_signal(barrier, inc=1, device_id=device_id, device_id_type=MESH)
    text_copy.wait()
    own_texts[0] = pack(text[...].astype(F32)).astype(BF16)
    image_copy.wait()
    images[0] = image[aligned(y * QUARTER, QUARTER), :]
    pl.semaphore_wait(barrier, len(met))

    crossing, over_core, over_z = {}, {}, {}

    def text_forward(slot):
        over_core[slot] = copies.start(
            own_texts.at[slot], other_texts.at[slot], peers.other_core()
        )

    def text_spread(a):
        crossing[a, 1] = copies.start(own_texts.at[a], own_texts.at[4 + a], peers.second_axis(3))
        crossing[a, 3] = copies.start(own_texts.at[a], own_texts.at[12 + a], peers.second_axis(1))

    def image_forward(distance, side):
        source = (distance if side > 0 else ZLO - distance) % ZLO
        target = (distance + 1 if side > 0 else ZLO - distance - 1) % ZLO
        over_z[target] = copies.start(
            images.at[ORDER.index(source)], images.at[ORDER.index(target)], peers.along_z(-side)
        )

    crossing[1, 0] = copies.start(own_texts.at[0], own_texts.at[1], peers.first_axis(3))
    crossing[3, 0] = copies.start(own_texts.at[0], own_texts.at[3], peers.first_axis(1))
    crossing[2, 0] = copies.start(own_texts.at[0], own_texts.at[2], peers.first_axis(2))
    image_forward(0, 1)
    image_forward(0, -1)
    text_spread(0)
    text_forward(0)

    def image_ready(place):
        rows = pl.ds(place * QUARTER, QUARTER)
        values = images[place].astype(F32)
        image_bf[rows, :] = (values * row_inverse(values)).astype(BF16)

    def texts_ready(texts, b, first):
        for half in range(2):
            slot = b * 4 + 2 * half
            rows = jnp.concatenate(
                [unpack(texts[slot + k].astype(F32)) for k in range(2)], axis=0
            )
            text_bf[pl.ds(first + slot * TEXTS, 2 * TEXTS), :] = (
                rows * row_inverse(rows)
            ).astype(BF16)

    image_ready(0)
    for a in (1, 3, 2):
        crossing[a, 0].wait_recv()
        text_spread(a)
        text_forward(a)
    for target, side in ((1, 1), (7, -1)):
        over_z[target].wait_recv()
        image_forward(1, side)
    texts_ready(own_texts, 0, 0)
    image_ready(1)
    image_ready(2)
    for a in (0, 1, 3, 2):
        for b in (1, 3):
            crossing[a, b].wait_recv()
            if (b == 1) == (a in (0, 3)):
                step = 3 if b == 1 else 1
                crossing[a, 2] = copies.start(
                    own_texts.at[b * 4 + a], own_texts.at[8 + a], peers.second_axis(step)
                )
            text_forward(b * 4 + a)
    for target, side in ((2, 1), (6, -1)):
        over_z[target].wait_recv()
        image_forward(2, side)
    texts_ready(own_texts, 1, 0)
    texts_ready(own_texts, 3, 0)
    for a in (0, 1, 3, 2):
        crossing[a, 2].wait_recv()
        text_forward(8 + a)
    texts_ready(own_texts, 2, 0)
    for b in (0, 1, 3):
        for a in range(4):
            over_core[b * 4 + a].wait_recv()
        texts_ready(other_texts, b, OWN)
    over_z[3].wait_recv()
    image_forward(3, 1)
    for a in range(4):
        over_core[8 + a].wait_recv()
    texts_ready(other_texts, 2, OWN)

    scale = jnp.exp(jnp.full((1, 1), log_temp[0], F32))
    shift = bias[0]
    column = lax.broadcasted_iota(jnp.int32, (1, COLUMNS), 1)
    block = (column * 2731) >> 16
    text_core = ((block >> 4) + core) & 1
    on_first, on_second = block & 3, (block >> 2) & 3
    text_x = (x + jnp.where(text_core == 0, on_first, on_second)) & (NX - 1)
    text_y = (y + jnp.where(text_core == 0, on_second, on_first)) & (NY - 1)
    text_ids = (
        ((z // ZLO) * NY + text_y) * (BATCH // 8)
        + ((text_x * ZLO + z % ZLO) * 2 + text_core) * TEXTS
        + column
        - block * TEXTS
    )

    def weigh(place, carry):
        losses, dlogits, weighted = carry
        rows = aligned(place * QUARTER, QUARTER)
        distance = ((place + 1) // 2) * (2 * (place % 2) - 1)
        image_z = (z + peers.sign * distance + NZ) % ZLO
        first = ((x * ZLO + image_z) * 2 + core) * ROWS + y * QUARTER
        image_ids = first + lax.broadcasted_iota(jnp.int32, (QUARTER, 1), 0)
        same = image_ids == text_ids
        product = similar[rows, :]
        logits = scale * product + shift
        power = jnp.exp(jnp.where(same, -logits, logits))
        above = 1.0 + power
        chance = power / above
        dlogit = jnp.where(same, -chance, chance)
        weights[rows, :] = (scale * dlogit).astype(BF16)
        losses = losses + jnp.sum(jnp.log(above), axis=0, keepdims=True)
        dlogits = dlogits + jnp.sum(dlogit, axis=0, keepdims=True)
        weighted = weighted + jnp.sum(dlogit * product, axis=0, keepdims=True)
        return losses, dlogits, weighted

    def project(place):
        values = images[place].astype(F32)
        unit = values * row_inverse(values)
        grad = grads[aligned(place * QUARTER, QUARTER), :]
        grad = grad - unit * jnp.sum(unit * grad, axis=1, keepdims=True)
        halves[place, 0] = grad[:, :WIDE]
        halves[place, 1] = grad[:, WIDE:]

    def image_group(low, high, carry):
        rows = pl.ds(low * QUARTER, (high - low) * QUARTER)
        similar[rows, :] = lax.dot_general(
            image_bf[rows, :],
            text_bf[...],
            (((1,), (1,)), ((), ())),
            preferred_element_type=F32,
        )
        carry = lax.fori_loop(low, high, weigh, carry)
        grads[rows, :] = jnp.dot(weights[rows, :], text_bf[...], preferred_element_type=F32)
        pl.loop(low, high)(project)
        return carry

    index = {}
    for side, most in Z_SIDES:
        for far in range(most, 0, -1):
            index[side, far] = len(index)
    flying = {}

    def part(step):
        return halves[ORDER.index(step % ZLO), peers.z_of(step) // ZLO]

    def gathered(side, most, to, value):
        for far in range(to + 1, min(to + STRIDE, most) + 1):
            flying[side, far].wait_recv()
            value = value + z_land[index[side, far]].astype(F32)
        return value

    def z_stage(now):
        for far in range(now, max(now - STRIDE, 0), -1):
            for side, most in Z_SIDES:
                if far > most:
                    continue
                value = part(side * far)
                if far % STRIDE == 0:
                    value = gathered(side, most, far, value)
                at = index[side, far]
                z_send[at] = value.astype(BF16)
                flying[side, far] = copies.start(
                    z_send.at[at], z_land.at[at], peers.along_z(side * hop(far))
                )

    zero = jnp.zeros((1, COLUMNS), F32)
    carry = image_group(0, NEAR, (zero, zero, zero))
    z_stage(8)
    for target, place in ((2, 3), (6, 4), (3, 5)):
        image_ready(place)
    over_z[5].wait_recv()
    image_ready(6)
    over_z[4].wait_recv()
    image_ready(7)
    carry = image_group(NEAR, ZLO, carry)
    z_stage(6)

    scalar = {"stage": 0, "slot": 0, "value": None}

    def scalar_send(value, to):
        stage = scalar["stage"]
        scalar["value"] = value
        s_send[stage] = value
        made = []
        for peer in to:
            slot = scalar["slot"]
            made.append((copies.start(s_send.at[stage], s_land.at[slot], peer), slot))
            scalar["slot"] += 1
        scalar["stage"] += 1
        return made

    def scalar_sum(made):
        value = scalar["value"]
        for copy, slot in made:
            copy.wait_recv()
            value = value + s_land[slot]
        return value

    row = lax.broadcasted_iota(jnp.int32, (8, LANES), 0)
    total = jnp.zeros((8, LANES), F32)
    for k in range(3):
        total = jnp.where(row == k, jnp.sum(carry[k], axis=1, keepdims=True), total)
    made = scalar_send(total, [peers.other_core()])

    def text_tile(at):
        lanes = aligned(at * LANES, LANES)
        text_part[lanes, :] = lax.dot_general(
            weights[:, lanes],
            image_bf[...],
            (((0,), (0,)), ((), ())),
            preferred_element_type=F32,
        )

    pl.loop(OWN // LANES, COLUMNS // LANES)(text_tile)
    pairs = {}
    for b in (2, 1, 3, 0):
        core_send[b] = text_part[pl.ds(OWN + b * GROUP, GROUP), :].astype(BF16)
        pairs[b] = copies.start(core_send.at[b], core_land.at[b], peers.other_core())
    pl.loop(0, OWN // LANES)(text_tile)
    made = scalar_send(scalar_sum(made), [peers.along_x(step) for step in range(1, NX)])

    def pair_sum(b):
        pairs[b].wait_recv()
        return text_part[pl.ds(b * GROUP, GROUP), :] + core_land[b].astype(F32)

    across = []
    for b in (2, 1, 3):
        b_send[b - 1] = pair_sum(b).astype(BF16)
        across.append(
            (copies.start(b_send.at[b - 1], b_land.at[3 - b], peers.second_axis(b)), 3 - b)
        )
    z_stage(4)
    made = scalar_send(scalar_sum(made), [peers.along_y(step) for step in range(1, NY)])
    text_sum = pair_sum(0)
    for copy, slot in across:
        copy.wait_recv()
        text_sum = text_sum + b_land[slot].astype(F32)
    last = []
    for a in (2, 1, 3):
        a_send[a - 1] = pack(text_sum[a * TEXTS : (a + 1) * TEXTS, :]).astype(BF16)
        last.append((copies.start(a_send.at[a - 1], a_land.at[3 - a], peers.first_axis(a)), 3 - a))
    text_sum = pack(text_sum[:TEXTS, :])
    z_stage(2)
    made = scalar_send(scalar_sum(made), [peers.along_z(step) for step in (4, 8, -4)])
    text_values = text[...].astype(F32)
    text_inverse = row_inverse(text_values)
    text_unit = text_values * text_inverse
    made = scalar_send(scalar_sum(made), [peers.along_z(step) for step in (1, 2, 3)])
    quarters = [aligned(((y + k) % NY) * QUARTER, QUARTER) for k in range(NY)]
    inverses = [row_inverse(image[rows, :].astype(F32)) for rows in quarters]

    grad = part(0)
    for side, most in Z_SIDES:
        grad = gathered(side, most, 0, grad)
    for k in range(NY):
        y_send[k] = grad[:, k * SLOT : (k + 1) * SLOT]
    over_y = {}
    for step in (2, 1, 3):
        over_y[NY - step] = copies.start(
            y_send.at[(y + step) % NY], y_land.at[NY - step - 1], peers.along_y(step)
        )
    grad_image[quarters[0], :] = y_send[y] * inverses[0]

    for copy, slot in last:
        copy.wait_recv()
        text_sum = text_sum + a_land[slot].astype(F32)
    text_sum = unpack(text_sum)
    inner = jnp.sum(text_unit * text_sum, axis=1, keepdims=True)
    grad_text[...] = (text_sum - text_unit * inner) * text_inverse
    for k in range(1, NY):
        over_y[k].wait_recv()
        grad_image[quarters[k], :] = y_land[k - 1] * inverses[k]
    totals[...] = scalar_sum(made)
    copies.finish()


def shards(image_emb, text_emb, log_temp, bias):
    vmem = pl.BlockSpec(memory_space=pltpu.VMEM)
    smem = pl.BlockSpec(memory_space=pltpu.SMEM)
    anywhere = pl.BlockSpec(memory_space=pl.ANY)
    grad_image, grad_text, totals = pl.pallas_call(
        kernel,
        out_shape=(
            jax.ShapeDtypeStruct((ROWS, SLOT), F32),
            jax.ShapeDtypeStruct((TEXTS, D), F32),
            jax.ShapeDtypeStruct((8, LANES), F32),
        ),
        in_specs=[smem, smem, anywhere, anywhere],
        out_specs=(vmem,) * 3,
        scratch_shapes=[
            pltpu.VMEM((ROWS, D), BF16),
            pltpu.VMEM((TEXTS, D), BF16),
            pltpu.VMEM((ZLO, QUARTER, D), BF16),
            pltpu.VMEM((SLOTS, PACKED, LANES), BF16),
            pltpu.VMEM((SLOTS, PACKED, LANES), BF16),
            pltpu.VMEM((COLUMNS, D), BF16),
            pltpu.VMEM((IMAGES, D), BF16),
            pltpu.VMEM((IMAGES, COLUMNS), F32),
            pltpu.VMEM((IMAGES, COLUMNS), BF16),
            pltpu.VMEM((IMAGES, D), F32),
            pltpu.VMEM((ZLO, 2, QUARTER, WIDE), F32),
            pltpu.VMEM((COLUMNS, D), F32),
            pltpu.VMEM((4, GROUP, D), BF16),
            pltpu.VMEM((4, GROUP, D), BF16),
            pltpu.VMEM((3, GROUP, D), BF16),
            pltpu.VMEM((3, GROUP, D), BF16),
            pltpu.VMEM((3, PACKED, LANES), BF16),
            pltpu.VMEM((3, PACKED, LANES), BF16),
            pltpu.VMEM((15, QUARTER, WIDE), BF16),
            pltpu.VMEM((15, QUARTER, WIDE), BF16),
            pltpu.VMEM((NY, QUARTER, SLOT), F32),
            pltpu.VMEM((NY - 1, QUARTER, SLOT), F32),
            pltpu.VMEM((5, 8, LANES), F32),
            pltpu.VMEM((13, 8, LANES), F32),
            pltpu.SemaphoreType.DMA((COPIES,)),
            pltpu.SemaphoreType.DMA((COPIES,)),
            pltpu.SemaphoreType.DMA((2,)),
        ],
        compiler_params=pltpu.CompilerParams(
            collective_id=0, has_side_effects=True, vmem_limit_bytes=VMEM_LIMIT
        ),
    )(log_temp, bias, image_emb, text_emb)
    loss = totals[0, :1] / BATCH
    grad_bias = totals[1, :1]
    grad_log_temp = jnp.exp(log_temp) * totals[2, :1]
    return (loss, grad_image, grad_text, grad_log_temp, grad_bias)


def solution(mesh):
    return jax.shard_map(
        shards,
        mesh=mesh,
        in_specs=(P("grp", None), P(("blk", "grp"), None), P(), P()),
        out_specs=(P(), P("grp", "blk"), P(("blk", "grp"), None), P(), P()),
        check_vma=False,
    )
```

```python
import jax
import jax.numpy as jnp
from jax import lax
from jax.experimental import pallas as pl
from jax.experimental.pallas import tpu as pltpu
from jax.sharding import PartitionSpec as P

MESH = pl.DeviceIdType.MESH
epsilon = 1e-06

NX, NY, NZ, ZLO = 4, 4, 16, 8
D = 1152
ROWS = 192
QUARTER = ROWS // NY
IMAGES = ZLO * QUARTER
TEXTS = 24
SLOTS = NX * NY
OWN = SLOTS * TEXTS
COLUMNS = 2 * OWN
GROUP = 4 * TEXTS
LANES = 128
TILES = D // LANES
PACKED = 224
WIDE = D // 2
SLOT = D // 8
BATCH = 12288
STRIDE = 2
Z_SIDES = ((-1, 8), (1, 7))
ORDER = (0, 1, 7, 2, 6, 3, 5, 4)
NEAR = 3
COPIES = 3 + 16 + 12 + 7 + 15 + 4 + 6 + 3 + 3 + 13
F32, BF16 = jnp.float32, jnp.bfloat16
VMEM_LIMIT = 64 * 1024 * 1024 - 480 * 1024


class Peers:
    def __init__(self):
        blk, grp = lax.axis_index("blk"), lax.axis_index("grp")
        z_hi, self.y = blk // NY, blk % NY
        self.core, z_lo, self.x = grp % 2, (grp // 2) % ZLO, grp // (2 * ZLO)
        self.z = z_hi * ZLO + z_lo
        self.sign = 1 - 2 * self.core

    def at(self, x, y, z, core):
        return ((z // ZLO) * NY + y, (x * ZLO + z % ZLO) * 2 + core)

    def other_core(self):
        return self.at(self.x, self.y, self.z, 1 - self.core)

    def along_x(self, step):
        return self.at((self.x + step) % NX, self.y, self.z, self.core)

    def along_y(self, step):
        return self.at(self.x, (self.y + step) % NY, self.z, self.core)

    def first_axis(self, step):
        return self.at(
            (self.x + step * (1 - self.core)) % NX,
            (self.y + step * self.core) % NY,
            self.z,
            self.core,
        )

    def second_axis(self, step):
        return self.at(
            (self.x + step * self.core) % NX,
            (self.y + step * (1 - self.core)) % NY,
            self.z,
            self.core,
        )

    def z_of(self, step):
        return (self.z + self.sign * step + NZ) % NZ

    def along_z(self, step):
        return self.at(self.x, self.y, self.z_of(step), self.core)


class Copies:
    def __init__(self, send_sem, recv_sem):
        self.send_sem, self.recv_sem, self.made = send_sem, recv_sem, []
        self.sent = 0

    def start(self, source, target, device_id):
        at = len(self.made)
        copy = pltpu.make_async_remote_copy(
            src_ref=source,
            dst_ref=target,
            send_sem=self.send_sem.at[at],
            recv_sem=self.recv_sem.at[at],
            device_id=device_id,
            device_id_type=MESH,
        )
        copy.start()
        self.made.append(copy)
        return copy

    def finish(self):
        for copy in self.made[self.sent :]:
            copy.wait_send()
        self.sent = len(self.made)


def pack(rows):
    pieces = [rows[:, k * LANES : (k + 1) * LANES] for k in range(TILES)]
    pieces.append(jnp.zeros((PACKED - TILES * TEXTS, LANES), F32))
    return jnp.concatenate(pieces, axis=0)


def unpack(packed):
    return jnp.concatenate(
        [packed[k * TEXTS : (k + 1) * TEXTS, :] for k in range(TILES)], axis=1
    )


def row_inverse(values):
    return lax.rsqrt(jnp.sum(values * values, axis=1, keepdims=True) + epsilon)


def narrow(rows):
    pieces = [rows[8 * k : 8 * k + 8, LANES:] for k in range(QUARTER // 8)]
    pieces.append(jnp.zeros((8, LANES - (SLOT - LANES) * QUARTER // 8), F32))
    return jnp.concatenate([rows[:, :LANES], jnp.concatenate(pieces, axis=1)], axis=0)


def widen(packed):
    rest = SLOT - LANES
    pieces = [packed[QUARTER:, rest * k : rest * (k + 1)] for k in range(QUARTER // 8)]
    return jnp.concatenate([packed[:QUARTER, :], jnp.concatenate(pieces, axis=0)], axis=1)


def hop(distance):
    return distance % STRIDE or STRIDE


def aligned(start, size):
    return pl.ds(pl.multiple_of(start, size), size)


def kernel(
    log_temp_in,
    bias_in,
    image_in,
    text_in,
    grad_image,
    grad_text,
    totals,
    log_temp,
    bias,
    image,
    text,
    images,
    own_texts,
    other_texts,
    text_bf,
    image_bf,
    similar,
    weights,
    grads,
    halves,
    text_part,
    core_send,
    core_land,
    b_send,
    b_land,
    a_send,
    a_land,
    z_send,
    z_land,
    y_send,
    y_land,
    s_send,
    s_land,
    send_sem,
    recv_sem,
    local_sem,
):
    peers = Peers()
    copies = Copies(send_sem, recv_sem)
    x, y, z, core = peers.x, peers.y, peers.z, peers.core

    image_copy = pltpu.make_async_copy(image_in, image, local_sem.at[0])
    text_copy = pltpu.make_async_copy(text_in, text, local_sem.at[1])
    scalar_copies = [
        pltpu.make_async_copy(log_temp_in, log_temp, local_sem.at[2]),
        pltpu.make_async_copy(bias_in, bias, local_sem.at[3]),
    ]
    for copy in (text_copy, image_copy, *scalar_copies):
        copy.start()
    barrier = pltpu.get_barrier_semaphore()
    met = (
        [peers.other_core()]
        + [peers.along_x(step) for step in range(1, NX)]
        + [peers.along_y(step) for step in range(1, NY)]
        + [peers.along_z(step) for step in (-4, -3, -2, -1, 1, 2, 3, 4, 8)]
    )
    for device_id in met:
        pl.semaphore_signal(barrier, inc=1, device_id=device_id, device_id_type=MESH)
    text_copy.wait()
    own_texts[0] = pack(text[...].astype(F32)).astype(BF16)
    image_copy.wait()
    images[0] = image[aligned(y * QUARTER, QUARTER), :]
    for copy in scalar_copies:
        copy.wait()
    pl.semaphore_wait(barrier, len(met))

    crossing, over_core, over_z = {}, {}, {}

    def text_forward(slot):
        over_core[slot] = copies.start(
            own_texts.at[slot], other_texts.at[slot], peers.other_core()
        )

    def text_spread(a):
        crossing[a, 1] = copies.start(own_texts.at[a], own_texts.at[4 + a], peers.second_axis(3))
        crossing[a, 3] = copies.start(own_texts.at[a], own_texts.at[12 + a], peers.second_axis(1))

    def image_forward(distance, side):
        source = (distance if side > 0 else ZLO - distance) % ZLO
        target = (distance + 1 if side > 0 else ZLO - distance - 1) % ZLO
        over_z[target] = copies.start(
            images.at[ORDER.index(source)], images.at[ORDER.index(target)], peers.along_z(-side)
        )

    crossing[1, 0] = copies.start(own_texts.at[0], own_texts.at[1], peers.first_axis(3))
    crossing[3, 0] = copies.start(own_texts.at[0], own_texts.at[3], peers.first_axis(1))
    crossing[2, 0] = copies.start(own_texts.at[0], own_texts.at[2], peers.first_axis(2))
    image_forward(0, 1)
    image_forward(0, -1)
    text_spread(0)
    text_forward(0)

    def image_ready(place):
        rows = pl.ds(place * QUARTER, QUARTER)
        values = images[place].astype(F32)
        image_bf[rows, :] = (values * row_inverse(values)).astype(BF16)

    def texts_ready(texts, b, first):
        for half in range(2):
            slot = b * 4 + 2 * half
            rows = jnp.concatenate(
                [unpack(texts[slot + k].astype(F32)) for k in range(2)], axis=0
            )
            text_bf[pl.ds(first + slot * TEXTS, 2 * TEXTS), :] = (
                rows * row_inverse(rows)
            ).astype(BF16)

    image_ready(0)
    for a in (1, 3, 2):
        crossing[a, 0].wait_recv()
        text_spread(a)
        text_forward(a)
    for target, side in ((1, 1), (7, -1)):
        over_z[target].wait_recv()
        image_forward(1, side)
    texts_ready(own_texts, 0, 0)
    image_ready(1)
    image_ready(2)
    for a in (0, 1, 3, 2):
        for b in (1, 3):
            crossing[a, b].wait_recv()
            if (b == 1) == (a in (0, 3)):
                step = 3 if b == 1 else 1
                crossing[a, 2] = copies.start(
                    own_texts.at[b * 4 + a], own_texts.at[8 + a], peers.second_axis(step)
                )
            text_forward(b * 4 + a)
    for target, side in ((2, 1), (6, -1)):
        over_z[target].wait_recv()
        image_forward(2, side)
    texts_ready(own_texts, 1, 0)
    texts_ready(own_texts, 3, 0)

    def others_ready(b):
        for a in range(4):
            over_core[b * 4 + a].wait_recv()
        texts_ready(other_texts, b, OWN)

    others_ready(0)
    for a in (0, 1, 3, 2):
        crossing[a, 2].wait_recv()
        text_forward(8 + a)
    texts_ready(own_texts, 2, 0)
    over_z[3].wait_recv()
    image_forward(3, 1)
    others_ready(1)
    others_ready(3)

    scale = jnp.exp(jnp.full((1, 1), log_temp[0], F32))
    shift = bias[0]
    column = lax.broadcasted_iota(jnp.int32, (1, COLUMNS), 1)
    block = (column * 2731) >> 16
    text_core = ((block >> 4) + core) & 1
    on_first, on_second = block & 3, (block >> 2) & 3
    text_x = (x + jnp.where(text_core == 0, on_first, on_second)) & (NX - 1)
    text_y = (y + jnp.where(text_core == 0, on_second, on_first)) & (NY - 1)
    text_ids = (
        ((z // ZLO) * NY + text_y) * (BATCH // 8)
        + ((text_x * ZLO + z % ZLO) * 2 + text_core) * TEXTS
        + column
        - block * TEXTS
    )

    def weigh(low, high, lanes, carry):
        rows = pl.ds(low * QUARTER, (high - low) * QUARTER)
        similar[rows, lanes] = lax.dot_general(
            image_bf[rows, :],
            text_bf[lanes, :],
            (((1,), (1,)), ((), ())),
            preferred_element_type=F32,
        )
        ids = text_ids[:, lanes.start : lanes.start + lanes.size]

        def step(place, carry):
            losses, dlogits, weighted = carry
            rows = aligned(place * QUARTER, QUARTER)
            distance = ((place + 1) // 2) * (2 * (place % 2) - 1)
            image_z = (z + peers.sign * distance + NZ) % ZLO
            first = ((x * ZLO + image_z) * 2 + core) * ROWS + y * QUARTER
            same = first + lax.broadcasted_iota(jnp.int32, (QUARTER, 1), 0) == ids
            product = similar[rows, lanes]
            logits = scale * product + shift
            power = jnp.exp(jnp.where(same, -logits, logits))
            above = 1.0 + power
            chance = power / above
            dlogit = jnp.where(same, -chance, chance)
            weights[rows, lanes] = (scale * dlogit).astype(BF16)
            losses = losses + jnp.sum(jnp.log(above), axis=0, keepdims=True)
            dlogits = dlogits + jnp.sum(dlogit, axis=0, keepdims=True)
            weighted = weighted + jnp.sum(dlogit * product, axis=0, keepdims=True)
            return losses, dlogits, weighted

        return lax.fori_loop(low, high, step, carry)

    def project(place):
        values = images[place].astype(F32)
        unit = values * row_inverse(values)
        grad = grads[aligned(place * QUARTER, QUARTER), :]
        grad = grad - unit * jnp.sum(unit * grad, axis=1, keepdims=True)
        halves[place, 0] = grad[:, :WIDE]
        halves[place, 1] = grad[:, WIDE:]

    def image_grads(low, high):
        rows = pl.ds(low * QUARTER, (high - low) * QUARTER)
        grads[rows, :] = jnp.dot(weights[rows, :], text_bf[...], preferred_element_type=F32)
        pl.loop(low, high)(project)

    index = {}
    for side, most in Z_SIDES:
        for far in range(most, 0, -1):
            index[side, far] = len(index)
    flying = {}

    def part(step):
        return halves[ORDER.index(step % ZLO), peers.z_of(step) // ZLO]

    def gathered(side, most, to, value):
        for far in range(to + 1, min(to + STRIDE, most) + 1):
            flying[side, far].wait_recv()
            value = value + z_land[index[side, far]].astype(F32)
        return value

    def z_start(far):
        for side, most in Z_SIDES:
            if far > most:
                continue
            value = part(side * far)
            if far % STRIDE == 0:
                value = gathered(side, most, far, value)
            at = index[side, far]
            z_send[at] = value.astype(BF16)
            flying[side, far] = copies.start(
                z_send.at[at], z_land.at[at], peers.along_z(side * hop(far))
            )

    own_lanes, other_lanes = pl.ds(0, OWN), pl.ds(OWN, OWN)
    zero = jnp.zeros((1, OWN), F32)
    carry = weigh(0, NEAR, own_lanes, (zero, zero, zero))
    others_ready(2)
    carry = weigh(0, NEAR, other_lanes, carry)
    image_grads(0, NEAR)
    for far in (8, 7, 1):
        z_start(far)
    for target, place in ((2, 3), (6, 4), (3, 5)):
        image_ready(place)
    over_z[5].wait_recv()
    image_ready(6)
    over_z[4].wait_recv()
    image_ready(7)
    carry = weigh(NEAR, ZLO, other_lanes, carry)
    carry = weigh(NEAR, ZLO, own_lanes, carry)

    scalar = {"stage": 0, "slot": 0, "value": None}

    def scalar_send(value, to):
        stage = scalar["stage"]
        scalar["value"] = value
        s_send[stage] = value
        made = []
        for peer in to:
            slot = scalar["slot"]
            made.append((copies.start(s_send.at[stage], s_land.at[slot], peer), slot))
            scalar["slot"] += 1
        scalar["stage"] += 1
        return made

    def scalar_sum(made):
        value = scalar["value"]
        for copy, slot in made:
            copy.wait_recv()
            value = value + s_land[slot]
        return value

    row = lax.broadcasted_iota(jnp.int32, (8, LANES), 0)
    total = jnp.zeros((8, LANES), F32)
    for k in range(3):
        total = jnp.where(row == k, jnp.sum(carry[k], axis=1, keepdims=True), total)
    made = scalar_send(total, [peers.other_core()])

    def text_tile(at):
        lanes = aligned(at * LANES, LANES)
        text_part[lanes, :] = lax.dot_general(
            weights[:, lanes],
            image_bf[...],
            (((0,), (0,)), ((), ())),
            preferred_element_type=F32,
        )

    pl.loop(OWN // LANES, COLUMNS // LANES)(text_tile)
    pairs = {}
    for b in (2, 1, 3, 0):
        core_send[b] = text_part[pl.ds(OWN + b * GROUP, GROUP), :].astype(BF16)
        pairs[b] = copies.start(core_send.at[b], core_land.at[b], peers.other_core())
    image_grads(NEAR, ZLO)
    for far in (6, 5, 3):
        z_start(far)
    pl.loop(0, OWN // LANES)(text_tile)
    made = scalar_send(scalar_sum(made), [peers.along_x(step) for step in range(1, NX)])

    def pair_sum(b):
        pairs[b].wait_recv()
        return text_part[pl.ds(b * GROUP, GROUP), :] + core_land[b].astype(F32)

    across = {}

    def b_start(at, value, step):
        b_send[at] = value.astype(BF16)
        across[at] = copies.start(b_send.at[at], b_land.at[at], peers.second_axis(step))

    def b_landed(at):
        across[at].wait_recv()
        return b_land[at].astype(F32)

    low, high = slice(0, GROUP // 2), slice(GROUP // 2, GROUP)
    opposite = pair_sum(2)
    b_start(0, opposite[low], 1)
    b_start(1, opposite[high], 3)
    above, below = pair_sum(1), pair_sum(3)
    b_start(2, above[high], 1)
    b_start(3, below[low], 3)
    text_sum = pair_sum(0)
    z_start(4)
    b_start(4, above[low] + b_landed(0), 1)
    b_start(5, below[high] + b_landed(1), 3)
    made = scalar_send(scalar_sum(made), [peers.along_y(step) for step in range(1, NY)])
    z_start(2)
    made = scalar_send(scalar_sum(made), [peers.along_z(step) for step in (4, 8, -4)])
    text_sum = jnp.concatenate(
        [
            text_sum[low] + b_landed(3) + b_landed(4),
            text_sum[high] + b_landed(2) + b_landed(5),
        ],
        axis=0,
    )
    last = []
    for a in (2, 1, 3):
        a_send[a - 1] = pack(text_sum[a * TEXTS : (a + 1) * TEXTS, :]).astype(BF16)
        last.append((copies.start(a_send.at[a - 1], a_land.at[3 - a], peers.first_axis(a)), 3 - a))
    text_sum = pack(text_sum[:TEXTS, :])
    text_values = text[...].astype(F32)
    text_inverse = row_inverse(text_values)
    text_unit = text_values * text_inverse
    made = scalar_send(scalar_sum(made), [peers.along_z(step) for step in (1, 2, 3)])
    quarters = [aligned(((y + k) % NY) * QUARTER, QUARTER) for k in range(NY)]
    inverses = [row_inverse(image[rows, :].astype(F32)) for rows in quarters]
    copies.finish()

    grad = part(0)
    for side, most in Z_SIDES:
        grad = gathered(side, most, 0, grad)
    for k in range(NY):
        y_send[k] = narrow(grad[:, k * SLOT : (k + 1) * SLOT])
    over_y = {}
    for step in (2, 1, 3):
        over_y[NY - step] = copies.start(
            y_send.at[(y + step) % NY], y_land.at[NY - step - 1], peers.along_y(step)
        )
    grad_image[quarters[0], :] = widen(y_send[y]) * inverses[0]

    for copy, slot in last:
        copy.wait_recv()
        text_sum = text_sum + a_land[slot].astype(F32)
    text_sum = unpack(text_sum)
    inner = jnp.sum(text_unit * text_sum, axis=1, keepdims=True)
    grad_text[...] = (text_sum - text_unit * inner) * text_inverse
    for k in range(1, NY):
        over_y[k].wait_recv()
        grad_image[quarters[k], :] = widen(y_land[k - 1]) * inverses[k]
    factor = jnp.where(row == 0, 1.0 / BATCH, jnp.where(row == 2, scale, 1.0))
    totals[...] = scalar_sum(made) * factor
    copies.finish()


def shards(image_emb, text_emb, log_temp, bias):
    vmem = pl.BlockSpec(memory_space=pltpu.VMEM)
    anywhere = pl.BlockSpec(memory_space=pl.ANY)
    grad_image, grad_text, totals = pl.pallas_call(
        kernel,
        out_shape=(
            jax.ShapeDtypeStruct((ROWS, SLOT), F32),
            jax.ShapeDtypeStruct((TEXTS, D), F32),
            jax.ShapeDtypeStruct((8, LANES), F32),
        ),
        in_specs=[anywhere] * 4,
        out_specs=(vmem,) * 3,
        scratch_shapes=[
            pltpu.SMEM((1,), F32),
            pltpu.SMEM((1,), F32),
            pltpu.VMEM((ROWS, D), BF16),
            pltpu.VMEM((TEXTS, D), BF16),
            pltpu.VMEM((ZLO, QUARTER, D), BF16),
            pltpu.VMEM((SLOTS, PACKED, LANES), BF16),
            pltpu.VMEM((SLOTS, PACKED, LANES), BF16),
            pltpu.VMEM((COLUMNS, D), BF16),
            pltpu.VMEM((IMAGES, D), BF16),
            pltpu.VMEM((IMAGES, COLUMNS), F32),
            pltpu.VMEM((IMAGES, COLUMNS), BF16),
            pltpu.VMEM((IMAGES, D), F32),
            pltpu.VMEM((ZLO, 2, QUARTER, WIDE), F32),
            pltpu.VMEM((COLUMNS, D), F32),
            pltpu.VMEM((4, GROUP, D), BF16),
            pltpu.VMEM((4, GROUP, D), BF16),
            pltpu.VMEM((6, GROUP // 2, D), BF16),
            pltpu.VMEM((6, GROUP // 2, D), BF16),
            pltpu.VMEM((3, PACKED, LANES), BF16),
            pltpu.VMEM((3, PACKED, LANES), BF16),
            pltpu.VMEM((15, QUARTER, WIDE), BF16),
            pltpu.VMEM((15, QUARTER, WIDE), BF16),
            pltpu.VMEM((NY, QUARTER + 8, LANES), F32),
            pltpu.VMEM((NY - 1, QUARTER + 8, LANES), F32),
            pltpu.VMEM((5, 8, LANES), F32),
            pltpu.VMEM((13, 8, LANES), F32),
            pltpu.SemaphoreType.DMA((COPIES,)),
            pltpu.SemaphoreType.DMA((COPIES,)),
            pltpu.SemaphoreType.DMA((4,)),
        ],
        compiler_params=pltpu.CompilerParams(
            collective_id=0, has_side_effects=True, vmem_limit_bytes=VMEM_LIMIT
        ),
    )(log_temp, bias, image_emb, text_emb)
    return (totals[0, :1], grad_image, grad_text, totals[2, :1], totals[1, :1])


def solution(mesh):
    return jax.shard_map(
        shards,
        mesh=mesh,
        in_specs=(P("grp", None), P(("blk", "grp"), None), P(), P()),
        out_specs=(P(), P("grp", "blk"), P(("blk", "grp"), None), P(), P()),
        check_vma=False,
    )
```

```python
import jax
import jax.numpy as jnp
from jax import lax
from jax.experimental import pallas as pl
from jax.experimental.pallas import tpu as pltpu
from jax.sharding import PartitionSpec as P

MESH = pl.DeviceIdType.MESH
epsilon = 1e-06

NX, NY, NZ, ZLO = 4, 4, 16, 8
D = 1152
ROWS = 192
QUARTER = ROWS // NY
IMAGES = ZLO * QUARTER
TEXTS = 24
SLOTS = NX * NY
OWN = SLOTS * TEXTS
COLUMNS = 2 * OWN
GROUP = 4 * TEXTS
LANES = 128
TILES = D // LANES
PACKED = 224
WIDE = D // 2
SLOT = D // 8
BATCH = 12288
STRIDE = 2
Z_SIDES = ((-1, 8), (1, 7))
ORDER = (0, 1, 7, 2, 6, 3, 5, 4)
NEAR, MIDDLE = 3, 5
COPIES = 3 + 16 + 12 + 7 + 15 + 4 + 6 + 3 + 3 + 13
F32, BF16 = jnp.float32, jnp.bfloat16
VMEM_LIMIT = 48 * 1024 * 1024


class Peers:
    def __init__(self):
        blk, grp = lax.axis_index("blk"), lax.axis_index("grp")
        z_hi, self.y = blk // NY, blk % NY
        self.core, z_lo, self.x = grp % 2, (grp // 2) % ZLO, grp // (2 * ZLO)
        self.z = z_hi * ZLO + z_lo
        self.sign = 1 - 2 * self.core

    def at(self, x, y, z, core):
        return ((z // ZLO) * NY + y, (x * ZLO + z % ZLO) * 2 + core)

    def other_core(self):
        return self.at(self.x, self.y, self.z, 1 - self.core)

    def along_x(self, step):
        return self.at((self.x + step) % NX, self.y, self.z, self.core)

    def along_y(self, step):
        return self.at(self.x, (self.y + step) % NY, self.z, self.core)

    def first_axis(self, step):
        return self.at(
            (self.x + step * (1 - self.core)) % NX,
            (self.y + step * self.core) % NY,
            self.z,
            self.core,
        )

    def second_axis(self, step):
        return self.at(
            (self.x + step * self.core) % NX,
            (self.y + step * (1 - self.core)) % NY,
            self.z,
            self.core,
        )

    def z_of(self, step):
        return (self.z + self.sign * step + NZ) % NZ

    def along_z(self, step):
        return self.at(self.x, self.y, self.z_of(step), self.core)


class Copies:
    def __init__(self, send_sem, recv_sem):
        self.send_sem, self.recv_sem, self.made = send_sem, recv_sem, []
        self.sent = 0

    def start(self, source, target, device_id):
        at = len(self.made)
        copy = pltpu.make_async_remote_copy(
            src_ref=source,
            dst_ref=target,
            send_sem=self.send_sem.at[at],
            recv_sem=self.recv_sem.at[at],
            device_id=device_id,
            device_id_type=MESH,
        )
        copy.start()
        self.made.append(copy)
        return copy

    def finish(self):
        for copy in self.made[self.sent :]:
            copy.wait_send()
        self.sent = len(self.made)


def pack(rows):
    pieces = [rows[:, k * LANES : (k + 1) * LANES] for k in range(TILES)]
    pieces.append(jnp.zeros((PACKED - TILES * TEXTS, LANES), F32))
    return jnp.concatenate(pieces, axis=0)


def unpack(packed):
    return jnp.concatenate(
        [packed[k * TEXTS : (k + 1) * TEXTS, :] for k in range(TILES)], axis=1
    )


def row_inverse(values):
    return lax.rsqrt(jnp.sum(values * values, axis=1, keepdims=True) + epsilon)


def narrow(rows):
    pieces = [rows[8 * k : 8 * k + 8, LANES:] for k in range(QUARTER // 8)]
    pieces.append(jnp.zeros((8, LANES - (SLOT - LANES) * QUARTER // 8), F32))
    return jnp.concatenate([rows[:, :LANES], jnp.concatenate(pieces, axis=1)], axis=0)


def widen(packed):
    rest = SLOT - LANES
    pieces = [packed[QUARTER:, rest * k : rest * (k + 1)] for k in range(QUARTER // 8)]
    return jnp.concatenate([packed[:QUARTER, :], jnp.concatenate(pieces, axis=0)], axis=1)


def hop(distance):
    return distance % STRIDE or STRIDE


def aligned(start, size):
    return pl.ds(pl.multiple_of(start, size), size)


def kernel(
    log_temp_in,
    bias_in,
    image_in,
    text_in,
    grad_image,
    grad_text,
    totals,
    log_temp,
    bias,
    image,
    text,
    images,
    own_texts,
    other_texts,
    text_bf,
    image_bf,
    similar,
    weights,
    grads,
    halves,
    text_part,
    core_send,
    core_land,
    b_send,
    b_land,
    a_send,
    a_land,
    z_send,
    z_land,
    y_send,
    y_land,
    s_send,
    s_land,
    send_sem,
    recv_sem,
    local_sem,
):
    peers = Peers()
    copies = Copies(send_sem, recv_sem)
    x, y, z, core = peers.x, peers.y, peers.z, peers.core

    image_copy = pltpu.make_async_copy(image_in, image, local_sem.at[0])
    text_copy = pltpu.make_async_copy(text_in, text, local_sem.at[1])
    scalar_copies = [
        pltpu.make_async_copy(log_temp_in, log_temp, local_sem.at[2]),
        pltpu.make_async_copy(bias_in, bias, local_sem.at[3]),
    ]
    for copy in (text_copy, image_copy, *scalar_copies):
        copy.start()
    barrier = pltpu.get_barrier_semaphore()
    met = (
        [peers.other_core()]
        + [peers.along_x(step) for step in range(1, NX)]
        + [peers.along_y(step) for step in range(1, NY)]
        + [peers.along_z(step) for step in (-4, -3, -2, -1, 1, 2, 3, 4, 8)]
    )
    for device_id in met:
        pl.semaphore_signal(barrier, inc=1, device_id=device_id, device_id_type=MESH)
    text_copy.wait()
    own_texts[0] = pack(text[...].astype(F32)).astype(BF16)
    image_copy.wait()
    images[0] = image[aligned(y * QUARTER, QUARTER), :]
    for copy in scalar_copies:
        copy.wait()
    pl.semaphore_wait(barrier, len(met))

    crossing, over_core, over_z = {}, {}, {}

    def text_forward(slot):
        over_core[slot] = copies.start(
            own_texts.at[slot], other_texts.at[slot], peers.other_core()
        )

    def text_spread(a):
        crossing[a, 1] = copies.start(own_texts.at[a], own_texts.at[4 + a], peers.second_axis(3))
        crossing[a, 3] = copies.start(own_texts.at[a], own_texts.at[12 + a], peers.second_axis(1))

    def image_forward(distance, side):
        source = (distance if side > 0 else ZLO - distance) % ZLO
        target = (distance + 1 if side > 0 else ZLO - distance - 1) % ZLO
        over_z[target] = copies.start(
            images.at[ORDER.index(source)], images.at[ORDER.index(target)], peers.along_z(-side)
        )

    crossing[1, 0] = copies.start(own_texts.at[0], own_texts.at[1], peers.first_axis(3))
    crossing[3, 0] = copies.start(own_texts.at[0], own_texts.at[3], peers.first_axis(1))
    crossing[2, 0] = copies.start(own_texts.at[0], own_texts.at[2], peers.first_axis(2))
    image_forward(0, 1)
    image_forward(0, -1)
    text_spread(0)
    text_forward(0)

    def image_ready(place):
        rows = pl.ds(place * QUARTER, QUARTER)
        values = images[place].astype(F32)
        image_bf[rows, :] = (values * row_inverse(values)).astype(BF16)

    def texts_ready(texts, b, first):
        for half in range(2):
            slot = b * 4 + 2 * half
            rows = jnp.concatenate(
                [unpack(texts[slot + k].astype(F32)) for k in range(2)], axis=0
            )
            text_bf[pl.ds(first + slot * TEXTS, 2 * TEXTS), :] = (
                rows * row_inverse(rows)
            ).astype(BF16)

    image_ready(0)
    for a in (1, 3, 2):
        crossing[a, 0].wait_recv()
        text_spread(a)
        text_forward(a)
    for target, side in ((1, 1), (7, -1)):
        over_z[target].wait_recv()
        image_forward(1, side)
    texts_ready(own_texts, 0, 0)
    image_ready(1)
    image_ready(2)
    for a in (0, 1, 3, 2):
        for b in (1, 3):
            crossing[a, b].wait_recv()
            if (b == 1) == (a in (0, 3)):
                step = 3 if b == 1 else 1
                crossing[a, 2] = copies.start(
                    own_texts.at[b * 4 + a], own_texts.at[8 + a], peers.second_axis(step)
                )
            text_forward(b * 4 + a)
    for target, side in ((2, 1), (6, -1)):
        over_z[target].wait_recv()
        image_forward(2, side)
    texts_ready(own_texts, 1, 0)
    texts_ready(own_texts, 3, 0)

    def others_ready(b):
        for a in range(4):
            over_core[b * 4 + a].wait_recv()
        texts_ready(other_texts, b, OWN)

    others_ready(0)
    for a in (0, 1, 3, 2):
        crossing[a, 2].wait_recv()
        text_forward(8 + a)
    texts_ready(own_texts, 2, 0)
    others_ready(1)
    others_ready(3)

    scale = jnp.exp(jnp.full((1, 1), log_temp[0], F32))
    shift = bias[0]
    column = lax.broadcasted_iota(jnp.int32, (1, COLUMNS), 1)
    block = (column * 2731) >> 16
    text_core = ((block >> 4) + core) & 1
    on_first, on_second = block & 3, (block >> 2) & 3
    text_x = (x + jnp.where(text_core == 0, on_first, on_second)) & (NX - 1)
    text_y = (y + jnp.where(text_core == 0, on_second, on_first)) & (NY - 1)
    text_ids = (
        ((z // ZLO) * NY + text_y) * (BATCH // 8)
        + ((text_x * ZLO + z % ZLO) * 2 + text_core) * TEXTS
        + column
        - block * TEXTS
    )

    def weigh(low, high, lanes, carry):
        rows = pl.ds(low * QUARTER, (high - low) * QUARTER)
        similar[rows, lanes] = lax.dot_general(
            image_bf[rows, :],
            text_bf[lanes, :],
            (((1,), (1,)), ((), ())),
            preferred_element_type=F32,
        )
        ids = text_ids[:, lanes.start : lanes.start + lanes.size]

        def step(place, carry):
            losses, dlogits, weighted = carry
            rows = aligned(place * QUARTER, QUARTER)
            distance = ((place + 1) // 2) * (2 * (place % 2) - 1)
            image_z = (z + peers.sign * distance + NZ) % ZLO
            first = ((x * ZLO + image_z) * 2 + core) * ROWS + y * QUARTER
            same = first + lax.broadcasted_iota(jnp.int32, (QUARTER, 1), 0) == ids
            product = similar[rows, lanes]
            logits = scale * product + shift
            power = jnp.exp(jnp.where(same, -logits, logits))
            above = 1.0 + power
            chance = power / above
            dlogit = jnp.where(same, -chance, chance)
            weights[rows, lanes] = (scale * dlogit).astype(BF16)
            losses = losses + jnp.sum(jnp.log(above), axis=0, keepdims=True)
            dlogits = dlogits + jnp.sum(dlogit, axis=0, keepdims=True)
            weighted = weighted + jnp.sum(dlogit * product, axis=0, keepdims=True)
            return losses, dlogits, weighted

        return lax.fori_loop(low, high, step, carry)

    def project(place):
        values = images[place].astype(F32)
        unit = values * row_inverse(values)
        grad = grads[aligned(place * QUARTER, QUARTER), :]
        grad = grad - unit * jnp.sum(unit * grad, axis=1, keepdims=True)
        halves[place, 0] = grad[:, :WIDE]
        halves[place, 1] = grad[:, WIDE:]

    def image_grads(low, high):
        rows = pl.ds(low * QUARTER, (high - low) * QUARTER)
        grads[rows, :] = jnp.dot(weights[rows, :], text_bf[...], preferred_element_type=F32)
        pl.loop(low, high)(project)

    index = {}
    for side, most in Z_SIDES:
        for far in range(most, 0, -1):
            index[side, far] = len(index)
    flying = {}

    def part(step):
        return halves[ORDER.index(step % ZLO), peers.z_of(step) // ZLO]

    def gathered(side, most, to, value):
        for far in range(to + 1, min(to + STRIDE, most) + 1):
            flying[side, far].wait_recv()
            value = value + z_land[index[side, far]].astype(F32)
        return value

    def z_start(far):
        for side, most in Z_SIDES:
            if far > most:
                continue
            value = part(side * far)
            if far % STRIDE == 0:
                value = gathered(side, most, far, value)
            at = index[side, far]
            z_send[at] = value.astype(BF16)
            flying[side, far] = copies.start(
                z_send.at[at], z_land.at[at], peers.along_z(side * hop(far))
            )

    own_lanes, other_lanes = pl.ds(0, OWN), pl.ds(OWN, OWN)
    zero = jnp.zeros((1, OWN), F32)
    carry = weigh(0, NEAR, own_lanes, (zero, zero, zero))
    others_ready(2)
    carry = weigh(0, NEAR, other_lanes, carry)
    image_grads(0, NEAR)
    for far in (8, 7, 1):
        z_start(far)
    over_z[3].wait_recv()
    image_forward(3, 1)
    image_ready(3)
    image_ready(4)
    carry = weigh(NEAR, MIDDLE, other_lanes, carry)
    carry = weigh(NEAR, MIDDLE, own_lanes, carry)
    image_grads(NEAR, MIDDLE)
    image_ready(5)
    over_z[5].wait_recv()
    image_ready(6)
    over_z[4].wait_recv()
    image_ready(7)
    carry = weigh(MIDDLE, ZLO, other_lanes, carry)
    z_start(6)
    carry = weigh(MIDDLE, ZLO, own_lanes, carry)

    scalar = {"stage": 0, "slot": 0, "value": None}

    def scalar_send(value, to):
        stage = scalar["stage"]
        scalar["value"] = value
        s_send[stage] = value
        made = []
        for peer in to:
            slot = scalar["slot"]
            made.append((copies.start(s_send.at[stage], s_land.at[slot], peer), slot))
            scalar["slot"] += 1
        scalar["stage"] += 1
        return made

    def scalar_sum(made):
        value = scalar["value"]
        for copy, slot in made:
            copy.wait_recv()
            value = value + s_land[slot]
        return value

    row = lax.broadcasted_iota(jnp.int32, (8, LANES), 0)
    total = jnp.zeros((8, LANES), F32)
    for k in range(3):
        total = jnp.where(row == k, jnp.sum(carry[k], axis=1, keepdims=True), total)
    made = scalar_send(total, [peers.other_core()])

    def text_tile(at):
        lanes = aligned(at * LANES, LANES)
        text_part[lanes, :] = lax.dot_general(
            weights[:, lanes],
            image_bf[...],
            (((0,), (0,)), ((), ())),
            preferred_element_type=F32,
        )

    pl.loop(OWN // LANES, COLUMNS // LANES)(text_tile)
    pairs = {}
    for b in (2, 1, 3, 0):
        core_send[b] = text_part[pl.ds(OWN + b * GROUP, GROUP), :].astype(BF16)
        pairs[b] = copies.start(core_send.at[b], core_land.at[b], peers.other_core())
    image_grads(MIDDLE, ZLO)
    z_start(5)
    z_start(3)
    pl.loop(0, OWN // LANES)(text_tile)
    made = scalar_send(scalar_sum(made), [peers.along_x(step) for step in range(1, NX)])

    def pair_sum(b):
        pairs[b].wait_recv()
        return text_part[pl.ds(b * GROUP, GROUP), :] + core_land[b].astype(F32)

    across = {}

    def b_start(at, value, step):
        b_send[at] = value.astype(BF16)
        across[at] = copies.start(b_send.at[at], b_land.at[at], peers.second_axis(step))

    def b_landed(at):
        across[at].wait_recv()
        return b_land[at].astype(F32)

    low, high = slice(0, GROUP // 2), slice(GROUP // 2, GROUP)
    opposite = pair_sum(2)
    b_start(0, opposite[low], 1)
    b_start(1, opposite[high], 3)
    above, below = pair_sum(1), pair_sum(3)
    b_start(2, above[high], 1)
    b_start(3, below[low], 3)
    text_sum = pair_sum(0)
    z_start(4)
    b_start(4, above[low] + b_landed(0), 1)
    b_start(5, below[high] + b_landed(1), 3)
    made = scalar_send(scalar_sum(made), [peers.along_y(step) for step in range(1, NY)])
    z_start(2)
    made = scalar_send(scalar_sum(made), [peers.along_z(step) for step in (4, 8, -4)])
    text_sum = jnp.concatenate(
        [
            text_sum[low] + b_landed(3) + b_landed(4),
            text_sum[high] + b_landed(2) + b_landed(5),
        ],
        axis=0,
    )
    last = []
    for a in (2, 1, 3):
        a_send[a - 1] = pack(text_sum[a * TEXTS : (a + 1) * TEXTS, :]).astype(BF16)
        last.append((copies.start(a_send.at[a - 1], a_land.at[3 - a], peers.first_axis(a)), 3 - a))
    text_sum = pack(text_sum[:TEXTS, :])
    text_values = text[...].astype(F32)
    text_inverse = row_inverse(text_values)
    text_unit = text_values * text_inverse
    made = scalar_send(scalar_sum(made), [peers.along_z(step) for step in (1, 2, 3)])
    quarters = [aligned(((y + k) % NY) * QUARTER, QUARTER) for k in range(NY)]
    inverses = [row_inverse(image[rows, :].astype(F32)) for rows in quarters]
    copies.finish()

    grad = part(0)
    for side, most in Z_SIDES:
        grad = gathered(side, most, 0, grad)
    for k in range(NY):
        y_send[k] = narrow(grad[:, k * SLOT : (k + 1) * SLOT])
    over_y = {}
    for step in (2, 1, 3):
        over_y[NY - step] = copies.start(
            y_send.at[(y + step) % NY], y_land.at[NY - step - 1], peers.along_y(step)
        )
    grad_image[quarters[0], :] = widen(y_send[y]) * inverses[0]

    for copy, slot in last:
        copy.wait_recv()
        text_sum = text_sum + a_land[slot].astype(F32)
    text_sum = unpack(text_sum)
    inner = jnp.sum(text_unit * text_sum, axis=1, keepdims=True)
    grad_text[...] = (text_sum - text_unit * inner) * text_inverse
    for k in range(1, NY):
        over_y[k].wait_recv()
        grad_image[quarters[k], :] = widen(y_land[k - 1]) * inverses[k]
    factor = jnp.where(row == 0, 1.0 / BATCH, jnp.where(row == 2, scale, 1.0))
    totals[...] = scalar_sum(made) * factor
    copies.finish()


def shards(image_emb, text_emb, log_temp, bias):
    vmem = pl.BlockSpec(memory_space=pltpu.VMEM)
    anywhere = pl.BlockSpec(memory_space=pl.ANY)
    grad_image, grad_text, totals = pl.pallas_call(
        kernel,
        out_shape=(
            jax.ShapeDtypeStruct((ROWS, SLOT), F32),
            jax.ShapeDtypeStruct((TEXTS, D), F32),
            jax.ShapeDtypeStruct((8, LANES), F32),
        ),
        in_specs=[anywhere] * 4,
        out_specs=(vmem,) * 3,
        scratch_shapes=[
            pltpu.SMEM((1,), F32),
            pltpu.SMEM((1,), F32),
            pltpu.VMEM((ROWS, D), BF16),
            pltpu.VMEM((TEXTS, D), BF16),
            pltpu.VMEM((ZLO, QUARTER, D), BF16),
            pltpu.VMEM((SLOTS, PACKED, LANES), BF16),
            pltpu.VMEM((SLOTS, PACKED, LANES), BF16),
            pltpu.VMEM((COLUMNS, D), BF16),
            pltpu.VMEM((IMAGES, D), BF16),
            pltpu.VMEM((IMAGES, COLUMNS), F32),
            pltpu.VMEM((IMAGES, COLUMNS), BF16),
            pltpu.VMEM((IMAGES, D), F32),
            pltpu.VMEM((ZLO, 2, QUARTER, WIDE), F32),
            pltpu.VMEM((COLUMNS, D), F32),
            pltpu.VMEM((4, GROUP, D), BF16),
            pltpu.VMEM((4, GROUP, D), BF16),
            pltpu.VMEM((6, GROUP // 2, D), BF16),
            pltpu.VMEM((6, GROUP // 2, D), BF16),
            pltpu.VMEM((3, PACKED, LANES), BF16),
            pltpu.VMEM((3, PACKED, LANES), BF16),
            pltpu.VMEM((15, QUARTER, WIDE), BF16),
            pltpu.VMEM((15, QUARTER, WIDE), BF16),
            pltpu.VMEM((NY, QUARTER + 8, LANES), F32),
            pltpu.VMEM((NY - 1, QUARTER + 8, LANES), F32),
            pltpu.VMEM((5, 8, LANES), F32),
            pltpu.VMEM((13, 8, LANES), F32),
            pltpu.SemaphoreType.DMA((COPIES,)),
            pltpu.SemaphoreType.DMA((COPIES,)),
            pltpu.SemaphoreType.DMA((4,)),
        ],
        compiler_params=pltpu.CompilerParams(
            collective_id=0, has_side_effects=True, vmem_limit_bytes=VMEM_LIMIT
        ),
    )(log_temp, bias, image_emb, text_emb)
    return (totals[0, :1], grad_image, grad_text, totals[2, :1], totals[1, :1])


def solution(mesh):
    return jax.shard_map(
        shards,
        mesh=mesh,
        in_specs=(P("grp", None), P(("blk", "grp"), None), P(), P()),
        out_specs=(P(), P("grp", "blk"), P(("blk", "grp"), None), P(), P()),
        check_vma=False,
    )
```

```python
import jax
import jax.numpy as jnp
from jax import lax
from jax.experimental import pallas as pl
from jax.experimental.pallas import tpu as pltpu
from jax.sharding import PartitionSpec as P

MESH = pl.DeviceIdType.MESH
epsilon = 1e-06

NX, NY, NZ, ZLO = 4, 4, 16, 8
D = 1152
ROWS = 192
QUARTER = ROWS // NY
IMAGES = ZLO * QUARTER
TEXTS = 24
SLOTS = NX * NY
OWN = SLOTS * TEXTS
COLUMNS = 2 * OWN
GROUP = 4 * TEXTS
LANES = 128
TILES = D // LANES
PACKED = 224
WIDE = D // 2
SLOT = D // 8
BATCH = 12288
STRIDE = 2
Z_SIDES = ((-1, 8), (1, 7))
ORDER = (0, 1, 7, 2, 6, 3, 5, 4)
NEAR, MIDDLE = 3, 5
COPIES = 3 + 16 + 12 + 7 + 15 + 4 + 6 + 3 + 3 + 13
F32, BF16 = jnp.float32, jnp.bfloat16
VMEM_LIMIT = 48 * 1024 * 1024


class Peers:
    def __init__(self):
        blk, grp = lax.axis_index("blk"), lax.axis_index("grp")
        z_hi, self.y = blk // NY, blk % NY
        self.core, z_lo, self.x = grp % 2, (grp // 2) % ZLO, grp // (2 * ZLO)
        self.z = z_hi * ZLO + z_lo
        self.sign = 1 - 2 * self.core

    def at(self, x, y, z, core):
        return ((z // ZLO) * NY + y, (x * ZLO + z % ZLO) * 2 + core)

    def other_core(self):
        return self.at(self.x, self.y, self.z, 1 - self.core)

    def along_x(self, step):
        return self.at((self.x + step) % NX, self.y, self.z, self.core)

    def along_y(self, step):
        return self.at(self.x, (self.y + step) % NY, self.z, self.core)

    def first_axis(self, step):
        return self.at(
            (self.x + step * (1 - self.core)) % NX,
            (self.y + step * self.core) % NY,
            self.z,
            self.core,
        )

    def second_axis(self, step):
        return self.at(
            (self.x + step * self.core) % NX,
            (self.y + step * (1 - self.core)) % NY,
            self.z,
            self.core,
        )

    def z_of(self, step):
        return (self.z + self.sign * step + NZ) % NZ

    def along_z(self, step):
        return self.at(self.x, self.y, self.z_of(step), self.core)


class Copies:
    def __init__(self, send_sem, recv_sem):
        self.send_sem, self.recv_sem, self.made = send_sem, recv_sem, []
        self.sent = 0

    def start(self, source, target, device_id):
        at = len(self.made)
        copy = pltpu.make_async_remote_copy(
            src_ref=source,
            dst_ref=target,
            send_sem=self.send_sem.at[at],
            recv_sem=self.recv_sem.at[at],
            device_id=device_id,
            device_id_type=MESH,
        )
        copy.start()
        self.made.append(copy)
        return copy

    def finish(self):
        for copy in self.made[self.sent :]:
            copy.wait_send()
        self.sent = len(self.made)


def pack(rows):
    pieces = [rows[:, k * LANES : (k + 1) * LANES] for k in range(TILES)]
    pieces.append(jnp.zeros((PACKED - TILES * TEXTS, LANES), F32))
    return jnp.concatenate(pieces, axis=0)


def unpack(packed):
    return jnp.concatenate(
        [packed[k * TEXTS : (k + 1) * TEXTS, :] for k in range(TILES)], axis=1
    )


def row_inverse(values):
    return lax.rsqrt(jnp.sum(values * values, axis=1, keepdims=True) + epsilon)


def narrow(rows):
    pieces = [rows[8 * k : 8 * k + 8, LANES:] for k in range(QUARTER // 8)]
    pieces.append(jnp.zeros((8, LANES - (SLOT - LANES) * QUARTER // 8), F32))
    return jnp.concatenate([rows[:, :LANES], jnp.concatenate(pieces, axis=1)], axis=0)


def widen(packed):
    rest = SLOT - LANES
    pieces = [packed[QUARTER:, rest * k : rest * (k + 1)] for k in range(QUARTER // 8)]
    return jnp.concatenate([packed[:QUARTER, :], jnp.concatenate(pieces, axis=0)], axis=1)


def hop(distance):
    return distance % STRIDE or STRIDE


def aligned(start, size):
    return pl.ds(pl.multiple_of(start, size), size)


def kernel(
    log_temp_in,
    bias_in,
    image_in,
    text_in,
    grad_image,
    grad_text,
    totals,
    log_temp,
    bias,
    image,
    text,
    images,
    own_texts,
    other_texts,
    text_bf,
    image_bf,
    similar,
    weights,
    grads,
    halves,
    text_part,
    core_send,
    core_land,
    b_send,
    b_land,
    a_send,
    a_land,
    z_send,
    z_land,
    y_send,
    y_land,
    s_send,
    s_land,
    send_sem,
    recv_sem,
    local_sem,
):
    peers = Peers()
    copies = Copies(send_sem, recv_sem)
    x, y, z, core = peers.x, peers.y, peers.z, peers.core

    image_copy = pltpu.make_async_copy(image_in, image, local_sem.at[0])
    text_copy = pltpu.make_async_copy(text_in, text, local_sem.at[1])
    scalar_copies = [
        pltpu.make_async_copy(log_temp_in, log_temp, local_sem.at[2]),
        pltpu.make_async_copy(bias_in, bias, local_sem.at[3]),
    ]
    for copy in (text_copy, image_copy, *scalar_copies):
        copy.start()
    barrier = pltpu.get_barrier_semaphore()
    met = (
        [peers.other_core()]
        + [peers.along_x(step) for step in range(1, NX)]
        + [peers.along_y(step) for step in range(1, NY)]
        + [peers.along_z(step) for step in (-4, -3, -2, -1, 1, 2, 3, 4, 8)]
    )
    for device_id in met:
        pl.semaphore_signal(barrier, inc=1, device_id=device_id, device_id_type=MESH)
    text_copy.wait()
    own_texts[0] = pack(text[...].astype(F32)).astype(BF16)
    image_copy.wait()
    images[0] = image[aligned(y * QUARTER, QUARTER), :]
    for copy in scalar_copies:
        copy.wait()
    pl.semaphore_wait(barrier, len(met))

    crossing, over_core, over_z = {}, {}, {}

    def text_forward(slot):
        over_core[slot] = copies.start(
            own_texts.at[slot], other_texts.at[slot], peers.other_core()
        )

    def text_spread(a):
        crossing[a, 1] = copies.start(own_texts.at[a], own_texts.at[4 + a], peers.second_axis(3))
        crossing[a, 3] = copies.start(own_texts.at[a], own_texts.at[12 + a], peers.second_axis(1))

    def image_forward(distance, side):
        source = (distance if side > 0 else ZLO - distance) % ZLO
        target = (distance + 1 if side > 0 else ZLO - distance - 1) % ZLO
        over_z[target] = copies.start(
            images.at[ORDER.index(source)], images.at[ORDER.index(target)], peers.along_z(-side)
        )

    crossing[1, 0] = copies.start(own_texts.at[0], own_texts.at[1], peers.first_axis(3))
    crossing[3, 0] = copies.start(own_texts.at[0], own_texts.at[3], peers.first_axis(1))
    crossing[2, 0] = copies.start(own_texts.at[0], own_texts.at[2], peers.first_axis(2))
    image_forward(0, 1)
    image_forward(0, -1)
    text_spread(0)
    text_forward(0)

    def image_ready(place):
        rows = pl.ds(place * QUARTER, QUARTER)
        values = images[place].astype(F32)
        image_bf[rows, :] = (values * row_inverse(values)).astype(BF16)

    def texts_ready(texts, b, first):
        for half in range(2):
            slot = b * 4 + 2 * half
            rows = jnp.concatenate(
                [unpack(texts[slot + k].astype(F32)) for k in range(2)], axis=0
            )
            text_bf[pl.ds(first + slot * TEXTS, 2 * TEXTS), :] = (
                rows * row_inverse(rows)
            ).astype(BF16)

    image_ready(0)
    for a in (1, 3, 2):
        crossing[a, 0].wait_recv()
        text_spread(a)
        text_forward(a)
    for target, side in ((1, 1), (7, -1)):
        over_z[target].wait_recv()
        image_forward(1, side)
    texts_ready(own_texts, 0, 0)
    image_ready(1)
    image_ready(2)
    for a in (0, 1, 3, 2):
        for b in (1, 3):
            crossing[a, b].wait_recv()
            if (b == 1) == (a in (0, 3)):
                step = 3 if b == 1 else 1
                crossing[a, 2] = copies.start(
                    own_texts.at[b * 4 + a], own_texts.at[8 + a], peers.second_axis(step)
                )
            text_forward(b * 4 + a)
    for target, side in ((2, 1), (6, -1)):
        over_z[target].wait_recv()
        image_forward(2, side)
    texts_ready(own_texts, 1, 0)
    texts_ready(own_texts, 3, 0)

    def others_ready(b):
        for a in range(4):
            over_core[b * 4 + a].wait_recv()
        texts_ready(other_texts, b, OWN)

    others_ready(0)
    for a in (0, 1, 3, 2):
        crossing[a, 2].wait_recv()
        text_forward(8 + a)
    texts_ready(own_texts, 2, 0)
    others_ready(1)
    others_ready(3)

    scale = jnp.exp(jnp.full((1, 1), log_temp[0], F32))
    shift = bias[0]
    column = lax.broadcasted_iota(jnp.int32, (1, COLUMNS), 1)
    block = (column * 2731) >> 16
    text_core = ((block >> 4) + core) & 1
    on_first, on_second = block & 3, (block >> 2) & 3
    text_x = (x + jnp.where(text_core == 0, on_first, on_second)) & (NX - 1)
    text_y = (y + jnp.where(text_core == 0, on_second, on_first)) & (NY - 1)
    text_ids = (
        ((z // ZLO) * NY + text_y) * (BATCH // 8)
        + ((text_x * ZLO + z % ZLO) * 2 + text_core) * TEXTS
        + column
        - block * TEXTS
    )

    def weigh(low, high, lanes, carry):
        rows = pl.ds(low * QUARTER, (high - low) * QUARTER)
        similar[rows, lanes] = lax.dot_general(
            image_bf[rows, :],
            text_bf[lanes, :],
            (((1,), (1,)), ((), ())),
            preferred_element_type=F32,
        )
        ids = text_ids[:, lanes.start : lanes.start + lanes.size]

        def step(place, carry):
            losses, dlogits, weighted = carry
            rows = aligned(place * QUARTER, QUARTER)
            distance = ((place + 1) // 2) * (2 * (place % 2) - 1)
            image_z = (z + peers.sign * distance + NZ) % ZLO
            first = ((x * ZLO + image_z) * 2 + core) * ROWS + y * QUARTER
            same = first + lax.broadcasted_iota(jnp.int32, (QUARTER, 1), 0) == ids
            product = similar[rows, lanes]
            logits = scale * product + shift
            power = jnp.exp(jnp.where(same, -logits, logits))
            above = 1.0 + power
            chance = power / above
            dlogit = jnp.where(same, -chance, chance)
            weights[rows, lanes] = (scale * dlogit).astype(BF16)
            losses = losses + jnp.sum(jnp.log(above), axis=0, keepdims=True)
            dlogits = dlogits + jnp.sum(dlogit, axis=0, keepdims=True)
            weighted = weighted + jnp.sum(dlogit * product, axis=0, keepdims=True)
            return losses, dlogits, weighted

        return lax.fori_loop(low, high, step, carry)

    def project(place):
        values = images[place].astype(F32)
        unit = values * row_inverse(values)
        grad = grads[aligned(place * QUARTER, QUARTER), :]
        grad = grad - unit * jnp.sum(unit * grad, axis=1, keepdims=True)
        halves[place, 0] = grad[:, :WIDE]
        halves[place, 1] = grad[:, WIDE:]

    def image_grads(low, high):
        rows = pl.ds(low * QUARTER, (high - low) * QUARTER)
        grads[rows, :] = jnp.dot(weights[rows, :], text_bf[...], preferred_element_type=F32)
        pl.loop(low, high)(project)

    index = {}
    for side, most in Z_SIDES:
        for far in range(most, 0, -1):
            index[side, far] = len(index)
    flying = {}

    def part(step):
        return halves[ORDER.index(step % ZLO), peers.z_of(step) // ZLO]

    def gathered(side, most, to, value):
        for far in range(to + 1, min(to + STRIDE, most) + 1):
            flying[side, far].wait_recv()
            value = value + z_land[index[side, far]].astype(F32)
        return value

    def z_start(far):
        for side, most in Z_SIDES:
            if far > most:
                continue
            value = part(side * far)
            if far % STRIDE == 0:
                value = gathered(side, most, far, value)
            at = index[side, far]
            z_send[at] = value.astype(BF16)
            flying[side, far] = copies.start(
                z_send.at[at], z_land.at[at], peers.along_z(side * hop(far))
            )

    own_lanes, other_lanes = pl.ds(0, OWN), pl.ds(OWN, OWN)
    zero = jnp.zeros((1, OWN), F32)
    carry = weigh(0, NEAR, own_lanes, (zero, zero, zero))
    over_z[3].wait_recv()
    image_forward(3, 1)
    others_ready(2)
    carry = weigh(0, NEAR, other_lanes, carry)
    image_grads(0, NEAR)
    for far in (8, 7, 1):
        z_start(far)
    image_ready(3)
    image_ready(4)
    carry = weigh(NEAR, MIDDLE, other_lanes, carry)
    carry = weigh(NEAR, MIDDLE, own_lanes, carry)
    image_grads(NEAR, MIDDLE)
    z_start(6)
    image_ready(5)
    over_z[5].wait_recv()
    image_ready(6)
    over_z[4].wait_recv()
    image_ready(7)
    carry = weigh(MIDDLE, ZLO, other_lanes, carry)
    carry = weigh(MIDDLE, ZLO, own_lanes, carry)
    image_grads(MIDDLE, ZLO)
    z_start(5)
    z_start(3)

    scalar = {"stage": 0, "slot": 0, "value": None}

    def scalar_send(value, to):
        stage = scalar["stage"]
        scalar["value"] = value
        s_send[stage] = value
        made = []
        for peer in to:
            slot = scalar["slot"]
            made.append((copies.start(s_send.at[stage], s_land.at[slot], peer), slot))
            scalar["slot"] += 1
        scalar["stage"] += 1
        return made

    def scalar_sum(made):
        value = scalar["value"]
        for copy, slot in made:
            copy.wait_recv()
            value = value + s_land[slot]
        return value

    row = lax.broadcasted_iota(jnp.int32, (8, LANES), 0)
    total = jnp.zeros((8, LANES), F32)
    for k in range(3):
        total = jnp.where(row == k, jnp.sum(carry[k], axis=1, keepdims=True), total)
    made = scalar_send(total, [peers.other_core()])

    def text_tile(at):
        lanes = aligned(at * LANES, LANES)
        text_part[lanes, :] = lax.dot_general(
            weights[:, lanes],
            image_bf[...],
            (((0,), (0,)), ((), ())),
            preferred_element_type=F32,
        )

    pl.loop(OWN // LANES, COLUMNS // LANES)(text_tile)
    pairs = {}
    for b in (2, 1, 3, 0):
        core_send[b] = text_part[pl.ds(OWN + b * GROUP, GROUP), :].astype(BF16)
        pairs[b] = copies.start(core_send.at[b], core_land.at[b], peers.other_core())
    pl.loop(0, OWN // LANES)(text_tile)
    made = scalar_send(scalar_sum(made), [peers.along_x(step) for step in range(1, NX)])

    def pair_sum(b):
        pairs[b].wait_recv()
        return text_part[pl.ds(b * GROUP, GROUP), :] + core_land[b].astype(F32)

    across = {}

    def b_start(at, value, step):
        b_send[at] = value.astype(BF16)
        across[at] = copies.start(b_send.at[at], b_land.at[at], peers.second_axis(step))

    def b_landed(at):
        across[at].wait_recv()
        return b_land[at].astype(F32)

    low, high = slice(0, GROUP // 2), slice(GROUP // 2, GROUP)
    opposite = pair_sum(2)
    b_start(0, opposite[low], 1)
    b_start(1, opposite[high], 3)
    above, below = pair_sum(1), pair_sum(3)
    b_start(2, above[high], 1)
    b_start(3, below[low], 3)
    text_sum = pair_sum(0)
    z_start(4)
    b_start(4, above[low] + b_landed(0), 1)
    b_start(5, below[high] + b_landed(1), 3)
    made = scalar_send(scalar_sum(made), [peers.along_y(step) for step in range(1, NY)])
    z_start(2)
    made = scalar_send(scalar_sum(made), [peers.along_z(step) for step in (4, 8, -4)])
    text_sum = jnp.concatenate(
        [
            text_sum[low] + b_landed(3) + b_landed(4),
            text_sum[high] + b_landed(2) + b_landed(5),
        ],
        axis=0,
    )
    last = []
    for a in (2, 1, 3):
        a_send[a - 1] = pack(text_sum[a * TEXTS : (a + 1) * TEXTS, :]).astype(BF16)
        last.append((copies.start(a_send.at[a - 1], a_land.at[3 - a], peers.first_axis(a)), 3 - a))
    text_sum = pack(text_sum[:TEXTS, :])
    text_values = text[...].astype(F32)
    text_inverse = row_inverse(text_values)
    text_unit = text_values * text_inverse
    made = scalar_send(scalar_sum(made), [peers.along_z(step) for step in (1, 2, 3)])
    quarters = [aligned(((y + k) % NY) * QUARTER, QUARTER) for k in range(NY)]
    inverses = [row_inverse(image[rows, :].astype(F32)) for rows in quarters]
    copies.finish()

    grad = part(0)
    for side, most in Z_SIDES:
        grad = gathered(side, most, 0, grad)
    for k in range(NY):
        y_send[k] = narrow(grad[:, k * SLOT : (k + 1) * SLOT])
    over_y = {}
    for step in (2, 1, 3):
        over_y[NY - step] = copies.start(
            y_send.at[(y + step) % NY], y_land.at[NY - step - 1], peers.along_y(step)
        )
    grad_image[quarters[0], :] = widen(y_send[y]) * inverses[0]

    for copy, slot in last:
        copy.wait_recv()
        text_sum = text_sum + a_land[slot].astype(F32)
    text_sum = unpack(text_sum)
    inner = jnp.sum(text_unit * text_sum, axis=1, keepdims=True)
    grad_text[...] = (text_sum - text_unit * inner) * text_inverse
    for k in range(1, NY):
        over_y[k].wait_recv()
        grad_image[quarters[k], :] = widen(y_land[k - 1]) * inverses[k]
    factor = jnp.where(row == 0, 1.0 / BATCH, jnp.where(row == 2, scale, 1.0))
    totals[...] = scalar_sum(made) * factor
    copies.finish()


def shards(image_emb, text_emb, log_temp, bias):
    vmem = pl.BlockSpec(memory_space=pltpu.VMEM)
    anywhere = pl.BlockSpec(memory_space=pl.ANY)
    grad_image, grad_text, totals = pl.pallas_call(
        kernel,
        out_shape=(
            jax.ShapeDtypeStruct((ROWS, SLOT), F32),
            jax.ShapeDtypeStruct((TEXTS, D), F32),
            jax.ShapeDtypeStruct((8, LANES), F32),
        ),
        in_specs=[anywhere] * 4,
        out_specs=(vmem,) * 3,
        scratch_shapes=[
            pltpu.SMEM((1,), F32),
            pltpu.SMEM((1,), F32),
            pltpu.VMEM((ROWS, D), BF16),
            pltpu.VMEM((TEXTS, D), BF16),
            pltpu.VMEM((ZLO, QUARTER, D), BF16),
            pltpu.VMEM((SLOTS, PACKED, LANES), BF16),
            pltpu.VMEM((SLOTS, PACKED, LANES), BF16),
            pltpu.VMEM((COLUMNS, D), BF16),
            pltpu.VMEM((IMAGES, D), BF16),
            pltpu.VMEM((IMAGES, COLUMNS), F32),
            pltpu.VMEM((IMAGES, COLUMNS), BF16),
            pltpu.VMEM((IMAGES, D), F32),
            pltpu.VMEM((ZLO, 2, QUARTER, WIDE), F32),
            pltpu.VMEM((COLUMNS, D), F32),
            pltpu.VMEM((4, GROUP, D), BF16),
            pltpu.VMEM((4, GROUP, D), BF16),
            pltpu.VMEM((6, GROUP // 2, D), BF16),
            pltpu.VMEM((6, GROUP // 2, D), BF16),
            pltpu.VMEM((3, PACKED, LANES), BF16),
            pltpu.VMEM((3, PACKED, LANES), BF16),
            pltpu.VMEM((15, QUARTER, WIDE), BF16),
            pltpu.VMEM((15, QUARTER, WIDE), BF16),
            pltpu.VMEM((NY, QUARTER + 8, LANES), F32),
            pltpu.VMEM((NY - 1, QUARTER + 8, LANES), F32),
            pltpu.VMEM((5, 8, LANES), F32),
            pltpu.VMEM((13, 8, LANES), F32),
            pltpu.SemaphoreType.DMA((COPIES,)),
            pltpu.SemaphoreType.DMA((COPIES,)),
            pltpu.SemaphoreType.DMA((4,)),
        ],
        compiler_params=pltpu.CompilerParams(
            collective_id=0, has_side_effects=True, vmem_limit_bytes=VMEM_LIMIT
        ),
    )(log_temp, bias, image_emb, text_emb)
    return (totals[0, :1], grad_image, grad_text, totals[2, :1], totals[1, :1])


def solution(mesh):
    return jax.shard_map(
        shards,
        mesh=mesh,
        in_specs=(P("grp", None), P(("blk", "grp"), None), P(), P()),
        out_specs=(P(), P("grp", "blk"), P(("blk", "grp"), None), P(), P()),
        check_vma=False,
    )
```

```python
import jax
import jax.numpy as jnp
from jax import lax
from jax.experimental import pallas as pl
from jax.experimental.pallas import tpu as pltpu
from jax.sharding import PartitionSpec as P

MESH = pl.DeviceIdType.MESH
epsilon = 1e-06

NX, NY, NZ, ZLO = 4, 4, 16, 8
D = 1152
ROWS = 192
QUARTER = ROWS // NY
IMAGES = ZLO * QUARTER
TEXTS = 24
SLOTS = NX * NY
OWN = SLOTS * TEXTS
COLUMNS = 2 * OWN
GROUP = 4 * TEXTS
LANES = 128
TILES = D // LANES
PACKED = 224
WIDE = D // 2
SLOT = D // 8
BATCH = 12288
STRIDE = 2
Z_SIDES = ((-1, 8), (1, 7))
ORDER = (0, 1, 7, 2, 6, 3, 5, 4)
NEAR, MIDDLE = 3, 5
COPIES = 3 + 4 + 12 + 7 + 15 + 4 + 6 + 3 + 3 + 13
F32, BF16 = jnp.float32, jnp.bfloat16
VMEM_LIMIT = 48 * 1024 * 1024


class Peers:
    def __init__(self):
        blk, grp = lax.axis_index("blk"), lax.axis_index("grp")
        z_hi, self.y = blk // NY, blk % NY
        self.core, z_lo, self.x = grp % 2, (grp // 2) % ZLO, grp // (2 * ZLO)
        self.z = z_hi * ZLO + z_lo
        self.sign = 1 - 2 * self.core

    def at(self, x, y, z, core):
        return ((z // ZLO) * NY + y, (x * ZLO + z % ZLO) * 2 + core)

    def other_core(self):
        return self.at(self.x, self.y, self.z, 1 - self.core)

    def along_x(self, step):
        return self.at((self.x + step) % NX, self.y, self.z, self.core)

    def along_y(self, step):
        return self.at(self.x, (self.y + step) % NY, self.z, self.core)

    def first_axis(self, step):
        return self.at(
            (self.x + step * (1 - self.core)) % NX,
            (self.y + step * self.core) % NY,
            self.z,
            self.core,
        )

    def second_axis(self, step):
        return self.at(
            (self.x + step * self.core) % NX,
            (self.y + step * (1 - self.core)) % NY,
            self.z,
            self.core,
        )

    def z_of(self, step):
        return (self.z + self.sign * step + NZ) % NZ

    def along_z(self, step):
        return self.at(self.x, self.y, self.z_of(step), self.core)


class Copies:
    def __init__(self, send_sem, recv_sem):
        self.send_sem, self.recv_sem, self.made = send_sem, recv_sem, []
        self.sent = 0

    def start(self, source, target, device_id):
        at = len(self.made)
        copy = pltpu.make_async_remote_copy(
            src_ref=source,
            dst_ref=target,
            send_sem=self.send_sem.at[at],
            recv_sem=self.recv_sem.at[at],
            device_id=device_id,
            device_id_type=MESH,
        )
        copy.start()
        self.made.append(copy)
        return copy

    def finish(self):
        for copy in self.made[self.sent :]:
            copy.wait_send()
        self.sent = len(self.made)


def pack(rows):
    pieces = [rows[:, k * LANES : (k + 1) * LANES] for k in range(TILES)]
    pieces.append(jnp.zeros((PACKED - TILES * TEXTS, LANES), F32))
    return jnp.concatenate(pieces, axis=0)


def unpack(packed):
    return jnp.concatenate(
        [packed[k * TEXTS : (k + 1) * TEXTS, :] for k in range(TILES)], axis=1
    )


def row_inverse(values):
    return lax.rsqrt(jnp.sum(values * values, axis=1, keepdims=True) + epsilon)


def narrow(rows):
    pieces = [rows[8 * k : 8 * k + 8, LANES:] for k in range(QUARTER // 8)]
    pieces.append(jnp.zeros((8, LANES - (SLOT - LANES) * QUARTER // 8), F32))
    return jnp.concatenate([rows[:, :LANES], jnp.concatenate(pieces, axis=1)], axis=0)


def widen(packed):
    rest = SLOT - LANES
    pieces = [packed[QUARTER:, rest * k : rest * (k + 1)] for k in range(QUARTER // 8)]
    return jnp.concatenate([packed[:QUARTER, :], jnp.concatenate(pieces, axis=0)], axis=1)


def hop(distance):
    return distance % STRIDE or STRIDE


def aligned(start, size):
    return pl.ds(pl.multiple_of(start, size), size)


def kernel(
    log_temp_in,
    bias_in,
    image_in,
    text_in,
    grad_image,
    grad_text,
    totals,
    log_temp,
    bias,
    image,
    text,
    images,
    own_texts,
    other_texts,
    text_bf,
    image_bf,
    similar,
    weights,
    grads,
    halves,
    text_part,
    core_send,
    core_land,
    b_send,
    b_land,
    a_send,
    a_land,
    z_send,
    z_land,
    y_send,
    y_land,
    s_send,
    s_land,
    send_sem,
    recv_sem,
    local_sem,
):
    peers = Peers()
    copies = Copies(send_sem, recv_sem)
    x, y, z, core = peers.x, peers.y, peers.z, peers.core

    image_copy = pltpu.make_async_copy(image_in, image, local_sem.at[0])
    text_copy = pltpu.make_async_copy(text_in, text, local_sem.at[1])
    scalar_copies = [
        pltpu.make_async_copy(log_temp_in, log_temp, local_sem.at[2]),
        pltpu.make_async_copy(bias_in, bias, local_sem.at[3]),
    ]
    for copy in (text_copy, image_copy, *scalar_copies):
        copy.start()
    barrier = pltpu.get_barrier_semaphore()
    met = (
        [peers.other_core()]
        + [peers.along_x(step) for step in range(1, NX)]
        + [peers.along_y(step) for step in range(1, NY)]
        + [peers.along_z(step) for step in (-4, -3, -2, -1, 1, 2, 3, 4, 8)]
    )
    for device_id in met:
        pl.semaphore_signal(barrier, inc=1, device_id=device_id, device_id_type=MESH)
    text_copy.wait()
    own_texts[0] = pack(text[...].astype(F32)).astype(BF16)
    image_copy.wait()
    images[0] = image[aligned(y * QUARTER, QUARTER), :]
    for copy in scalar_copies:
        copy.wait()
    pl.semaphore_wait(barrier, len(met))

    crossing, over_core, over_z = {}, {}, {}

    def text_forward(b):
        slots = pl.ds(4 * b, 4)
        over_core[b] = copies.start(
            own_texts.at[slots], other_texts.at[slots], peers.other_core()
        )

    def text_spread(a):
        crossing[a, 1] = copies.start(own_texts.at[a], own_texts.at[4 + a], peers.second_axis(3))
        crossing[a, 3] = copies.start(own_texts.at[a], own_texts.at[12 + a], peers.second_axis(1))

    def image_forward(distance, side):
        source = (distance if side > 0 else ZLO - distance) % ZLO
        target = (distance + 1 if side > 0 else ZLO - distance - 1) % ZLO
        over_z[target] = copies.start(
            images.at[ORDER.index(source)], images.at[ORDER.index(target)], peers.along_z(-side)
        )

    crossing[1, 0] = copies.start(own_texts.at[0], own_texts.at[1], peers.first_axis(3))
    crossing[3, 0] = copies.start(own_texts.at[0], own_texts.at[3], peers.first_axis(1))
    crossing[2, 0] = copies.start(own_texts.at[0], own_texts.at[2], peers.first_axis(2))
    image_forward(0, 1)
    image_forward(0, -1)
    text_spread(0)

    def image_ready(place):
        rows = pl.ds(place * QUARTER, QUARTER)
        values = images[place].astype(F32)
        image_bf[rows, :] = (values * row_inverse(values)).astype(BF16)

    def texts_ready(texts, b, first):
        for half in range(2):
            slot = b * 4 + 2 * half
            rows = jnp.concatenate(
                [unpack(texts[slot + k].astype(F32)) for k in range(2)], axis=0
            )
            text_bf[pl.ds(first + slot * TEXTS, 2 * TEXTS), :] = (
                rows * row_inverse(rows)
            ).astype(BF16)

    image_ready(0)
    for a in (1, 3, 2):
        crossing[a, 0].wait_recv()
        text_spread(a)
    text_forward(0)
    for target, side in ((1, 1), (7, -1)):
        over_z[target].wait_recv()
        image_forward(1, side)
    texts_ready(own_texts, 0, 0)
    image_ready(1)
    image_ready(2)
    for a in (0, 1, 3, 2):
        for b in (1, 3):
            crossing[a, b].wait_recv()
            if (b == 1) == (a in (0, 3)):
                step = 3 if b == 1 else 1
                crossing[a, 2] = copies.start(
                    own_texts.at[b * 4 + a], own_texts.at[8 + a], peers.second_axis(step)
                )
    text_forward(1)
    text_forward(3)
    for target, side in ((2, 1), (6, -1)):
        over_z[target].wait_recv()
        image_forward(2, side)
    texts_ready(own_texts, 1, 0)
    texts_ready(own_texts, 3, 0)

    def others_ready(b):
        over_core[b].wait_recv()
        texts_ready(other_texts, b, OWN)

    others_ready(0)
    for a in (0, 1, 3, 2):
        crossing[a, 2].wait_recv()
    text_forward(2)
    texts_ready(own_texts, 2, 0)
    others_ready(1)
    others_ready(3)

    scale = jnp.exp(jnp.full((1, 1), log_temp[0], F32))
    shift = bias[0]
    column = lax.broadcasted_iota(jnp.int32, (1, COLUMNS), 1)
    block = (column * 2731) >> 16
    text_core = ((block >> 4) + core) & 1
    on_first, on_second = block & 3, (block >> 2) & 3
    text_x = (x + jnp.where(text_core == 0, on_first, on_second)) & (NX - 1)
    text_y = (y + jnp.where(text_core == 0, on_second, on_first)) & (NY - 1)
    text_ids = (
        ((z // ZLO) * NY + text_y) * (BATCH // 8)
        + ((text_x * ZLO + z % ZLO) * 2 + text_core) * TEXTS
        + column
        - block * TEXTS
    )

    def weigh(low, high, lanes, carry):
        rows = pl.ds(low * QUARTER, (high - low) * QUARTER)
        similar[rows, lanes] = lax.dot_general(
            image_bf[rows, :],
            text_bf[lanes, :],
            (((1,), (1,)), ((), ())),
            preferred_element_type=F32,
        )
        ids = text_ids[:, lanes.start : lanes.start + lanes.size]

        def step(place, carry):
            losses, dlogits, weighted = carry
            rows = aligned(place * QUARTER, QUARTER)
            distance = ((place + 1) // 2) * (2 * (place % 2) - 1)
            image_z = (z + peers.sign * distance + NZ) % ZLO
            first = ((x * ZLO + image_z) * 2 + core) * ROWS + y * QUARTER
            same = first + lax.broadcasted_iota(jnp.int32, (QUARTER, 1), 0) == ids
            product = similar[rows, lanes]
            logits = scale * product + shift
            power = jnp.exp(jnp.where(same, -logits, logits))
            above = 1.0 + power
            chance = power / above
            dlogit = jnp.where(same, -chance, chance)
            weights[rows, lanes] = (scale * dlogit).astype(BF16)
            losses = losses + jnp.sum(jnp.log(above), axis=0, keepdims=True)
            dlogits = dlogits + jnp.sum(dlogit, axis=0, keepdims=True)
            weighted = weighted + jnp.sum(dlogit * product, axis=0, keepdims=True)
            return losses, dlogits, weighted

        return lax.fori_loop(low, high, step, carry)

    def project(place):
        values = images[place].astype(F32)
        unit = values * row_inverse(values)
        grad = grads[aligned(place * QUARTER, QUARTER), :]
        grad = grad - unit * jnp.sum(unit * grad, axis=1, keepdims=True)
        halves[place, 0] = grad[:, :WIDE]
        halves[place, 1] = grad[:, WIDE:]

    def image_grads(low, high):
        rows = pl.ds(low * QUARTER, (high - low) * QUARTER)
        grads[rows, :] = jnp.dot(weights[rows, :], text_bf[...], preferred_element_type=F32)
        pl.loop(low, high)(project)

    index = {}
    for side, most in Z_SIDES:
        for far in range(most, 0, -1):
            index[side, far] = len(index)
    flying = {}

    def part(step):
        return halves[ORDER.index(step % ZLO), peers.z_of(step) // ZLO]

    def gathered(side, most, to, value):
        for far in range(to + 1, min(to + STRIDE, most) + 1):
            flying[side, far].wait_recv()
            value = value + z_land[index[side, far]].astype(F32)
        return value

    def z_start(far):
        for side, most in Z_SIDES:
            if far > most:
                continue
            value = part(side * far)
            if far % STRIDE == 0:
                value = gathered(side, most, far, value)
            at = index[side, far]
            z_send[at] = value.astype(BF16)
            flying[side, far] = copies.start(
                z_send.at[at], z_land.at[at], peers.along_z(side * hop(far))
            )

    scalar = {"stage": 0, "slot": 0, "value": None}

    def scalar_send(value, to):
        stage = scalar["stage"]
        scalar["value"] = value
        s_send[stage] = value
        made = []
        for peer in to:
            slot = scalar["slot"]
            made.append((copies.start(s_send.at[stage], s_land.at[slot], peer), slot))
            scalar["slot"] += 1
        scalar["stage"] += 1
        return made

    def scalar_sum(made):
        value = scalar["value"]
        for copy, slot in made:
            copy.wait_recv()
            value = value + s_land[slot]
        return value

    own_lanes, other_lanes = pl.ds(0, OWN), pl.ds(OWN, OWN)
    zero = jnp.zeros((1, OWN), F32)
    carry = weigh(0, NEAR, own_lanes, (zero, zero, zero))
    over_z[3].wait_recv()
    image_forward(3, 1)
    others_ready(2)
    carry = weigh(0, NEAR, other_lanes, carry)
    image_grads(0, NEAR)
    for far in (8, 7, 1):
        z_start(far)
    image_ready(3)
    image_ready(4)
    carry = weigh(NEAR, MIDDLE, other_lanes, carry)
    carry = weigh(NEAR, MIDDLE, own_lanes, carry)
    image_grads(NEAR, MIDDLE)
    z_start(6)
    image_ready(5)
    over_z[5].wait_recv()
    image_ready(6)
    over_z[4].wait_recv()
    image_ready(7)
    carry = weigh(MIDDLE, ZLO, other_lanes, carry)
    carry = weigh(MIDDLE, ZLO, own_lanes, carry)
    row = lax.broadcasted_iota(jnp.int32, (8, LANES), 0)
    total = jnp.zeros((8, LANES), F32)
    for k in range(3):
        total = jnp.where(row == k, jnp.sum(carry[k], axis=1, keepdims=True), total)
    made = scalar_send(total, [peers.other_core()])
    image_grads(MIDDLE, ZLO)
    z_start(5)
    z_start(3)
    made = scalar_send(scalar_sum(made), [peers.along_x(step) for step in range(1, NX)])

    def text_tile(at):
        lanes = aligned(at * LANES, LANES)
        text_part[lanes, :] = lax.dot_general(
            weights[:, lanes],
            image_bf[...],
            (((0,), (0,)), ((), ())),
            preferred_element_type=F32,
        )

    pl.loop(OWN // LANES, COLUMNS // LANES)(text_tile)
    pairs = {}
    for b in (2, 1, 3, 0):
        core_send[b] = text_part[pl.ds(OWN + b * GROUP, GROUP), :].astype(BF16)
        pairs[b] = copies.start(core_send.at[b], core_land.at[b], peers.other_core())
    made = scalar_send(scalar_sum(made), [peers.along_y(step) for step in range(1, NY)])
    pl.loop(0, OWN // LANES)(text_tile)
    made = scalar_send(scalar_sum(made), [peers.along_z(step) for step in (4, 8, -4)])

    def pair_sum(b):
        pairs[b].wait_recv()
        return text_part[pl.ds(b * GROUP, GROUP), :] + core_land[b].astype(F32)

    across = {}

    def b_start(at, value, step):
        b_send[at] = value.astype(BF16)
        across[at] = copies.start(b_send.at[at], b_land.at[at], peers.second_axis(step))

    def b_landed(at):
        across[at].wait_recv()
        return b_land[at].astype(F32)

    low, high = slice(0, GROUP // 2), slice(GROUP // 2, GROUP)
    opposite = pair_sum(2)
    b_start(0, opposite[low], 1)
    b_start(1, opposite[high], 3)
    above, below = pair_sum(1), pair_sum(3)
    b_start(2, above[high], 1)
    b_start(3, below[low], 3)
    text_sum = pair_sum(0)
    z_start(4)
    b_start(4, above[low] + b_landed(0), 1)
    b_start(5, below[high] + b_landed(1), 3)
    z_start(2)
    text_sum = jnp.concatenate(
        [
            text_sum[low] + b_landed(3) + b_landed(4),
            text_sum[high] + b_landed(2) + b_landed(5),
        ],
        axis=0,
    )
    last = []
    for a in (2, 1, 3):
        a_send[a - 1] = pack(text_sum[a * TEXTS : (a + 1) * TEXTS, :]).astype(BF16)
        last.append((copies.start(a_send.at[a - 1], a_land.at[3 - a], peers.first_axis(a)), 3 - a))
    text_sum = pack(text_sum[:TEXTS, :])
    text_values = text[...].astype(F32)
    text_inverse = row_inverse(text_values)
    text_unit = text_values * text_inverse
    made = scalar_send(scalar_sum(made), [peers.along_z(step) for step in (1, 2, 3)])
    quarters = [aligned(((y + k) % NY) * QUARTER, QUARTER) for k in range(NY)]
    inverses = [row_inverse(image[rows, :].astype(F32)) for rows in quarters]

    grad = part(0)
    for side, most in Z_SIDES:
        grad = gathered(side, most, 0, grad)
    for k in range(NY):
        y_send[k] = narrow(grad[:, k * SLOT : (k + 1) * SLOT])
    over_y = {}
    for step in (2, 1, 3):
        over_y[NY - step] = copies.start(
            y_send.at[(y + step) % NY], y_land.at[NY - step - 1], peers.along_y(step)
        )
    grad_image[quarters[0], :] = widen(y_send[y]) * inverses[0]
    copies.finish()

    for copy, slot in last:
        copy.wait_recv()
        text_sum = text_sum + a_land[slot].astype(F32)
    text_sum = unpack(text_sum)
    inner = jnp.sum(text_unit * text_sum, axis=1, keepdims=True)
    grad_text[...] = (text_sum - text_unit * inner) * text_inverse
    for k in range(1, NY):
        over_y[k].wait_recv()
        grad_image[quarters[k], :] = widen(y_land[k - 1]) * inverses[k]
    factor = jnp.where(row == 0, 1.0 / BATCH, jnp.where(row == 2, scale, 1.0))
    totals[...] = scalar_sum(made) * factor
    copies.finish()


def shards(image_emb, text_emb, log_temp, bias):
    vmem = pl.BlockSpec(memory_space=pltpu.VMEM)
    anywhere = pl.BlockSpec(memory_space=pl.ANY)
    grad_image, grad_text, totals = pl.pallas_call(
        kernel,
        out_shape=(
            jax.ShapeDtypeStruct((ROWS, SLOT), F32),
            jax.ShapeDtypeStruct((TEXTS, D), F32),
            jax.ShapeDtypeStruct((8, LANES), F32),
        ),
        in_specs=[anywhere] * 4,
        out_specs=(vmem,) * 3,
        scratch_shapes=[
            pltpu.SMEM((1,), F32),
            pltpu.SMEM((1,), F32),
            pltpu.VMEM((ROWS, D), BF16),
            pltpu.VMEM((TEXTS, D), BF16),
            pltpu.VMEM((ZLO, QUARTER, D), BF16),
            pltpu.VMEM((SLOTS, PACKED, LANES), BF16),
            pltpu.VMEM((SLOTS, PACKED, LANES), BF16),
            pltpu.VMEM((COLUMNS, D), BF16),
            pltpu.VMEM((IMAGES, D), BF16),
            pltpu.VMEM((IMAGES, COLUMNS), F32),
            pltpu.VMEM((IMAGES, COLUMNS), BF16),
            pltpu.VMEM((IMAGES, D), F32),
            pltpu.VMEM((ZLO, 2, QUARTER, WIDE), F32),
            pltpu.VMEM((COLUMNS, D), F32),
            pltpu.VMEM((4, GROUP, D), BF16),
            pltpu.VMEM((4, GROUP, D), BF16),
            pltpu.VMEM((6, GROUP // 2, D), BF16),
            pltpu.VMEM((6, GROUP // 2, D), BF16),
            pltpu.VMEM((3, PACKED, LANES), BF16),
            pltpu.VMEM((3, PACKED, LANES), BF16),
            pltpu.VMEM((15, QUARTER, WIDE), BF16),
            pltpu.VMEM((15, QUARTER, WIDE), BF16),
            pltpu.VMEM((NY, QUARTER + 8, LANES), F32),
            pltpu.VMEM((NY - 1, QUARTER + 8, LANES), F32),
            pltpu.VMEM((5, 8, LANES), F32),
            pltpu.VMEM((13, 8, LANES), F32),
            pltpu.SemaphoreType.DMA((COPIES,)),
            pltpu.SemaphoreType.DMA((COPIES,)),
            pltpu.SemaphoreType.DMA((4,)),
        ],
        compiler_params=pltpu.CompilerParams(
            collective_id=0, has_side_effects=True, vmem_limit_bytes=VMEM_LIMIT
        ),
    )(log_temp, bias, image_emb, text_emb)
    return (totals[0, :1], grad_image, grad_text, totals[2, :1], totals[1, :1])


def solution(mesh):
    return jax.shard_map(
        shards,
        mesh=mesh,
        in_specs=(P("grp", None), P(("blk", "grp"), None), P(), P()),
        out_specs=(P(), P("grp", "blk"), P(("blk", "grp"), None), P(), P()),
        check_vma=False,
    )
```

```python
import jax
import jax.numpy as jnp
from jax import lax
from jax.experimental import pallas as pl
from jax.experimental.pallas import tpu as pltpu
from jax.sharding import PartitionSpec as P

MESH = pl.DeviceIdType.MESH
epsilon = 1e-06

NX, NY, NZ, ZLO = 4, 4, 16, 8
D = 1152
ROWS = 192
QUARTER = ROWS // NY
IMAGES = ZLO * QUARTER
TEXTS = 24
SLOTS = NX * NY
OWN = SLOTS * TEXTS
COLUMNS = 2 * OWN
GROUP = 4 * TEXTS
LANES = 128
TILES = D // LANES
PACKED = 224
WIDE = D // 2
SLOT = D // 8
BATCH = 12288
STRIDE = 2
Z_SIDES = ((-1, 8), (1, 7))
ORDER = (0, 1, 7, 2, 6, 3, 5, 4)
NEAR, MIDDLE = 3, 5
COPIES = 3 + 4 + 12 + 7 + 15 + 4 + 6 + 3 + 3 + 13
F32, BF16 = jnp.float32, jnp.bfloat16
VMEM_LIMIT = 48 * 1024 * 1024


class Peers:
    def __init__(self):
        blk, grp = lax.axis_index("blk"), lax.axis_index("grp")
        z_hi, self.y = blk // NY, blk % NY
        self.core, z_lo, self.x = grp % 2, (grp // 2) % ZLO, grp // (2 * ZLO)
        self.z = z_hi * ZLO + z_lo
        self.sign = 1 - 2 * self.core

    def at(self, x, y, z, core):
        return ((z // ZLO) * NY + y, (x * ZLO + z % ZLO) * 2 + core)

    def other_core(self):
        return self.at(self.x, self.y, self.z, 1 - self.core)

    def along_x(self, step):
        return self.at((self.x + step) % NX, self.y, self.z, self.core)

    def along_y(self, step):
        return self.at(self.x, (self.y + step) % NY, self.z, self.core)

    def first_axis(self, step):
        return self.at(
            (self.x + step * (1 - self.core)) % NX,
            (self.y + step * self.core) % NY,
            self.z,
            self.core,
        )

    def second_axis(self, step):
        return self.at(
            (self.x + step * self.core) % NX,
            (self.y + step * (1 - self.core)) % NY,
            self.z,
            self.core,
        )

    def z_of(self, step):
        return (self.z + self.sign * step + NZ) % NZ

    def along_z(self, step):
        return self.at(self.x, self.y, self.z_of(step), self.core)


class Copies:
    def __init__(self, send_sem, recv_sem):
        self.send_sem, self.recv_sem, self.made = send_sem, recv_sem, []
        self.sent = 0

    def start(self, source, target, device_id):
        at = len(self.made)
        copy = pltpu.make_async_remote_copy(
            src_ref=source,
            dst_ref=target,
            send_sem=self.send_sem.at[at],
            recv_sem=self.recv_sem.at[at],
            device_id=device_id,
            device_id_type=MESH,
        )
        copy.start()
        self.made.append(copy)
        return copy

    def finish(self):
        for copy in self.made[self.sent :]:
            copy.wait_send()
        self.sent = len(self.made)


def pack(rows):
    pieces = [rows[:, k * LANES : (k + 1) * LANES] for k in range(TILES)]
    pieces.append(jnp.zeros((PACKED - TILES * TEXTS, LANES), F32))
    return jnp.concatenate(pieces, axis=0)


def unpack(packed):
    return jnp.concatenate(
        [packed[k * TEXTS : (k + 1) * TEXTS, :] for k in range(TILES)], axis=1
    )


def row_inverse(values):
    return lax.rsqrt(jnp.sum(values * values, axis=1, keepdims=True) + epsilon)


def narrow(rows):
    pieces = [rows[8 * k : 8 * k + 8, LANES:] for k in range(QUARTER // 8)]
    pieces.append(jnp.zeros((8, LANES - (SLOT - LANES) * QUARTER // 8), F32))
    return jnp.concatenate([rows[:, :LANES], jnp.concatenate(pieces, axis=1)], axis=0)


def widen(packed):
    rest = SLOT - LANES
    pieces = [packed[QUARTER:, rest * k : rest * (k + 1)] for k in range(QUARTER // 8)]
    return jnp.concatenate([packed[:QUARTER, :], jnp.concatenate(pieces, axis=0)], axis=1)


def hop(distance):
    return distance % STRIDE or STRIDE


def aligned(start, size):
    return pl.ds(pl.multiple_of(start, size), size)


def kernel(
    log_temp_in,
    bias_in,
    image_in,
    text_in,
    grad_image,
    grad_text,
    totals,
    log_temp,
    bias,
    image,
    text,
    images,
    own_texts,
    other_texts,
    text_bf,
    image_bf,
    similar,
    weights,
    grads,
    halves,
    text_part,
    core_send,
    core_land,
    b_send,
    b_land,
    a_send,
    a_land,
    z_send,
    z_land,
    y_send,
    y_land,
    s_send,
    s_land,
    send_sem,
    recv_sem,
    local_sem,
):
    peers = Peers()
    copies = Copies(send_sem, recv_sem)
    x, y, z, core = peers.x, peers.y, peers.z, peers.core

    image_copy = pltpu.make_async_copy(image_in, image, local_sem.at[0])
    text_copy = pltpu.make_async_copy(text_in, text, local_sem.at[1])
    scalar_copies = [
        pltpu.make_async_copy(log_temp_in, log_temp, local_sem.at[2]),
        pltpu.make_async_copy(bias_in, bias, local_sem.at[3]),
    ]
    for copy in (text_copy, image_copy, *scalar_copies):
        copy.start()
    barrier = pltpu.get_barrier_semaphore()
    met = (
        [peers.other_core()]
        + [peers.along_x(step) for step in range(1, NX)]
        + [peers.along_y(step) for step in range(1, NY)]
        + [peers.along_z(step) for step in (-4, -3, -2, -1, 1, 2, 3, 4, 8)]
    )
    for device_id in met:
        pl.semaphore_signal(barrier, inc=1, device_id=device_id, device_id_type=MESH)
    text_copy.wait()
    own_texts[0] = pack(text[...].astype(F32)).astype(BF16)
    image_copy.wait()
    images[0] = image[aligned(y * QUARTER, QUARTER), :]
    for copy in scalar_copies:
        copy.wait()
    pl.semaphore_wait(barrier, len(met))

    crossing, over_core, over_z = {}, {}, {}

    def text_forward(b):
        slots = pl.ds(4 * b, 4)
        over_core[b] = copies.start(
            own_texts.at[slots], other_texts.at[slots], peers.other_core()
        )

    def text_spread(a):
        crossing[a, 1] = copies.start(own_texts.at[a], own_texts.at[4 + a], peers.second_axis(3))
        crossing[a, 3] = copies.start(own_texts.at[a], own_texts.at[12 + a], peers.second_axis(1))

    def image_forward(distance, side):
        source = (distance if side > 0 else ZLO - distance) % ZLO
        target = (distance + 1 if side > 0 else ZLO - distance - 1) % ZLO
        over_z[target] = copies.start(
            images.at[ORDER.index(source)], images.at[ORDER.index(target)], peers.along_z(-side)
        )

    crossing[1, 0] = copies.start(own_texts.at[0], own_texts.at[1], peers.first_axis(3))
    crossing[3, 0] = copies.start(own_texts.at[0], own_texts.at[3], peers.first_axis(1))
    crossing[2, 0] = copies.start(own_texts.at[0], own_texts.at[2], peers.first_axis(2))
    image_forward(0, 1)
    image_forward(0, -1)
    text_spread(0)

    def image_ready(place):
        rows = pl.ds(place * QUARTER, QUARTER)
        values = images[place].astype(F32)
        image_bf[rows, :] = (values * row_inverse(values)).astype(BF16)

    def texts_ready(texts, b, first):
        for half in range(2):
            slot = b * 4 + 2 * half
            rows = jnp.concatenate(
                [unpack(texts[slot + k].astype(F32)) for k in range(2)], axis=0
            )
            text_bf[pl.ds(first + slot * TEXTS, 2 * TEXTS), :] = (
                rows * row_inverse(rows)
            ).astype(BF16)

    image_ready(0)
    for a in (1, 3, 2):
        crossing[a, 0].wait_recv()
        text_spread(a)
    text_forward(0)
    for target, side in ((1, 1), (7, -1)):
        over_z[target].wait_recv()
        image_forward(1, side)
    texts_ready(own_texts, 0, 0)
    image_ready(1)
    image_ready(2)
    for a in (0, 1, 3, 2):
        for b in (1, 3):
            crossing[a, b].wait_recv()
            if (b == 1) == (a in (0, 3)):
                step = 3 if b == 1 else 1
                crossing[a, 2] = copies.start(
                    own_texts.at[b * 4 + a], own_texts.at[8 + a], peers.second_axis(step)
                )
    text_forward(1)
    text_forward(3)
    texts_ready(own_texts, 1, 0)
    texts_ready(own_texts, 3, 0)

    def others_ready(b):
        over_core[b].wait_recv()
        texts_ready(other_texts, b, OWN)

    others_ready(0)
    for a in (0, 1, 3, 2):
        crossing[a, 2].wait_recv()
    text_forward(2)
    for target, side in ((2, 1), (6, -1)):
        over_z[target].wait_recv()
        image_forward(2, side)
    texts_ready(own_texts, 2, 0)
    others_ready(1)
    others_ready(3)

    scale = jnp.exp(jnp.full((1, 1), log_temp[0], F32))
    shift = bias[0]
    column = lax.broadcasted_iota(jnp.int32, (1, COLUMNS), 1)
    block = (column * 2731) >> 16
    text_core = ((block >> 4) + core) & 1
    on_first, on_second = block & 3, (block >> 2) & 3
    text_x = (x + jnp.where(text_core == 0, on_first, on_second)) & (NX - 1)
    text_y = (y + jnp.where(text_core == 0, on_second, on_first)) & (NY - 1)
    text_ids = (
        ((z // ZLO) * NY + text_y) * (BATCH // 8)
        + ((text_x * ZLO + z % ZLO) * 2 + text_core) * TEXTS
        + column
        - block * TEXTS
    )

    def weigh(low, high, lanes, carry):
        rows = pl.ds(low * QUARTER, (high - low) * QUARTER)
        similar[rows, lanes] = lax.dot_general(
            image_bf[rows, :],
            text_bf[lanes, :],
            (((1,), (1,)), ((), ())),
            preferred_element_type=F32,
        )
        ids = text_ids[:, lanes.start : lanes.start + lanes.size]

        def step(place, carry):
            losses, dlogits, weighted = carry
            rows = aligned(place * QUARTER, QUARTER)
            distance = ((place + 1) // 2) * (2 * (place % 2) - 1)
            image_z = (z + peers.sign * distance + NZ) % ZLO
            first = ((x * ZLO + image_z) * 2 + core) * ROWS + y * QUARTER
            same = first + lax.broadcasted_iota(jnp.int32, (QUARTER, 1), 0) == ids
            product = similar[rows, lanes]
            logits = scale * product + shift
            power = jnp.exp(jnp.where(same, -logits, logits))
            above = 1.0 + power
            chance = power / above
            dlogit = jnp.where(same, -chance, chance)
            weights[rows, lanes] = (scale * dlogit).astype(BF16)
            losses = losses + jnp.sum(jnp.log(above), axis=0, keepdims=True)
            dlogits = dlogits + jnp.sum(dlogit, axis=0, keepdims=True)
            weighted = weighted + jnp.sum(dlogit * product, axis=0, keepdims=True)
            return losses, dlogits, weighted

        return lax.fori_loop(low, high, step, carry)

    def project(place):
        values = images[place].astype(F32)
        unit = values * row_inverse(values)
        grad = grads[aligned(place * QUARTER, QUARTER), :]
        grad = grad - unit * jnp.sum(unit * grad, axis=1, keepdims=True)
        halves[place, 0] = grad[:, :WIDE]
        halves[place, 1] = grad[:, WIDE:]

    def image_grads(low, high):
        rows = pl.ds(low * QUARTER, (high - low) * QUARTER)
        grads[rows, :] = jnp.dot(weights[rows, :], text_bf[...], preferred_element_type=F32)
        pl.loop(low, high)(project)

    index = {}
    for side, most in Z_SIDES:
        for far in range(most, 0, -1):
            index[side, far] = len(index)
    flying = {}

    def part(step):
        return halves[ORDER.index(step % ZLO), peers.z_of(step) // ZLO]

    def gathered(side, most, to, value):
        for far in range(to + 1, min(to + STRIDE, most) + 1):
            flying[side, far].wait_recv()
            value = value + z_land[index[side, far]].astype(F32)
        return value

    def z_start(far):
        for side, most in Z_SIDES:
            if far > most:
                continue
            value = part(side * far)
            if far % STRIDE == 0:
                value = gathered(side, most, far, value)
            at = index[side, far]
            z_send[at] = value.astype(BF16)
            flying[side, far] = copies.start(
                z_send.at[at], z_land.at[at], peers.along_z(side * hop(far))
            )

    scalar = {"stage": 0, "slot": 0, "value": None}

    def scalar_send(value, to):
        stage = scalar["stage"]
        scalar["value"] = value
        s_send[stage] = value
        made = []
        for peer in to:
            slot = scalar["slot"]
            made.append((copies.start(s_send.at[stage], s_land.at[slot], peer), slot))
            scalar["slot"] += 1
        scalar["stage"] += 1
        return made

    def scalar_sum(made):
        value = scalar["value"]
        for copy, slot in made:
            copy.wait_recv()
            value = value + s_land[slot]
        return value

    own_lanes, other_lanes = pl.ds(0, OWN), pl.ds(OWN, OWN)
    zero = jnp.zeros((1, OWN), F32)
    carry = weigh(0, NEAR, own_lanes, (zero, zero, zero))
    others_ready(2)
    carry = weigh(0, NEAR, other_lanes, carry)
    over_z[3].wait_recv()
    image_forward(3, 1)
    image_grads(0, NEAR)
    for far in (8, 7, 1):
        z_start(far)
    image_ready(3)
    image_ready(4)
    carry = weigh(NEAR, MIDDLE, other_lanes, carry)
    carry = weigh(NEAR, MIDDLE, own_lanes, carry)
    image_grads(NEAR, MIDDLE)
    z_start(6)
    image_ready(5)
    over_z[5].wait_recv()
    image_ready(6)
    over_z[4].wait_recv()
    image_ready(7)
    carry = weigh(MIDDLE, ZLO, other_lanes, carry)
    carry = weigh(MIDDLE, ZLO, own_lanes, carry)
    row = lax.broadcasted_iota(jnp.int32, (8, LANES), 0)
    total = jnp.zeros((8, LANES), F32)
    for k in range(3):
        total = jnp.where(row == k, jnp.sum(carry[k], axis=1, keepdims=True), total)
    made = scalar_send(total, [peers.other_core()])
    image_grads(MIDDLE, ZLO)
    z_start(5)
    z_start(3)
    made = scalar_send(scalar_sum(made), [peers.along_x(step) for step in range(1, NX)])

    def text_tile(at):
        lanes = aligned(at * LANES, LANES)
        text_part[lanes, :] = lax.dot_general(
            weights[:, lanes],
            image_bf[...],
            (((0,), (0,)), ((), ())),
            preferred_element_type=F32,
        )

    pl.loop(OWN // LANES, COLUMNS // LANES)(text_tile)
    pairs = {}
    for b in (2, 1, 3, 0):
        core_send[b] = text_part[pl.ds(OWN + b * GROUP, GROUP), :].astype(BF16)
        pairs[b] = copies.start(core_send.at[b], core_land.at[b], peers.other_core())
    z_start(4)
    made = scalar_send(scalar_sum(made), [peers.along_y(step) for step in range(1, NY)])
    pl.loop(0, OWN // LANES)(text_tile)
    made = scalar_send(scalar_sum(made), [peers.along_z(step) for step in (4, 8, -4)])

    def pair_sum(b):
        pairs[b].wait_recv()
        return text_part[pl.ds(b * GROUP, GROUP), :] + core_land[b].astype(F32)

    across = {}

    def b_start(at, value, step):
        b_send[at] = value.astype(BF16)
        across[at] = copies.start(b_send.at[at], b_land.at[at], peers.second_axis(step))

    def b_landed(at):
        across[at].wait_recv()
        return b_land[at].astype(F32)

    low, high = slice(0, GROUP // 2), slice(GROUP // 2, GROUP)
    opposite = pair_sum(2)
    b_start(0, opposite[low], 1)
    b_start(1, opposite[high], 3)
    above, below = pair_sum(1), pair_sum(3)
    b_start(2, above[high], 1)
    b_start(3, below[low], 3)
    text_sum = pair_sum(0)
    z_start(2)
    b_start(4, above[low] + b_landed(0), 1)
    b_start(5, below[high] + b_landed(1), 3)
    quarters = [aligned(((y + k) % NY) * QUARTER, QUARTER) for k in range(NY)]
    inverses = [row_inverse(image[rows, :].astype(F32)) for rows in quarters]
    grad = part(0)
    for side, most in Z_SIDES:
        grad = gathered(side, most, 0, grad)
    for k in range(NY):
        y_send[k] = narrow(grad[:, k * SLOT : (k + 1) * SLOT])
    over_y = {}
    for step in (2, 1, 3):
        over_y[NY - step] = copies.start(
            y_send.at[(y + step) % NY], y_land.at[NY - step - 1], peers.along_y(step)
        )
    grad_image[quarters[0], :] = widen(y_send[y]) * inverses[0]
    made = scalar_send(scalar_sum(made), [peers.along_z(step) for step in (1, 2, 3)])
    text_sum = jnp.concatenate(
        [
            text_sum[low] + b_landed(3) + b_landed(4),
            text_sum[high] + b_landed(2) + b_landed(5),
        ],
        axis=0,
    )
    last = []
    for a in (2, 1, 3):
        a_send[a - 1] = pack(text_sum[a * TEXTS : (a + 1) * TEXTS, :]).astype(BF16)
        last.append((copies.start(a_send.at[a - 1], a_land.at[3 - a], peers.first_axis(a)), 3 - a))
    text_sum = pack(text_sum[:TEXTS, :])
    text_values = text[...].astype(F32)
    text_inverse = row_inverse(text_values)
    text_unit = text_values * text_inverse
    copies.finish()
    for copy, slot in last:
        copy.wait_recv()
        text_sum = text_sum + a_land[slot].astype(F32)
    text_sum = unpack(text_sum)
    inner = jnp.sum(text_unit * text_sum, axis=1, keepdims=True)
    grad_text[...] = (text_sum - text_unit * inner) * text_inverse
    for k in range(1, NY):
        over_y[k].wait_recv()
        grad_image[quarters[k], :] = widen(y_land[k - 1]) * inverses[k]
    factor = jnp.where(row == 0, 1.0 / BATCH, jnp.where(row == 2, scale, 1.0))
    totals[...] = scalar_sum(made) * factor
    copies.finish()


def shards(image_emb, text_emb, log_temp, bias):
    vmem = pl.BlockSpec(memory_space=pltpu.VMEM)
    anywhere = pl.BlockSpec(memory_space=pl.ANY)
    grad_image, grad_text, totals = pl.pallas_call(
        kernel,
        out_shape=(
            jax.ShapeDtypeStruct((ROWS, SLOT), F32),
            jax.ShapeDtypeStruct((TEXTS, D), F32),
            jax.ShapeDtypeStruct((8, LANES), F32),
        ),
        in_specs=[anywhere] * 4,
        out_specs=(vmem,) * 3,
        scratch_shapes=[
            pltpu.SMEM((1,), F32),
            pltpu.SMEM((1,), F32),
            pltpu.VMEM((ROWS, D), BF16),
            pltpu.VMEM((TEXTS, D), BF16),
            pltpu.VMEM((ZLO, QUARTER, D), BF16),
            pltpu.VMEM((SLOTS, PACKED, LANES), BF16),
            pltpu.VMEM((SLOTS, PACKED, LANES), BF16),
            pltpu.VMEM((COLUMNS, D), BF16),
            pltpu.VMEM((IMAGES, D), BF16),
            pltpu.VMEM((IMAGES, COLUMNS), F32),
            pltpu.VMEM((IMAGES, COLUMNS), BF16),
            pltpu.VMEM((IMAGES, D), F32),
            pltpu.VMEM((ZLO, 2, QUARTER, WIDE), F32),
            pltpu.VMEM((COLUMNS, D), F32),
            pltpu.VMEM((4, GROUP, D), BF16),
            pltpu.VMEM((4, GROUP, D), BF16),
            pltpu.VMEM((6, GROUP // 2, D), BF16),
            pltpu.VMEM((6, GROUP // 2, D), BF16),
            pltpu.VMEM((3, PACKED, LANES), BF16),
            pltpu.VMEM((3, PACKED, LANES), BF16),
            pltpu.VMEM((15, QUARTER, WIDE), BF16),
            pltpu.VMEM((15, QUARTER, WIDE), BF16),
            pltpu.VMEM((NY, QUARTER + 8, LANES), F32),
            pltpu.VMEM((NY - 1, QUARTER + 8, LANES), F32),
            pltpu.VMEM((5, 8, LANES), F32),
            pltpu.VMEM((13, 8, LANES), F32),
            pltpu.SemaphoreType.DMA((COPIES,)),
            pltpu.SemaphoreType.DMA((COPIES,)),
            pltpu.SemaphoreType.DMA((4,)),
        ],
        compiler_params=pltpu.CompilerParams(
            collective_id=0, has_side_effects=True, vmem_limit_bytes=VMEM_LIMIT
        ),
    )(log_temp, bias, image_emb, text_emb)
    return (totals[0, :1], grad_image, grad_text, totals[2, :1], totals[1, :1])


def solution(mesh):
    return jax.shard_map(
        shards,
        mesh=mesh,
        in_specs=(P("grp", None), P(("blk", "grp"), None), P(), P()),
        out_specs=(P(), P("grp", "blk"), P(("blk", "grp"), None), P(), P()),
        check_vma=False,
    )
```

```python
import jax
import jax.numpy as jnp
from jax import lax
from jax.experimental import pallas as pl
from jax.experimental.pallas import tpu as pltpu
from jax.sharding import PartitionSpec as P

MESH = pl.DeviceIdType.MESH
epsilon = 1e-06

NX, NY, NZ, ZLO = 4, 4, 16, 8
D = 1152
ROWS = 192
QUARTER = ROWS // NY
IMAGES = ZLO * QUARTER
TEXTS = 24
SLOTS = NX * NY
OWN = SLOTS * TEXTS
COLUMNS = 2 * OWN
GROUP = 4 * TEXTS
LANES = 128
TILES = D // LANES
PACKED = 224
WIDE = D // 2
SLOT = D // 8
BATCH = 12288
STRIDE = 2
Z_SIDES = ((-1, 8), (1, 7))
ORDER = (0, 1, 7, 2, 6, 3, 5, 4)
NEAR = 3
COPIES = 3 + 4 + 12 + 7 + 15 + 4 + 6 + 3 + 3 + 13
F32, BF16 = jnp.float32, jnp.bfloat16
VMEM_LIMIT = 48 * 1024 * 1024


class Peers:
    def __init__(self):
        blk, grp = lax.axis_index("blk"), lax.axis_index("grp")
        z_hi, self.y = blk // NY, blk % NY
        self.core, z_lo, self.x = grp % 2, (grp // 2) % ZLO, grp // (2 * ZLO)
        self.z = z_hi * ZLO + z_lo
        self.sign = 1 - 2 * self.core

    def at(self, x, y, z, core):
        return ((z // ZLO) * NY + y, (x * ZLO + z % ZLO) * 2 + core)

    def other_core(self):
        return self.at(self.x, self.y, self.z, 1 - self.core)

    def along_x(self, step):
        return self.at((self.x + step) % NX, self.y, self.z, self.core)

    def along_y(self, step):
        return self.at(self.x, (self.y + step) % NY, self.z, self.core)

    def first_axis(self, step):
        return self.at(
            (self.x + step * (1 - self.core)) % NX,
            (self.y + step * self.core) % NY,
            self.z,
            self.core,
        )

    def second_axis(self, step):
        return self.at(
            (self.x + step * self.core) % NX,
            (self.y + step * (1 - self.core)) % NY,
            self.z,
            self.core,
        )

    def z_of(self, step):
        return (self.z + self.sign * step + NZ) % NZ

    def along_z(self, step):
        return self.at(self.x, self.y, self.z_of(step), self.core)


class Copies:
    def __init__(self, send_sem, recv_sem):
        self.send_sem, self.recv_sem, self.made = send_sem, recv_sem, []
        self.sent = 0

    def start(self, source, target, device_id):
        at = len(self.made)
        copy = pltpu.make_async_remote_copy(
            src_ref=source,
            dst_ref=target,
            send_sem=self.send_sem.at[at],
            recv_sem=self.recv_sem.at[at],
            device_id=device_id,
            device_id_type=MESH,
        )
        copy.start()
        self.made.append(copy)
        return copy

    def finish(self):
        for copy in self.made[self.sent :]:
            copy.wait_send()
        self.sent = len(self.made)


def pack(rows):
    pieces = [rows[:, k * LANES : (k + 1) * LANES] for k in range(TILES)]
    pieces.append(jnp.zeros((PACKED - TILES * TEXTS, LANES), F32))
    return jnp.concatenate(pieces, axis=0)


def unpack(packed):
    return jnp.concatenate(
        [packed[k * TEXTS : (k + 1) * TEXTS, :] for k in range(TILES)], axis=1
    )


def row_inverse(values):
    return lax.rsqrt(jnp.sum(values * values, axis=1, keepdims=True) + epsilon)


def narrow(rows):
    pieces = [rows[8 * k : 8 * k + 8, LANES:] for k in range(QUARTER // 8)]
    pieces.append(jnp.zeros((8, LANES - (SLOT - LANES) * QUARTER // 8), F32))
    return jnp.concatenate([rows[:, :LANES], jnp.concatenate(pieces, axis=1)], axis=0)


def widen(packed):
    rest = SLOT - LANES
    pieces = [packed[QUARTER:, rest * k : rest * (k + 1)] for k in range(QUARTER // 8)]
    return jnp.concatenate([packed[:QUARTER, :], jnp.concatenate(pieces, axis=0)], axis=1)


def hop(distance):
    return distance % STRIDE or STRIDE


def aligned(start, size):
    return pl.ds(pl.multiple_of(start, size), size)


def kernel(
    log_temp_in,
    bias_in,
    image_in,
    text_in,
    grad_image,
    grad_text,
    totals,
    log_temp,
    bias,
    image,
    text,
    images,
    own_texts,
    other_texts,
    text_bf,
    image_bf,
    similar,
    weights,
    grads,
    halves,
    text_part,
    core_send,
    core_land,
    b_send,
    b_land,
    a_send,
    a_land,
    z_send,
    z_land,
    y_send,
    y_land,
    s_send,
    s_land,
    send_sem,
    recv_sem,
    local_sem,
):
    peers = Peers()
    copies = Copies(send_sem, recv_sem)
    x, y, z, core = peers.x, peers.y, peers.z, peers.core

    image_copy = pltpu.make_async_copy(image_in, image, local_sem.at[0])
    text_copy = pltpu.make_async_copy(text_in, text, local_sem.at[1])
    scalar_copies = [
        pltpu.make_async_copy(log_temp_in, log_temp, local_sem.at[2]),
        pltpu.make_async_copy(bias_in, bias, local_sem.at[3]),
    ]
    for copy in (text_copy, image_copy, *scalar_copies):
        copy.start()
    barrier = pltpu.get_barrier_semaphore()
    met = (
        [peers.other_core()]
        + [peers.along_x(step) for step in range(1, NX)]
        + [peers.along_y(step) for step in range(1, NY)]
        + [peers.along_z(step) for step in (-4, -3, -2, -1, 1, 2, 3, 4, 8)]
    )
    for device_id in met:
        pl.semaphore_signal(barrier, inc=1, device_id=device_id, device_id_type=MESH)
    text_copy.wait()
    own_texts[0] = pack(text[...].astype(F32)).astype(BF16)
    image_copy.wait()
    images[0] = image[aligned(y * QUARTER, QUARTER), :]
    for copy in scalar_copies:
        copy.wait()
    pl.semaphore_wait(barrier, len(met))

    crossing, over_core, over_z = {}, {}, {}

    def text_forward(b):
        slots = pl.ds(4 * b, 4)
        over_core[b] = copies.start(
            own_texts.at[slots], other_texts.at[slots], peers.other_core()
        )

    def text_spread(a):
        crossing[a, 1] = copies.start(own_texts.at[a], own_texts.at[4 + a], peers.second_axis(3))
        crossing[a, 3] = copies.start(own_texts.at[a], own_texts.at[12 + a], peers.second_axis(1))

    def image_forward(distance, side):
        source = (distance if side > 0 else ZLO - distance) % ZLO
        target = (distance + 1 if side > 0 else ZLO - distance - 1) % ZLO
        over_z[target] = copies.start(
            images.at[ORDER.index(source)], images.at[ORDER.index(target)], peers.along_z(-side)
        )

    crossing[1, 0] = copies.start(own_texts.at[0], own_texts.at[1], peers.first_axis(3))
    crossing[3, 0] = copies.start(own_texts.at[0], own_texts.at[3], peers.first_axis(1))
    crossing[2, 0] = copies.start(own_texts.at[0], own_texts.at[2], peers.first_axis(2))
    image_forward(0, 1)
    image_forward(0, -1)
    text_spread(0)

    def image_ready(place):
        rows = pl.ds(place * QUARTER, QUARTER)
        values = images[place].astype(F32)
        image_bf[rows, :] = (values * row_inverse(values)).astype(BF16)

    def texts_ready(texts, b, first):
        for half in range(2):
            slot = b * 4 + 2 * half
            rows = jnp.concatenate(
                [unpack(texts[slot + k].astype(F32)) for k in range(2)], axis=0
            )
            text_bf[pl.ds(first + slot * TEXTS, 2 * TEXTS), :] = (
                rows * row_inverse(rows)
            ).astype(BF16)

    image_ready(0)
    for a in (1, 3, 2):
        crossing[a, 0].wait_recv()
        text_spread(a)
    text_forward(0)
    for target, side in ((1, 1), (7, -1)):
        over_z[target].wait_recv()
        image_forward(1, side)
    texts_ready(own_texts, 0, 0)
    image_ready(1)
    image_ready(2)
    for a in (0, 1, 3, 2):
        for b in (1, 3):
            crossing[a, b].wait_recv()
            if (b == 1) == (a in (0, 3)):
                step = 3 if b == 1 else 1
                crossing[a, 2] = copies.start(
                    own_texts.at[b * 4 + a], own_texts.at[8 + a], peers.second_axis(step)
                )
    text_forward(1)
    text_forward(3)
    for target, side in ((2, 1), (6, -1)):
        over_z[target].wait_recv()
        image_forward(2, side)
    texts_ready(own_texts, 1, 0)
    texts_ready(own_texts, 3, 0)

    def others_ready(b):
        over_core[b].wait_recv()
        texts_ready(other_texts, b, OWN)

    others_ready(0)
    for a in (0, 1, 3, 2):
        crossing[a, 2].wait_recv()
    text_forward(2)
    texts_ready(own_texts, 2, 0)
    others_ready(1)
    others_ready(3)

    scale = jnp.exp(jnp.full((1, 1), log_temp[0], F32))
    shift = bias[0]
    column = lax.broadcasted_iota(jnp.int32, (1, COLUMNS), 1)
    block = (column * 2731) >> 16
    text_core = ((block >> 4) + core) & 1
    on_first, on_second = block & 3, (block >> 2) & 3
    text_x = (x + jnp.where(text_core == 0, on_first, on_second)) & (NX - 1)
    text_y = (y + jnp.where(text_core == 0, on_second, on_first)) & (NY - 1)
    text_ids = (
        ((z // ZLO) * NY + text_y) * (BATCH // 8)
        + ((text_x * ZLO + z % ZLO) * 2 + text_core) * TEXTS
        + column
        - block * TEXTS
    )

    def weigh(low, high, lanes, carry):
        rows = pl.ds(low * QUARTER, (high - low) * QUARTER)
        similar[rows, lanes] = lax.dot_general(
            image_bf[rows, :],
            text_bf[lanes, :],
            (((1,), (1,)), ((), ())),
            preferred_element_type=F32,
        )
        ids = text_ids[:, lanes.start : lanes.start + lanes.size]

        def step(place, carry):
            losses, dlogits, weighted = carry
            rows = aligned(place * QUARTER, QUARTER)
            distance = ((place + 1) // 2) * (2 * (place % 2) - 1)
            image_z = (z + peers.sign * distance + NZ) % ZLO
            first = ((x * ZLO + image_z) * 2 + core) * ROWS + y * QUARTER
            same = first + lax.broadcasted_iota(jnp.int32, (QUARTER, 1), 0) == ids
            product = similar[rows, lanes]
            logits = scale * product + shift
            power = jnp.exp(jnp.where(same, -logits, logits))
            above = 1.0 + power
            chance = power / above
            dlogit = jnp.where(same, -chance, chance)
            weights[rows, lanes] = (scale * dlogit).astype(BF16)
            losses = losses + jnp.sum(jnp.log(above), axis=0, keepdims=True)
            dlogits = dlogits + jnp.sum(dlogit, axis=0, keepdims=True)
            weighted = weighted + jnp.sum(dlogit * product, axis=0, keepdims=True)
            return losses, dlogits, weighted

        return lax.fori_loop(low, high, step, carry)

    def project(place):
        values = images[place].astype(F32)
        unit = values * row_inverse(values)
        grad = grads[aligned(place * QUARTER, QUARTER), :]
        grad = grad - unit * jnp.sum(unit * grad, axis=1, keepdims=True)
        halves[place, 0] = grad[:, :WIDE]
        halves[place, 1] = grad[:, WIDE:]

    def image_grads(low, high):
        rows = pl.ds(low * QUARTER, (high - low) * QUARTER)
        grads[rows, :] = jnp.dot(weights[rows, :], text_bf[...], preferred_element_type=F32)
        pl.loop(low, high)(project)

    index = {}
    for side, most in Z_SIDES:
        for far in range(most, 0, -1):
            index[side, far] = len(index)
    flying = {}

    def part(step):
        return halves[ORDER.index(step % ZLO), peers.z_of(step) // ZLO]

    def gathered(side, most, to, value):
        for far in range(to + 1, min(to + STRIDE, most) + 1):
            flying[side, far].wait_recv()
            value = value + z_land[index[side, far]].astype(F32)
        return value

    def z_start(far):
        for side, most in Z_SIDES:
            if far > most:
                continue
            value = part(side * far)
            if far % STRIDE == 0:
                value = gathered(side, most, far, value)
            at = index[side, far]
            z_send[at] = value.astype(BF16)
            flying[side, far] = copies.start(
                z_send.at[at], z_land.at[at], peers.along_z(side * hop(far))
            )

    scalar = {"stage": 0, "slot": 0, "value": None}

    def scalar_send(value, to):
        stage = scalar["stage"]
        scalar["value"] = value
        s_send[stage] = value
        made = []
        for peer in to:
            slot = scalar["slot"]
            made.append((copies.start(s_send.at[stage], s_land.at[slot], peer), slot))
            scalar["slot"] += 1
        scalar["stage"] += 1
        return made

    def scalar_sum(made):
        value = scalar["value"]
        for copy, slot in made:
            copy.wait_recv()
            value = value + s_land[slot]
        return value

    own_lanes, other_lanes = pl.ds(0, OWN), pl.ds(OWN, OWN)
    zero = jnp.zeros((1, OWN), F32)
    carry = weigh(0, NEAR, own_lanes, (zero, zero, zero))
    over_z[3].wait_recv()
    image_forward(3, 1)
    others_ready(2)
    carry = weigh(0, NEAR, other_lanes, carry)
    image_grads(0, NEAR)
    for far in (8, 7, 1):
        z_start(far)
    for place in (3, 4, 5):
        image_ready(place)
    over_z[5].wait_recv()
    image_ready(6)
    over_z[4].wait_recv()
    image_ready(7)
    wide_zero = jnp.zeros((1, COLUMNS), F32)
    late = weigh(NEAR, ZLO, pl.ds(0, COLUMNS), (wide_zero, wide_zero, wide_zero))

    row = lax.broadcasted_iota(jnp.int32, (8, LANES), 0)
    total = jnp.zeros((8, LANES), F32)
    for k in range(3):
        part_sum = jnp.sum(carry[k], axis=1, keepdims=True)
        part_sum = part_sum + jnp.sum(late[k], axis=1, keepdims=True)
        total = jnp.where(row == k, part_sum, total)
    made = scalar_send(total, [peers.other_core()])

    def text_product(lanes):
        text_part[lanes, :] = lax.dot_general(
            weights[:, lanes],
            image_bf[...],
            (((0,), (0,)), ((), ())),
            preferred_element_type=F32,
        )

    text_product(other_lanes)
    pairs = {}
    for b in (2, 1, 3, 0):
        core_send[b] = text_part[pl.ds(OWN + b * GROUP, GROUP), :].astype(BF16)
        pairs[b] = copies.start(core_send.at[b], core_land.at[b], peers.other_core())
    image_grads(NEAR, ZLO)
    for far in (6, 5, 3):
        z_start(far)
    made = scalar_send(scalar_sum(made), [peers.along_x(step) for step in range(1, NX)])
    text_product(own_lanes)
    made = scalar_send(scalar_sum(made), [peers.along_y(step) for step in range(1, NY)])

    def pair_sum(b):
        pairs[b].wait_recv()
        return text_part[pl.ds(b * GROUP, GROUP), :] + core_land[b].astype(F32)

    across = {}

    def b_start(at, value, step):
        b_send[at] = value.astype(BF16)
        across[at] = copies.start(b_send.at[at], b_land.at[at], peers.second_axis(step))

    def b_landed(at):
        across[at].wait_recv()
        return b_land[at].astype(F32)

    low, high = slice(0, GROUP // 2), slice(GROUP // 2, GROUP)
    opposite = pair_sum(2)
    b_start(0, opposite[low], 1)
    b_start(1, opposite[high], 3)
    above, below = pair_sum(1), pair_sum(3)
    b_start(2, above[high], 1)
    b_start(3, below[low], 3)
    text_sum = pair_sum(0)
    made = scalar_send(scalar_sum(made), [peers.along_z(step) for step in (4, 8, -4)])
    z_start(4)
    b_start(4, above[low] + b_landed(0), 1)
    b_start(5, below[high] + b_landed(1), 3)
    z_start(2)
    text_sum = jnp.concatenate(
        [
            text_sum[low] + b_landed(3) + b_landed(4),
            text_sum[high] + b_landed(2) + b_landed(5),
        ],
        axis=0,
    )
    last = []
    for a in (2, 1, 3):
        a_send[a - 1] = pack(text_sum[a * TEXTS : (a + 1) * TEXTS, :]).astype(BF16)
        last.append((copies.start(a_send.at[a - 1], a_land.at[3 - a], peers.first_axis(a)), 3 - a))
    text_sum = pack(text_sum[:TEXTS, :])
    text_values = text[...].astype(F32)
    text_inverse = row_inverse(text_values)
    text_unit = text_values * text_inverse
    made = scalar_send(scalar_sum(made), [peers.along_z(step) for step in (1, 2, 3)])
    quarters = [aligned(((y + k) % NY) * QUARTER, QUARTER) for k in range(NY)]
    inverses = [row_inverse(image[rows, :].astype(F32)) for rows in quarters]

    grad = part(0)
    for side, most in Z_SIDES:
        grad = gathered(side, most, 0, grad)
    for k in range(NY):
        y_send[k] = narrow(grad[:, k * SLOT : (k + 1) * SLOT])
    over_y = {}
    for step in (2, 1, 3):
        over_y[NY - step] = copies.start(
            y_send.at[(y + step) % NY], y_land.at[NY - step - 1], peers.along_y(step)
        )
    grad_image[quarters[0], :] = widen(y_send[y]) * inverses[0]
    copies.finish()

    for copy, slot in last:
        copy.wait_recv()
        text_sum = text_sum + a_land[slot].astype(F32)
    text_sum = unpack(text_sum)
    inner = jnp.sum(text_unit * text_sum, axis=1, keepdims=True)
    grad_text[...] = (text_sum - text_unit * inner) * text_inverse
    for k in range(1, NY):
        over_y[k].wait_recv()
        grad_image[quarters[k], :] = widen(y_land[k - 1]) * inverses[k]
    factor = jnp.where(row == 0, 1.0 / BATCH, jnp.where(row == 2, scale, 1.0))
    totals[...] = scalar_sum(made) * factor
    copies.finish()


def shards(image_emb, text_emb, log_temp, bias):
    vmem = pl.BlockSpec(memory_space=pltpu.VMEM)
    anywhere = pl.BlockSpec(memory_space=pl.ANY)
    grad_image, grad_text, totals = pl.pallas_call(
        kernel,
        out_shape=(
            jax.ShapeDtypeStruct((ROWS, SLOT), F32),
            jax.ShapeDtypeStruct((TEXTS, D), F32),
            jax.ShapeDtypeStruct((8, LANES), F32),
        ),
        in_specs=[anywhere] * 4,
        out_specs=(vmem,) * 3,
        scratch_shapes=[
            pltpu.SMEM((1,), F32),
            pltpu.SMEM((1,), F32),
            pltpu.VMEM((ROWS, D), BF16),
            pltpu.VMEM((TEXTS, D), BF16),
            pltpu.VMEM((ZLO, QUARTER, D), BF16),
            pltpu.VMEM((SLOTS, PACKED, LANES), BF16),
            pltpu.VMEM((SLOTS, PACKED, LANES), BF16),
            pltpu.VMEM((COLUMNS, D), BF16),
            pltpu.VMEM((IMAGES, D), BF16),
            pltpu.VMEM((IMAGES, COLUMNS), F32),
            pltpu.VMEM((IMAGES, COLUMNS), BF16),
            pltpu.VMEM((IMAGES, D), F32),
            pltpu.VMEM((ZLO, 2, QUARTER, WIDE), F32),
            pltpu.VMEM((COLUMNS, D), F32),
            pltpu.VMEM((4, GROUP, D), BF16),
            pltpu.VMEM((4, GROUP, D), BF16),
            pltpu.VMEM((6, GROUP // 2, D), BF16),
            pltpu.VMEM((6, GROUP // 2, D), BF16),
            pltpu.VMEM((3, PACKED, LANES), BF16),
            pltpu.VMEM((3, PACKED, LANES), BF16),
            pltpu.VMEM((15, QUARTER, WIDE), BF16),
            pltpu.VMEM((15, QUARTER, WIDE), BF16),
            pltpu.VMEM((NY, QUARTER + 8, LANES), F32),
            pltpu.VMEM((NY - 1, QUARTER + 8, LANES), F32),
            pltpu.VMEM((5, 8, LANES), F32),
            pltpu.VMEM((13, 8, LANES), F32),
            pltpu.SemaphoreType.DMA((COPIES,)),
            pltpu.SemaphoreType.DMA((COPIES,)),
            pltpu.SemaphoreType.DMA((4,)),
        ],
        compiler_params=pltpu.CompilerParams(
            collective_id=0, has_side_effects=True, vmem_limit_bytes=VMEM_LIMIT
        ),
    )(log_temp, bias, image_emb, text_emb)
    return (totals[0, :1], grad_image, grad_text, totals[2, :1], totals[1, :1])


def solution(mesh):
    return jax.shard_map(
        shards,
        mesh=mesh,
        in_specs=(P("grp", None), P(("blk", "grp"), None), P(), P()),
        out_specs=(P(), P("grp", "blk"), P(("blk", "grp"), None), P(), P()),
        check_vma=False,
    )
```

```python
import jax
import jax.numpy as jnp
from jax import lax
from jax.experimental import pallas as pl
from jax.experimental.pallas import tpu as pltpu
from jax.sharding import PartitionSpec as P

MESH = pl.DeviceIdType.MESH
epsilon = 1e-06

NX, NY, NZ, ZLO = 4, 4, 16, 8
D = 1152
ROWS = 192
QUARTER = ROWS // NY
IMAGES = ZLO * QUARTER
TEXTS = 24
SLOTS = NX * NY
OWN = SLOTS * TEXTS
COLUMNS = 2 * OWN
GROUP = 4 * TEXTS
LANES = 128
TILES = D // LANES
PACKED = 224
WIDE = D // 2
SLOT = D // 8
BATCH = 12288
STRIDE = 2
Z_SIDES = ((-1, 8), (1, 7))
ORDER = (0, 1, 7, 2, 6, 3, 5, 4)
NEAR = 3
COPIES = 3 + 4 + 12 + 7 + 15 + 4 + 6 + 3 + 3 + 13
F32, BF16 = jnp.float32, jnp.bfloat16
VMEM_LIMIT = 48 * 1024 * 1024


class Peers:
    def __init__(self):
        blk, grp = lax.axis_index("blk"), lax.axis_index("grp")
        z_hi, self.y = blk // NY, blk % NY
        self.core, z_lo, self.x = grp % 2, (grp // 2) % ZLO, grp // (2 * ZLO)
        self.z = z_hi * ZLO + z_lo
        self.sign = 1 - 2 * self.core

    def at(self, x, y, z, core):
        return ((z // ZLO) * NY + y, (x * ZLO + z % ZLO) * 2 + core)

    def other_core(self):
        return self.at(self.x, self.y, self.z, 1 - self.core)

    def along_x(self, step):
        return self.at((self.x + step) % NX, self.y, self.z, self.core)

    def along_y(self, step):
        return self.at(self.x, (self.y + step) % NY, self.z, self.core)

    def first_axis(self, step):
        return self.at(
            (self.x + step * self.core) % NX,
            (self.y + step * (1 - self.core)) % NY,
            self.z,
            self.core,
        )

    def second_axis(self, step):
        return self.at(
            (self.x + step * (1 - self.core)) % NX,
            (self.y + step * self.core) % NY,
            self.z,
            self.core,
        )

    def z_of(self, step):
        return (self.z + self.sign * step + NZ) % NZ

    def along_z(self, step):
        return self.at(self.x, self.y, self.z_of(step), self.core)


class Copies:
    def __init__(self, send_sem, recv_sem):
        self.send_sem, self.recv_sem, self.made = send_sem, recv_sem, []
        self.sent = 0

    def start(self, source, target, device_id):
        at = len(self.made)
        copy = pltpu.make_async_remote_copy(
            src_ref=source,
            dst_ref=target,
            send_sem=self.send_sem.at[at],
            recv_sem=self.recv_sem.at[at],
            device_id=device_id,
            device_id_type=MESH,
        )
        copy.start()
        self.made.append(copy)
        return copy

    def finish(self):
        for copy in self.made[self.sent :]:
            copy.wait_send()
        self.sent = len(self.made)


def pack(rows):
    pieces = [rows[:, k * LANES : (k + 1) * LANES] for k in range(TILES)]
    pieces.append(jnp.zeros((PACKED - TILES * TEXTS, LANES), F32))
    return jnp.concatenate(pieces, axis=0)


def unpack(packed):
    return jnp.concatenate(
        [packed[k * TEXTS : (k + 1) * TEXTS, :] for k in range(TILES)], axis=1
    )


def row_inverse(values):
    return lax.rsqrt(jnp.sum(values * values, axis=1, keepdims=True) + epsilon)


def narrow(rows):
    pieces = [rows[8 * k : 8 * k + 8, LANES:] for k in range(QUARTER // 8)]
    pieces.append(jnp.zeros((8, LANES - (SLOT - LANES) * QUARTER // 8), F32))
    return jnp.concatenate([rows[:, :LANES], jnp.concatenate(pieces, axis=1)], axis=0)


def widen(packed):
    rest = SLOT - LANES
    pieces = [packed[QUARTER:, rest * k : rest * (k + 1)] for k in range(QUARTER // 8)]
    return jnp.concatenate([packed[:QUARTER, :], jnp.concatenate(pieces, axis=0)], axis=1)


def hop(distance):
    return distance % STRIDE or STRIDE


def aligned(start, size):
    return pl.ds(pl.multiple_of(start, size), size)


def kernel(
    log_temp_in,
    bias_in,
    image_in,
    text_in,
    grad_image,
    grad_text,
    totals,
    log_temp,
    bias,
    image,
    text,
    images,
    own_texts,
    other_texts,
    text_bf,
    image_bf,
    similar,
    weights,
    grads,
    halves,
    text_part,
    core_send,
    core_land,
    b_send,
    b_land,
    a_send,
    a_land,
    z_send,
    z_land,
    y_send,
    y_land,
    s_send,
    s_land,
    send_sem,
    recv_sem,
    local_sem,
):
    peers = Peers()
    copies = Copies(send_sem, recv_sem)
    x, y, z, core = peers.x, peers.y, peers.z, peers.core

    image_copy = pltpu.make_async_copy(image_in, image, local_sem.at[0])
    text_copy = pltpu.make_async_copy(text_in, text, local_sem.at[1])
    scalar_copies = [
        pltpu.make_async_copy(log_temp_in, log_temp, local_sem.at[2]),
        pltpu.make_async_copy(bias_in, bias, local_sem.at[3]),
    ]
    for copy in (text_copy, image_copy, *scalar_copies):
        copy.start()
    barrier = pltpu.get_barrier_semaphore()
    met = (
        [peers.other_core()]
        + [peers.along_x(step) for step in range(1, NX)]
        + [peers.along_y(step) for step in range(1, NY)]
        + [peers.along_z(step) for step in (-4, -3, -2, -1, 1, 2, 3, 4, 8)]
    )
    for device_id in met:
        pl.semaphore_signal(barrier, inc=1, device_id=device_id, device_id_type=MESH)
    text_copy.wait()
    own_texts[0] = pack(text[...].astype(F32)).astype(BF16)
    image_copy.wait()
    images[0] = image[aligned(y * QUARTER, QUARTER), :]
    for copy in scalar_copies:
        copy.wait()
    def image_ready(place):
        rows = pl.ds(place * QUARTER, QUARTER)
        values = images[place].astype(F32)
        image_bf[rows, :] = (values * row_inverse(values)).astype(BF16)

    image_ready(0)
    quarters = [aligned(((y + k) % NY) * QUARTER, QUARTER) for k in range(NY)]
    inverses = [row_inverse(image[rows, :].astype(F32)) for rows in quarters]

    pl.semaphore_wait(barrier, len(met))

    crossing, over_core, over_z = {}, {}, {}

    def text_forward(b):
        slots = pl.ds(4 * b, 4)
        over_core[b] = copies.start(
            own_texts.at[slots], other_texts.at[slots], peers.other_core()
        )

    def text_spread(a):
        crossing[a, 1] = copies.start(own_texts.at[a], own_texts.at[4 + a], peers.second_axis(3))
        crossing[a, 3] = copies.start(own_texts.at[a], own_texts.at[12 + a], peers.second_axis(1))

    def image_forward(distance, side):
        source = (distance if side > 0 else ZLO - distance) % ZLO
        target = (distance + 1 if side > 0 else ZLO - distance - 1) % ZLO
        over_z[target] = copies.start(
            images.at[ORDER.index(source)], images.at[ORDER.index(target)], peers.along_z(-side)
        )

    crossing[1, 0] = copies.start(own_texts.at[0], own_texts.at[1], peers.first_axis(3))
    crossing[3, 0] = copies.start(own_texts.at[0], own_texts.at[3], peers.first_axis(1))
    crossing[2, 0] = copies.start(own_texts.at[0], own_texts.at[2], peers.first_axis(2))
    image_forward(0, 1)
    image_forward(0, -1)
    text_spread(0)

    def texts_ready(texts, b, first):
        for half in range(2):
            slot = b * 4 + 2 * half
            rows = jnp.concatenate(
                [unpack(texts[slot + k].astype(F32)) for k in range(2)], axis=0
            )
            text_bf[pl.ds(first + slot * TEXTS, 2 * TEXTS), :] = (
                rows * row_inverse(rows)
            ).astype(BF16)

    for a in (1, 3, 2):
        crossing[a, 0].wait_recv()
        text_spread(a)
    text_forward(0)
    for target, side in ((1, 1), (7, -1)):
        over_z[target].wait_recv()
        image_forward(1, side)
    texts_ready(own_texts, 0, 0)
    image_ready(1)
    image_ready(2)
    for a in (0, 1, 3, 2):
        for b in (1, 3):
            crossing[a, b].wait_recv()
            if (b == 1) == (a in (0, 3)):
                step = 3 if b == 1 else 1
                crossing[a, 2] = copies.start(
                    own_texts.at[b * 4 + a], own_texts.at[8 + a], peers.second_axis(step)
                )
    text_forward(1)
    text_forward(3)
    for target, side in ((2, 1), (6, -1)):
        over_z[target].wait_recv()
        image_forward(2, side)
    texts_ready(own_texts, 1, 0)
    texts_ready(own_texts, 3, 0)

    def others_ready(b):
        over_core[b].wait_recv()
        texts_ready(other_texts, b, OWN)

    others_ready(0)
    for a in (0, 1, 3, 2):
        crossing[a, 2].wait_recv()
    text_forward(2)
    texts_ready(own_texts, 2, 0)
    others_ready(1)
    others_ready(3)

    scale = jnp.exp(jnp.full((1, 1), log_temp[0], F32))
    shift = bias[0]
    column = lax.broadcasted_iota(jnp.int32, (1, COLUMNS), 1)
    block = (column * 2731) >> 16
    text_core = ((block >> 4) + core) & 1
    on_first, on_second = block & 3, (block >> 2) & 3
    text_x = (x + jnp.where(text_core == 0, on_second, on_first)) & (NX - 1)
    text_y = (y + jnp.where(text_core == 0, on_first, on_second)) & (NY - 1)
    text_ids = (
        ((z // ZLO) * NY + text_y) * (BATCH // 8)
        + ((text_x * ZLO + z % ZLO) * 2 + text_core) * TEXTS
        + column
        - block * TEXTS
    )

    def weigh(low, high, lanes, carry):
        rows = pl.ds(low * QUARTER, (high - low) * QUARTER)
        similar[rows, lanes] = lax.dot_general(
            image_bf[rows, :],
            text_bf[lanes, :],
            (((1,), (1,)), ((), ())),
            preferred_element_type=F32,
        )
        ids = text_ids[:, lanes.start : lanes.start + lanes.size]

        def step(place, carry):
            losses, dlogits, weighted = carry
            rows = aligned(place * QUARTER, QUARTER)
            distance = ((place + 1) // 2) * (2 * (place % 2) - 1)
            image_z = (z + peers.sign * distance + NZ) % ZLO
            first = ((x * ZLO + image_z) * 2 + core) * ROWS + y * QUARTER
            same = first + lax.broadcasted_iota(jnp.int32, (QUARTER, 1), 0) == ids
            product = similar[rows, lanes]
            logits = scale * product + shift
            power = jnp.exp(jnp.where(same, -logits, logits))
            above = 1.0 + power
            chance = power / above
            dlogit = jnp.where(same, -chance, chance)
            weights[rows, lanes] = (scale * dlogit).astype(BF16)
            losses = losses + jnp.sum(jnp.log(above), axis=0, keepdims=True)
            dlogits = dlogits + jnp.sum(dlogit, axis=0, keepdims=True)
            weighted = weighted + jnp.sum(dlogit * product, axis=0, keepdims=True)
            return losses, dlogits, weighted

        return lax.fori_loop(low, high, step, carry)

    def project(place):
        values = images[place].astype(F32)
        unit = values * row_inverse(values)
        grad = grads[aligned(place * QUARTER, QUARTER), :]
        grad = grad - unit * jnp.sum(unit * grad, axis=1, keepdims=True)
        halves[place, 0] = grad[:, :WIDE]
        halves[place, 1] = grad[:, WIDE:]

    def image_grads(low, high):
        rows = pl.ds(low * QUARTER, (high - low) * QUARTER)
        grads[rows, :] = jnp.dot(weights[rows, :], text_bf[...], preferred_element_type=F32)
        pl.loop(low, high)(project)

    index = {}
    for side, most in Z_SIDES:
        for far in range(most, 0, -1):
            index[side, far] = len(index)
    flying = {}

    def part(step):
        return halves[ORDER.index(step % ZLO), peers.z_of(step) // ZLO]

    def gathered(side, most, to, value):
        for far in range(to + 1, min(to + STRIDE, most) + 1):
            flying[side, far].wait_recv()
            value = value + z_land[index[side, far]].astype(F32)
        return value

    def z_start(far):
        for side, most in Z_SIDES:
            if far > most:
                continue
            value = part(side * far)
            if far % STRIDE == 0:
                value = gathered(side, most, far, value)
            at = index[side, far]
            z_send[at] = value.astype(BF16)
            flying[side, far] = copies.start(
                z_send.at[at], z_land.at[at], peers.along_z(side * hop(far))
            )

    scalar = {"stage": 0, "slot": 0, "value": None}

    def scalar_send(value, to):
        stage = scalar["stage"]
        scalar["value"] = value
        s_send[stage] = value
        made = []
        for peer in to:
            slot = scalar["slot"]
            made.append((copies.start(s_send.at[stage], s_land.at[slot], peer), slot))
            scalar["slot"] += 1
        scalar["stage"] += 1
        return made

    def scalar_sum(made):
        value = scalar["value"]
        for copy, slot in made:
            copy.wait_recv()
            value = value + s_land[slot]
        return value

    own_lanes, other_lanes = pl.ds(0, OWN), pl.ds(OWN, OWN)
    zero = jnp.zeros((1, OWN), F32)
    carry = weigh(0, NEAR, own_lanes, (zero, zero, zero))
    over_z[3].wait_recv()
    image_forward(3, 1)
    others_ready(2)
    carry = weigh(0, NEAR, other_lanes, carry)
    image_grads(0, NEAR)
    for far in (8, 7, 1):
        z_start(far)
    for place in (3, 4, 5):
        image_ready(place)
    over_z[5].wait_recv()
    image_ready(6)
    over_z[4].wait_recv()
    image_ready(7)
    wide_zero = jnp.zeros((1, COLUMNS), F32)
    late = weigh(NEAR, ZLO, pl.ds(0, COLUMNS), (wide_zero, wide_zero, wide_zero))

    row = lax.broadcasted_iota(jnp.int32, (8, LANES), 0)
    total = jnp.zeros((8, LANES), F32)
    for k in range(3):
        part_sum = jnp.sum(carry[k], axis=1, keepdims=True)
        part_sum = part_sum + jnp.sum(late[k], axis=1, keepdims=True)
        total = jnp.where(row == k, part_sum, total)
    made = scalar_send(total, [peers.other_core()])

    def text_product(lanes):
        text_part[lanes, :] = lax.dot_general(
            weights[:, lanes],
            image_bf[...],
            (((0,), (0,)), ((), ())),
            preferred_element_type=F32,
        )

    text_product(other_lanes)
    pairs = {}
    for b in (2, 1, 3, 0):
        core_send[b] = text_part[pl.ds(OWN + b * GROUP, GROUP), :].astype(BF16)
        pairs[b] = copies.start(core_send.at[b], core_land.at[b], peers.other_core())
    image_grads(NEAR, ZLO)
    for far in (6, 5, 3):
        z_start(far)
    made = scalar_send(scalar_sum(made), [peers.along_x(step) for step in range(1, NX)])
    text_product(own_lanes)
    made = scalar_send(scalar_sum(made), [peers.along_y(step) for step in range(1, NY)])

    ready = set()

    def pair_sum(b, half):
        if b not in ready:
            pairs[b].wait_recv()
            ready.add(b)
        first = half * (GROUP // 2)
        mine = text_part[pl.ds(b * GROUP + first, GROUP // 2), :]
        return mine + core_land[b, pl.ds(first, GROUP // 2), :].astype(F32)

    across = {}

    def b_start(at, value, step):
        b_send[at] = value.astype(BF16)
        across[at] = copies.start(b_send.at[at], b_land.at[at], peers.second_axis(step))

    def b_landed(at):
        across[at].wait_recv()
        return b_land[at].astype(F32)

    b_start(0, pair_sum(2, 0), 1)
    b_start(1, pair_sum(2, 1), 3)
    b_start(2, pair_sum(1, 1), 1)
    b_start(3, pair_sum(3, 0), 3)
    made = scalar_send(scalar_sum(made), [peers.along_z(step) for step in (4, 8, -4)])
    z_start(4)
    b_start(4, pair_sum(1, 0) + b_landed(0), 1)
    b_start(5, pair_sum(3, 1) + b_landed(1), 3)
    z_start(2)
    last = []

    def a_start(a, rows):
        a_send[a - 1] = pack(rows).astype(BF16)
        last.append((copies.start(a_send.at[a - 1], a_land.at[3 - a], peers.first_axis(a)), 3 - a))

    rows = pair_sum(0, 1) + b_landed(2) + b_landed(5)
    a_start(2, rows[:TEXTS])
    a_start(3, rows[TEXTS:])
    rows = pair_sum(0, 0) + b_landed(3) + b_landed(4)
    a_start(1, rows[TEXTS:])
    text_sum = pack(rows[:TEXTS])
    text_values = text[...].astype(F32)
    text_inverse = row_inverse(text_values)
    text_unit = text_values * text_inverse
    made = scalar_send(scalar_sum(made), [peers.along_z(step) for step in (1, 2, 3)])
    grad = part(0)
    for side, most in Z_SIDES:
        grad = gathered(side, most, 0, grad)
    for k in range(NY):
        y_send[k] = narrow(grad[:, k * SLOT : (k + 1) * SLOT])
    over_y = {}
    for step in (2, 1, 3):
        over_y[NY - step] = copies.start(
            y_send.at[(y + step) % NY], y_land.at[NY - step - 1], peers.along_y(step)
        )
    grad_image[quarters[0], :] = widen(y_send[y]) * inverses[0]
    copies.finish()

    for copy, slot in last:
        copy.wait_recv()
        text_sum = text_sum + a_land[slot].astype(F32)
    text_sum = unpack(text_sum)
    inner = jnp.sum(text_unit * text_sum, axis=1, keepdims=True)
    grad_text[...] = (text_sum - text_unit * inner) * text_inverse
    for k in range(1, NY):
        over_y[k].wait_recv()
        grad_image[quarters[k], :] = widen(y_land[k - 1]) * inverses[k]
    factor = jnp.where(row == 0, 1.0 / BATCH, jnp.where(row == 2, scale, 1.0))
    totals[...] = scalar_sum(made) * factor
    copies.finish()


def shards(image_emb, text_emb, log_temp, bias):
    vmem = pl.BlockSpec(memory_space=pltpu.VMEM)
    anywhere = pl.BlockSpec(memory_space=pl.ANY)
    grad_image, grad_text, totals = pl.pallas_call(
        kernel,
        out_shape=(
            jax.ShapeDtypeStruct((ROWS, SLOT), F32),
            jax.ShapeDtypeStruct((TEXTS, D), F32),
            jax.ShapeDtypeStruct((8, LANES), F32),
        ),
        in_specs=[anywhere] * 4,
        out_specs=(vmem,) * 3,
        scratch_shapes=[
            pltpu.SMEM((1,), F32),
            pltpu.SMEM((1,), F32),
            pltpu.VMEM((ROWS, D), BF16),
            pltpu.VMEM((TEXTS, D), BF16),
            pltpu.VMEM((ZLO, QUARTER, D), BF16),
            pltpu.VMEM((SLOTS, PACKED, LANES), BF16),
            pltpu.VMEM((SLOTS, PACKED, LANES), BF16),
            pltpu.VMEM((COLUMNS, D), BF16),
            pltpu.VMEM((IMAGES, D), BF16),
            pltpu.VMEM((IMAGES, COLUMNS), F32),
            pltpu.VMEM((IMAGES, COLUMNS), BF16),
            pltpu.VMEM((IMAGES, D), F32),
            pltpu.VMEM((ZLO, 2, QUARTER, WIDE), F32),
            pltpu.VMEM((COLUMNS, D), F32),
            pltpu.VMEM((4, GROUP, D), BF16),
            pltpu.VMEM((4, GROUP, D), BF16),
            pltpu.VMEM((6, GROUP // 2, D), BF16),
            pltpu.VMEM((6, GROUP // 2, D), BF16),
            pltpu.VMEM((3, PACKED, LANES), BF16),
            pltpu.VMEM((3, PACKED, LANES), BF16),
            pltpu.VMEM((15, QUARTER, WIDE), BF16),
            pltpu.VMEM((15, QUARTER, WIDE), BF16),
            pltpu.VMEM((NY, QUARTER + 8, LANES), F32),
            pltpu.VMEM((NY - 1, QUARTER + 8, LANES), F32),
            pltpu.VMEM((5, 8, LANES), F32),
            pltpu.VMEM((13, 8, LANES), F32),
            pltpu.SemaphoreType.DMA((COPIES,)),
            pltpu.SemaphoreType.DMA((COPIES,)),
            pltpu.SemaphoreType.DMA((4,)),
        ],
        compiler_params=pltpu.CompilerParams(
            collective_id=0, has_side_effects=True, vmem_limit_bytes=VMEM_LIMIT
        ),
    )(log_temp, bias, image_emb, text_emb)
    return (totals[0, :1], grad_image, grad_text, totals[2, :1], totals[1, :1])


def solution(mesh):
    return jax.shard_map(
        shards,
        mesh=mesh,
        in_specs=(P("grp", None), P(("blk", "grp"), None), P(), P()),
        out_specs=(P(), P("grp", "blk"), P(("blk", "grp"), None), P(), P()),
        check_vma=False,
    )
```

```python
import jax
import jax.numpy as jnp
from jax import lax
from jax.experimental import pallas as pl
from jax.experimental.pallas import tpu as pltpu
from jax.sharding import PartitionSpec as P

MESH = pl.DeviceIdType.MESH
epsilon = 1e-06

NX, NY, NZ, ZLO = 4, 4, 16, 8
D = 1152
ROWS = 192
QUARTER = ROWS // NY
IMAGES = ZLO * QUARTER
TEXTS = 24
SLOTS = NX * NY
OWN = SLOTS * TEXTS
COLUMNS = 2 * OWN
GROUP = 4 * TEXTS
LANES = 128
TILES = D // LANES
PACKED = 224
WIDE = D // 2
SLOT = D // 8
BATCH = 12288
STRIDE = 2
Z_SIDES = ((-1, 8), (1, 7))
ORDER = (0, 1, 7, 2, 6, 3, 5, 4)
NEAR = 3
COPIES = 3 + 4 + 12 + 7 + 15 + 4 + 6 + 3 + 3 + 13
F32, BF16 = jnp.float32, jnp.bfloat16
VMEM_LIMIT = 48 * 1024 * 1024


class Peers:
    def __init__(self):
        blk, grp = lax.axis_index("blk"), lax.axis_index("grp")
        z_hi, self.y = blk // NY, blk % NY
        self.core, z_lo, self.x = grp % 2, (grp // 2) % ZLO, grp // (2 * ZLO)
        self.z = z_hi * ZLO + z_lo
        self.sign = 1 - 2 * self.core

    def at(self, x, y, z, core):
        return ((z // ZLO) * NY + y, (x * ZLO + z % ZLO) * 2 + core)

    def other_core(self):
        return self.at(self.x, self.y, self.z, 1 - self.core)

    def along_x(self, step):
        return self.at((self.x + step) % NX, self.y, self.z, self.core)

    def along_y(self, step):
        return self.at(self.x, (self.y + step) % NY, self.z, self.core)

    def first_axis(self, step):
        return self.at(
            (self.x + step * self.core) % NX,
            (self.y + step * (1 - self.core)) % NY,
            self.z,
            self.core,
        )

    def second_axis(self, step):
        return self.at(
            (self.x + step * (1 - self.core)) % NX,
            (self.y + step * self.core) % NY,
            self.z,
            self.core,
        )

    def z_of(self, step):
        return (self.z + self.sign * step + NZ) % NZ

    def along_z(self, step):
        return self.at(self.x, self.y, self.z_of(step), self.core)


class Copies:
    def __init__(self, send_sem, recv_sem):
        self.send_sem, self.recv_sem, self.made = send_sem, recv_sem, []
        self.sent = 0

    def start(self, source, target, device_id):
        at = len(self.made)
        copy = pltpu.make_async_remote_copy(
            src_ref=source,
            dst_ref=target,
            send_sem=self.send_sem.at[at],
            recv_sem=self.recv_sem.at[at],
            device_id=device_id,
            device_id_type=MESH,
        )
        copy.start()
        self.made.append(copy)
        return copy

    def finish(self):
        for copy in self.made[self.sent :]:
            copy.wait_send()
        self.sent = len(self.made)


def pack(rows):
    pieces = [rows[:, k * LANES : (k + 1) * LANES] for k in range(TILES)]
    pieces.append(jnp.zeros((PACKED - TILES * TEXTS, LANES), F32))
    return jnp.concatenate(pieces, axis=0)


def unpack(packed):
    return jnp.concatenate(
        [packed[k * TEXTS : (k + 1) * TEXTS, :] for k in range(TILES)], axis=1
    )


def row_inverse(values):
    return lax.rsqrt(jnp.sum(values * values, axis=1, keepdims=True) + epsilon)


def narrow(rows):
    pieces = [rows[8 * k : 8 * k + 8, LANES:] for k in range(QUARTER // 8)]
    pieces.append(jnp.zeros((8, LANES - (SLOT - LANES) * QUARTER // 8), F32))
    return jnp.concatenate([rows[:, :LANES], jnp.concatenate(pieces, axis=1)], axis=0)


def widen(packed):
    rest = SLOT - LANES
    pieces = [packed[QUARTER:, rest * k : rest * (k + 1)] for k in range(QUARTER // 8)]
    return jnp.concatenate([packed[:QUARTER, :], jnp.concatenate(pieces, axis=0)], axis=1)


def hop(distance):
    return distance % STRIDE or STRIDE


def aligned(start, size):
    return pl.ds(pl.multiple_of(start, size), size)


def kernel(
    log_temp_in,
    bias_in,
    image_in,
    text_in,
    grad_image,
    grad_text,
    totals,
    log_temp,
    bias,
    image,
    text,
    images,
    own_texts,
    other_texts,
    text_bf,
    image_bf,
    similar,
    weights,
    grads,
    halves,
    text_part,
    core_send,
    core_land,
    b_send,
    b_land,
    a_send,
    a_land,
    z_send,
    z_land,
    y_send,
    y_land,
    s_send,
    s_land,
    send_sem,
    recv_sem,
    local_sem,
):
    peers = Peers()
    copies = Copies(send_sem, recv_sem)
    x, y, z, core = peers.x, peers.y, peers.z, peers.core

    image_copy = pltpu.make_async_copy(image_in, image, local_sem.at[0])
    text_copy = pltpu.make_async_copy(text_in, text, local_sem.at[1])
    scalar_copies = [
        pltpu.make_async_copy(log_temp_in, log_temp, local_sem.at[2]),
        pltpu.make_async_copy(bias_in, bias, local_sem.at[3]),
    ]
    for copy in (text_copy, image_copy, *scalar_copies):
        copy.start()
    barrier = pltpu.get_barrier_semaphore()
    met = (
        [peers.other_core()]
        + [peers.along_x(step) for step in range(1, NX)]
        + [peers.along_y(step) for step in range(1, NY)]
        + [peers.along_z(step) for step in (-4, -3, -2, -1, 1, 2, 3, 4, 8)]
    )
    for device_id in met:
        pl.semaphore_signal(barrier, inc=1, device_id=device_id, device_id_type=MESH)
    text_copy.wait()
    own_texts[0] = pack(text[...].astype(F32)).astype(BF16)
    image_copy.wait()
    images[0] = image[aligned(y * QUARTER, QUARTER), :]
    for copy in scalar_copies:
        copy.wait()
    def image_ready(place):
        rows = pl.ds(place * QUARTER, QUARTER)
        values = images[place].astype(F32)
        image_bf[rows, :] = (values * row_inverse(values)).astype(BF16)

    image_ready(0)
    quarters = [aligned(((y + k) % NY) * QUARTER, QUARTER) for k in range(NY)]
    inverses = [row_inverse(image[rows, :].astype(F32)) for rows in quarters]

    pl.semaphore_wait(barrier, len(met))

    crossing, over_core, over_z = {}, {}, {}

    def text_forward(b):
        slots = pl.ds(4 * b, 4)
        over_core[b] = copies.start(
            own_texts.at[slots], other_texts.at[slots], peers.other_core()
        )

    def text_spread(a):
        crossing[a, 1] = copies.start(own_texts.at[a], own_texts.at[4 + a], peers.second_axis(3))
        crossing[a, 3] = copies.start(own_texts.at[a], own_texts.at[12 + a], peers.second_axis(1))

    def image_forward(distance, side):
        source = (distance if side > 0 else ZLO - distance) % ZLO
        target = (distance + 1 if side > 0 else ZLO - distance - 1) % ZLO
        over_z[target] = copies.start(
            images.at[ORDER.index(source)], images.at[ORDER.index(target)], peers.along_z(-side)
        )

    crossing[1, 0] = copies.start(own_texts.at[0], own_texts.at[1], peers.first_axis(3))
    crossing[3, 0] = copies.start(own_texts.at[0], own_texts.at[3], peers.first_axis(1))
    crossing[2, 0] = copies.start(own_texts.at[0], own_texts.at[2], peers.first_axis(2))
    image_forward(0, 1)
    image_forward(0, -1)
    text_spread(0)

    def texts_ready(texts, b, first):
        for half in range(2):
            slot = b * 4 + 2 * half
            rows = jnp.concatenate(
                [unpack(texts[slot + k].astype(F32)) for k in range(2)], axis=0
            )
            text_bf[pl.ds(first + slot * TEXTS, 2 * TEXTS), :] = (
                rows * row_inverse(rows)
            ).astype(BF16)

    for a in (1, 3, 2):
        crossing[a, 0].wait_recv()
        text_spread(a)
    text_forward(0)
    for target, side in ((1, 1), (7, -1)):
        over_z[target].wait_recv()
        image_forward(1, side)
    texts_ready(own_texts, 0, 0)
    image_ready(1)
    image_ready(2)
    for a in (0, 1, 3, 2):
        for b in (1, 3):
            crossing[a, b].wait_recv()
            if (b == 1) == (a in (0, 3)):
                step = 3 if b == 1 else 1
                crossing[a, 2] = copies.start(
                    own_texts.at[b * 4 + a], own_texts.at[8 + a], peers.second_axis(step)
                )
    text_forward(1)
    text_forward(3)
    for target, side in ((2, 1), (6, -1)):
        over_z[target].wait_recv()
        image_forward(2, side)
    texts_ready(own_texts, 1, 0)
    texts_ready(own_texts, 3, 0)

    def others_ready(b):
        over_core[b].wait_recv()
        texts_ready(other_texts, b, OWN)

    others_ready(0)
    for a in (0, 1, 3, 2):
        crossing[a, 2].wait_recv()
    text_forward(2)
    texts_ready(own_texts, 2, 0)
    others_ready(1)
    others_ready(3)

    scale = jnp.exp(jnp.full((1, 1), log_temp[0], F32))
    shift = bias[0]
    column = lax.broadcasted_iota(jnp.int32, (1, COLUMNS), 1)
    block = (column * 2731) >> 16
    text_core = ((block >> 4) + core) & 1
    on_first, on_second = block & 3, (block >> 2) & 3
    text_x = (x + jnp.where(text_core == 0, on_second, on_first)) & (NX - 1)
    text_y = (y + jnp.where(text_core == 0, on_first, on_second)) & (NY - 1)
    text_ids = (
        ((z // ZLO) * NY + text_y) * (BATCH // 8)
        + ((text_x * ZLO + z % ZLO) * 2 + text_core) * TEXTS
        + column
        - block * TEXTS
    )

    def weigh(low, high, lanes, carry):
        rows = pl.ds(low * QUARTER, (high - low) * QUARTER)
        similar[rows, lanes] = lax.dot_general(
            image_bf[rows, :],
            text_bf[lanes, :],
            (((1,), (1,)), ((), ())),
            preferred_element_type=F32,
        )
        ids = text_ids[:, lanes.start : lanes.start + lanes.size]

        def step(place, carry):
            losses, dlogits, weighted = carry
            rows = aligned(place * QUARTER, QUARTER)
            distance = ((place + 1) // 2) * (2 * (place % 2) - 1)
            image_z = (z + peers.sign * distance + NZ) % ZLO
            first = ((x * ZLO + image_z) * 2 + core) * ROWS + y * QUARTER
            same = first + lax.broadcasted_iota(jnp.int32, (QUARTER, 1), 0) == ids
            product = similar[rows, lanes]
            logits = scale * product + shift
            power = jnp.exp(jnp.where(same, -logits, logits))
            above = 1.0 + power
            chance = power / above
            dlogit = jnp.where(same, -chance, chance)
            weights[rows, lanes] = (scale * dlogit).astype(BF16)
            losses = losses + jnp.sum(jnp.log(above), axis=0, keepdims=True)
            dlogits = dlogits + jnp.sum(dlogit, axis=0, keepdims=True)
            weighted = weighted + jnp.sum(dlogit * product, axis=0, keepdims=True)
            return losses, dlogits, weighted

        return lax.fori_loop(low, high, step, carry)

    def project(place):
        values = images[place].astype(F32)
        unit = values * row_inverse(values)
        grad = grads[aligned(place * QUARTER, QUARTER), :]
        grad = grad - unit * jnp.sum(unit * grad, axis=1, keepdims=True)
        halves[place, 0] = grad[:, :WIDE]
        halves[place, 1] = grad[:, WIDE:]

    def image_grads(low, high):
        rows = pl.ds(low * QUARTER, (high - low) * QUARTER)
        grads[rows, :] = jnp.dot(weights[rows, :], text_bf[...], preferred_element_type=F32)
        pl.loop(low, high)(project)

    index = {}
    for side, most in Z_SIDES:
        for far in range(most, 0, -1):
            index[side, far] = len(index)
    flying = {}

    def part(step):
        return halves[ORDER.index(step % ZLO), peers.z_of(step) // ZLO]

    def gathered(side, most, to, value):
        for far in range(to + 1, min(to + STRIDE, most) + 1):
            flying[side, far].wait_recv()
            value = value + z_land[index[side, far]].astype(F32)
        return value

    def z_start(far):
        for side, most in Z_SIDES:
            if far > most:
                continue
            value = part(side * far)
            if far % STRIDE == 0:
                value = gathered(side, most, far, value)
            at = index[side, far]
            z_send[at] = value.astype(BF16)
            flying[side, far] = copies.start(
                z_send.at[at], z_land.at[at], peers.along_z(side * hop(far))
            )

    scalar = {"stage": 0, "slot": 0, "value": None}

    def scalar_send(value, to):
        stage = scalar["stage"]
        scalar["value"] = value
        s_send[stage] = value
        made = []
        for peer in to:
            slot = scalar["slot"]
            made.append((copies.start(s_send.at[stage], s_land.at[slot], peer), slot))
            scalar["slot"] += 1
        scalar["stage"] += 1
        return made

    def scalar_sum(made):
        value = scalar["value"]
        for copy, slot in made:
            copy.wait_recv()
            value = value + s_land[slot]
        return value

    own_lanes, other_lanes = pl.ds(0, OWN), pl.ds(OWN, OWN)
    zero = jnp.zeros((1, OWN), F32)
    carry = weigh(0, NEAR, own_lanes, (zero, zero, zero))
    over_z[3].wait_recv()
    image_forward(3, 1)
    others_ready(2)
    carry = weigh(0, NEAR, other_lanes, carry)
    image_grads(0, NEAR)
    z_start(8)
    z_start(7)
    for place in (3, 4, 5):
        image_ready(place)
    over_z[5].wait_recv()
    image_ready(6)
    over_z[4].wait_recv()
    image_ready(7)
    wide_zero = jnp.zeros((1, COLUMNS), F32)
    late = weigh(NEAR, ZLO, pl.ds(0, COLUMNS), (wide_zero, wide_zero, wide_zero))

    row = lax.broadcasted_iota(jnp.int32, (8, LANES), 0)
    total = jnp.zeros((8, LANES), F32)
    for k in range(3):
        part_sum = jnp.sum(carry[k], axis=1, keepdims=True)
        part_sum = part_sum + jnp.sum(late[k], axis=1, keepdims=True)
        total = jnp.where(row == k, part_sum, total)
    made = scalar_send(total, [peers.other_core()])

    def text_product(lanes):
        text_part[lanes, :] = lax.dot_general(
            weights[:, lanes],
            image_bf[...],
            (((0,), (0,)), ((), ())),
            preferred_element_type=F32,
        )

    text_product(other_lanes)
    pairs = {}
    for b in (2, 1, 3, 0):
        core_send[b] = text_part[pl.ds(OWN + b * GROUP, GROUP), :].astype(BF16)
        pairs[b] = copies.start(core_send.at[b], core_land.at[b], peers.other_core())
    image_grads(NEAR, ZLO)
    z_start(6)
    z_start(5)
    made = scalar_send(scalar_sum(made), [peers.along_x(step) for step in range(1, NX)])
    text_product(own_lanes)
    made = scalar_send(scalar_sum(made), [peers.along_y(step) for step in range(1, NY)])

    ready = set()

    def pair_sum(b, half):
        if b not in ready:
            pairs[b].wait_recv()
            ready.add(b)
        first = half * (GROUP // 2)
        mine = text_part[pl.ds(b * GROUP + first, GROUP // 2), :]
        return mine + core_land[b, pl.ds(first, GROUP // 2), :].astype(F32)

    across = {}

    def b_start(at, value, step):
        b_send[at] = value.astype(BF16)
        across[at] = copies.start(b_send.at[at], b_land.at[at], peers.second_axis(step))

    def b_landed(at):
        across[at].wait_recv()
        return b_land[at].astype(F32)

    b_start(0, pair_sum(2, 0), 1)
    b_start(1, pair_sum(2, 1), 3)
    b_start(2, pair_sum(1, 1), 1)
    b_start(3, pair_sum(3, 0), 3)
    made = scalar_send(scalar_sum(made), [peers.along_z(step) for step in (4, 8, -4)])
    z_start(4)
    z_start(3)
    b_start(4, pair_sum(1, 0) + b_landed(0), 1)
    b_start(5, pair_sum(3, 1) + b_landed(1), 3)
    z_start(2)
    z_start(1)
    last = []

    def a_start(a, rows):
        a_send[a - 1] = pack(rows).astype(BF16)
        last.append((copies.start(a_send.at[a - 1], a_land.at[3 - a], peers.first_axis(a)), 3 - a))

    rows = pair_sum(0, 1) + b_landed(2) + b_landed(5)
    a_start(2, rows[:TEXTS])
    a_start(3, rows[TEXTS:])
    rows = pair_sum(0, 0) + b_landed(3) + b_landed(4)
    a_start(1, rows[TEXTS:])
    text_sum = pack(rows[:TEXTS])
    text_values = text[...].astype(F32)
    text_inverse = row_inverse(text_values)
    text_unit = text_values * text_inverse
    made = scalar_send(scalar_sum(made), [peers.along_z(step) for step in (1, 2, 3)])
    grad = part(0)
    for side, most in Z_SIDES:
        grad = gathered(side, most, 0, grad)
    for k in range(NY):
        y_send[k] = narrow(grad[:, k * SLOT : (k + 1) * SLOT])
    over_y = {}
    for step in (2, 1, 3):
        over_y[NY - step] = copies.start(
            y_send.at[(y + step) % NY], y_land.at[NY - step - 1], peers.along_y(step)
        )
    grad_image[quarters[0], :] = widen(y_send[y]) * inverses[0]
    copies.finish()

    for copy, slot in last:
        copy.wait_recv()
        text_sum = text_sum + a_land[slot].astype(F32)
    text_sum = unpack(text_sum)
    inner = jnp.sum(text_unit * text_sum, axis=1, keepdims=True)
    grad_text[...] = (text_sum - text_unit * inner) * text_inverse
    for k in range(1, NY):
        over_y[k].wait_recv()
        grad_image[quarters[k], :] = widen(y_land[k - 1]) * inverses[k]
    factor = jnp.where(row == 0, 1.0 / BATCH, jnp.where(row == 2, scale, 1.0))
    totals[...] = scalar_sum(made) * factor
    copies.finish()


def shards(image_emb, text_emb, log_temp, bias):
    vmem = pl.BlockSpec(memory_space=pltpu.VMEM)
    anywhere = pl.BlockSpec(memory_space=pl.ANY)
    grad_image, grad_text, totals = pl.pallas_call(
        kernel,
        out_shape=(
            jax.ShapeDtypeStruct((ROWS, SLOT), F32),
            jax.ShapeDtypeStruct((TEXTS, D), F32),
            jax.ShapeDtypeStruct((8, LANES), F32),
        ),
        in_specs=[anywhere] * 4,
        out_specs=(vmem,) * 3,
        scratch_shapes=[
            pltpu.SMEM((1,), F32),
            pltpu.SMEM((1,), F32),
            pltpu.VMEM((ROWS, D), BF16),
            pltpu.VMEM((TEXTS, D), BF16),
            pltpu.VMEM((ZLO, QUARTER, D), BF16),
            pltpu.VMEM((SLOTS, PACKED, LANES), BF16),
            pltpu.VMEM((SLOTS, PACKED, LANES), BF16),
            pltpu.VMEM((COLUMNS, D), BF16),
            pltpu.VMEM((IMAGES, D), BF16),
            pltpu.VMEM((IMAGES, COLUMNS), F32),
            pltpu.VMEM((IMAGES, COLUMNS), BF16),
            pltpu.VMEM((IMAGES, D), F32),
            pltpu.VMEM((ZLO, 2, QUARTER, WIDE), F32),
            pltpu.VMEM((COLUMNS, D), F32),
            pltpu.VMEM((4, GROUP, D), BF16),
            pltpu.VMEM((4, GROUP, D), BF16),
            pltpu.VMEM((6, GROUP // 2, D), BF16),
            pltpu.VMEM((6, GROUP // 2, D), BF16),
            pltpu.VMEM((3, PACKED, LANES), BF16),
            pltpu.VMEM((3, PACKED, LANES), BF16),
            pltpu.VMEM((15, QUARTER, WIDE), BF16),
            pltpu.VMEM((15, QUARTER, WIDE), BF16),
            pltpu.VMEM((NY, QUARTER + 8, LANES), F32),
            pltpu.VMEM((NY - 1, QUARTER + 8, LANES), F32),
            pltpu.VMEM((5, 8, LANES), F32),
            pltpu.VMEM((13, 8, LANES), F32),
            pltpu.SemaphoreType.DMA((COPIES,)),
            pltpu.SemaphoreType.DMA((COPIES,)),
            pltpu.SemaphoreType.DMA((4,)),
        ],
        compiler_params=pltpu.CompilerParams(
            collective_id=0, has_side_effects=True, vmem_limit_bytes=VMEM_LIMIT
        ),
    )(log_temp, bias, image_emb, text_emb)
    return (totals[0, :1], grad_image, grad_text, totals[2, :1], totals[1, :1])


def solution(mesh):
    return jax.shard_map(
        shards,
        mesh=mesh,
        in_specs=(P("grp", None), P(("blk", "grp"), None), P(), P()),
        out_specs=(P(), P("grp", "blk"), P(("blk", "grp"), None), P(), P()),
        check_vma=False,
    )
```

```python
import jax
import jax.numpy as jnp
from jax import lax
from jax.experimental import pallas as pl
from jax.experimental.pallas import tpu as pltpu
from jax.sharding import PartitionSpec as P

MESH = pl.DeviceIdType.MESH
epsilon = 1e-06

NX, NY, NZ, ZLO = 4, 4, 16, 8
D = 1152
ROWS = 192
QUARTER = ROWS // NY
IMAGES = ZLO * QUARTER
TEXTS = 24
SLOTS = NX * NY
OWN = SLOTS * TEXTS
COLUMNS = 2 * OWN
GROUP = 4 * TEXTS
LANES = 128
TILES = D // LANES
PACKED = 224
WIDE = D // 2
SLOT = D // 8
BATCH = 12288
STRIDE = 2
Z_SIDES = ((-1, 8), (1, 7))
ORDER = (0, 1, 7, 2, 6, 3, 5, 4)
NEAR = 3
COPIES = 3 + 4 + 12 + 7 + 15 + 4 + 6 + 3 + 3 + 13
F32, BF16 = jnp.float32, jnp.bfloat16
VMEM_LIMIT = 48 * 1024 * 1024


class Peers:
    def __init__(self):
        blk, grp = lax.axis_index("blk"), lax.axis_index("grp")
        z_hi, self.y = blk // NY, blk % NY
        self.core, z_lo, self.x = grp % 2, (grp // 2) % ZLO, grp // (2 * ZLO)
        self.z = z_hi * ZLO + z_lo
        self.sign = 1 - 2 * self.core

    def at(self, x, y, z, core):
        return ((z // ZLO) * NY + y, (x * ZLO + z % ZLO) * 2 + core)

    def other_core(self):
        return self.at(self.x, self.y, self.z, 1 - self.core)

    def along_x(self, step):
        return self.at((self.x + step) % NX, self.y, self.z, self.core)

    def along_y(self, step):
        return self.at(self.x, (self.y + step) % NY, self.z, self.core)

    def first_axis(self, step):
        return self.at(
            (self.x + step * self.core) % NX,
            (self.y + step * (1 - self.core)) % NY,
            self.z,
            self.core,
        )

    def second_axis(self, step):
        return self.at(
            (self.x + step * (1 - self.core)) % NX,
            (self.y + step * self.core) % NY,
            self.z,
            self.core,
        )

    def z_of(self, step):
        return (self.z + self.sign * step + NZ) % NZ

    def along_z(self, step):
        return self.at(self.x, self.y, self.z_of(step), self.core)


class Copies:
    def __init__(self, send_sem, recv_sem):
        self.send_sem, self.recv_sem, self.made = send_sem, recv_sem, []
        self.sent = 0

    def start(self, source, target, device_id):
        at = len(self.made)
        copy = pltpu.make_async_remote_copy(
            src_ref=source,
            dst_ref=target,
            send_sem=self.send_sem.at[at],
            recv_sem=self.recv_sem.at[at],
            device_id=device_id,
            device_id_type=MESH,
        )
        copy.start()
        self.made.append(copy)
        return copy

    def finish(self):
        for copy in self.made[self.sent :]:
            copy.wait_send()
        self.sent = len(self.made)


def pack(rows):
    pieces = [rows[:, k * LANES : (k + 1) * LANES] for k in range(TILES)]
    pieces.append(jnp.zeros((PACKED - TILES * TEXTS, LANES), F32))
    return jnp.concatenate(pieces, axis=0)


def unpack(packed):
    return jnp.concatenate(
        [packed[k * TEXTS : (k + 1) * TEXTS, :] for k in range(TILES)], axis=1
    )


def row_inverse(values):
    return lax.rsqrt(jnp.sum(values * values, axis=1, keepdims=True) + epsilon)


def narrow(rows):
    pieces = [rows[8 * k : 8 * k + 8, LANES:] for k in range(QUARTER // 8)]
    pieces.append(jnp.zeros((8, LANES - (SLOT - LANES) * QUARTER // 8), F32))
    return jnp.concatenate([rows[:, :LANES], jnp.concatenate(pieces, axis=1)], axis=0)


def widen(packed):
    rest = SLOT - LANES
    pieces = [packed[QUARTER:, rest * k : rest * (k + 1)] for k in range(QUARTER // 8)]
    return jnp.concatenate([packed[:QUARTER, :], jnp.concatenate(pieces, axis=0)], axis=1)


def hop(distance):
    return distance % STRIDE or STRIDE


def aligned(start, size):
    return pl.ds(pl.multiple_of(start, size), size)


def kernel(
    log_temp_in,
    bias_in,
    image_in,
    text_in,
    grad_image,
    grad_text,
    totals,
    log_temp,
    bias,
    image,
    text,
    images,
    own_texts,
    other_texts,
    text_bf,
    image_bf,
    similar,
    weights,
    grads,
    halves,
    text_part,
    core_send,
    core_land,
    b_send,
    b_land,
    a_send,
    a_land,
    z_send,
    z_land,
    y_send,
    y_land,
    s_send,
    s_land,
    send_sem,
    recv_sem,
    local_sem,
):
    peers = Peers()
    copies = Copies(send_sem, recv_sem)
    x, y, z, core = peers.x, peers.y, peers.z, peers.core

    image_copy = pltpu.make_async_copy(image_in, image, local_sem.at[0])
    text_copy = pltpu.make_async_copy(text_in, text, local_sem.at[1])
    scalar_copies = [
        pltpu.make_async_copy(log_temp_in, log_temp, local_sem.at[2]),
        pltpu.make_async_copy(bias_in, bias, local_sem.at[3]),
    ]
    for copy in (text_copy, image_copy, *scalar_copies):
        copy.start()
    barrier = pltpu.get_barrier_semaphore()
    met = (
        [peers.other_core()]
        + [peers.along_x(step) for step in range(1, NX)]
        + [peers.along_y(step) for step in range(1, NY)]
        + [peers.along_z(step) for step in (-4, -3, -2, -1, 1, 2, 3, 4, 8)]
    )
    for device_id in met:
        pl.semaphore_signal(barrier, inc=1, device_id=device_id, device_id_type=MESH)
    text_copy.wait()
    own_texts[0] = pack(text[...].astype(F32)).astype(BF16)
    image_copy.wait()
    images[0] = image[aligned(y * QUARTER, QUARTER), :]
    for copy in scalar_copies:
        copy.wait()
    def image_ready(place):
        rows = pl.ds(place * QUARTER, QUARTER)
        values = images[place].astype(F32)
        image_bf[rows, :] = (values * row_inverse(values)).astype(BF16)

    image_ready(0)
    quarters = [aligned(((y + k) % NY) * QUARTER, QUARTER) for k in range(NY)]
    inverses = [row_inverse(image[rows, :].astype(F32)) for rows in quarters]

    pl.semaphore_wait(barrier, len(met))

    crossing, over_core, over_z = {}, {}, {}

    def text_forward(b):
        slots = pl.ds(4 * b, 4)
        over_core[b] = copies.start(
            own_texts.at[slots], other_texts.at[slots], peers.other_core()
        )

    def text_spread(a):
        crossing[a, 1] = copies.start(own_texts.at[a], own_texts.at[4 + a], peers.second_axis(3))
        crossing[a, 3] = copies.start(own_texts.at[a], own_texts.at[12 + a], peers.second_axis(1))

    def image_forward(distance, side):
        source = (distance if side > 0 else ZLO - distance) % ZLO
        target = (distance + 1 if side > 0 else ZLO - distance - 1) % ZLO
        over_z[target] = copies.start(
            images.at[ORDER.index(source)], images.at[ORDER.index(target)], peers.along_z(-side)
        )

    crossing[1, 0] = copies.start(own_texts.at[0], own_texts.at[1], peers.first_axis(3))
    crossing[3, 0] = copies.start(own_texts.at[0], own_texts.at[3], peers.first_axis(1))
    crossing[2, 0] = copies.start(own_texts.at[0], own_texts.at[2], peers.first_axis(2))
    image_forward(0, 1)
    image_forward(0, -1)
    text_spread(0)

    def texts_ready(texts, b, first):
        for half in range(2):
            slot = b * 4 + 2 * half
            rows = jnp.concatenate(
                [unpack(texts[slot + k].astype(F32)) for k in range(2)], axis=0
            )
            text_bf[pl.ds(first + slot * TEXTS, 2 * TEXTS), :] = (
                rows * row_inverse(rows)
            ).astype(BF16)

    for a in (1, 3, 2):
        crossing[a, 0].wait_recv()
        text_spread(a)
    text_forward(0)
    for target, side in ((1, 1), (7, -1)):
        over_z[target].wait_recv()
        image_forward(1, side)
    texts_ready(own_texts, 0, 0)
    image_ready(1)
    image_ready(2)
    for a in (0, 1, 3, 2):
        for b in (1, 3):
            crossing[a, b].wait_recv()
            if (b == 1) == (a in (0, 3)):
                step = 3 if b == 1 else 1
                crossing[a, 2] = copies.start(
                    own_texts.at[b * 4 + a], own_texts.at[8 + a], peers.second_axis(step)
                )
    text_forward(1)
    text_forward(3)
    for target, side in ((2, 1), (6, -1)):
        over_z[target].wait_recv()
        image_forward(2, side)
    texts_ready(own_texts, 1, 0)
    texts_ready(own_texts, 3, 0)

    def others_ready(b):
        over_core[b].wait_recv()
        texts_ready(other_texts, b, OWN)

    others_ready(0)
    for a in (0, 1, 3, 2):
        crossing[a, 2].wait_recv()
    text_forward(2)
    texts_ready(own_texts, 2, 0)
    others_ready(1)
    others_ready(3)

    scale = jnp.exp(jnp.full((1, 1), log_temp[0], F32))
    shift = bias[0]
    column = lax.broadcasted_iota(jnp.int32, (1, COLUMNS), 1)
    block = (column * 2731) >> 16
    text_core = ((block >> 4) + core) & 1
    on_first, on_second = block & 3, (block >> 2) & 3
    text_x = (x + jnp.where(text_core == 0, on_second, on_first)) & (NX - 1)
    text_y = (y + jnp.where(text_core == 0, on_first, on_second)) & (NY - 1)
    text_ids = (
        ((z // ZLO) * NY + text_y) * (BATCH // 8)
        + ((text_x * ZLO + z % ZLO) * 2 + text_core) * TEXTS
        + column
        - block * TEXTS
    )

    def weigh(low, high, lanes, carry):
        rows = pl.ds(low * QUARTER, (high - low) * QUARTER)
        similar[rows, lanes] = lax.dot_general(
            image_bf[rows, :],
            text_bf[lanes, :],
            (((1,), (1,)), ((), ())),
            preferred_element_type=F32,
        )
        ids = text_ids[:, lanes.start : lanes.start + lanes.size]

        def step(place, carry):
            losses, dlogits, weighted = carry
            rows = aligned(place * QUARTER, QUARTER)
            distance = ((place + 1) // 2) * (2 * (place % 2) - 1)
            image_z = (z + peers.sign * distance + NZ) % ZLO
            first = ((x * ZLO + image_z) * 2 + core) * ROWS + y * QUARTER
            same = first + lax.broadcasted_iota(jnp.int32, (QUARTER, 1), 0) == ids
            product = similar[rows, lanes]
            logits = scale * product + shift
            power = jnp.exp(jnp.where(same, -logits, logits))
            above = 1.0 + power
            chance = power / above
            dlogit = jnp.where(same, -chance, chance)
            weights[rows, lanes] = (scale * dlogit).astype(BF16)
            losses = losses + jnp.sum(jnp.log(above), axis=0, keepdims=True)
            dlogits = dlogits + jnp.sum(dlogit, axis=0, keepdims=True)
            weighted = weighted + jnp.sum(dlogit * product, axis=0, keepdims=True)
            return losses, dlogits, weighted

        return lax.fori_loop(low, high, step, carry)

    def project(place):
        values = images[place].astype(F32)
        unit = values * row_inverse(values)
        grad = grads[aligned(place * QUARTER, QUARTER), :]
        grad = grad - unit * jnp.sum(unit * grad, axis=1, keepdims=True)
        halves[place, 0] = grad[:, :WIDE]
        halves[place, 1] = grad[:, WIDE:]

    def image_grads(low, high):
        rows = pl.ds(low * QUARTER, (high - low) * QUARTER)
        grads[rows, :] = jnp.dot(weights[rows, :], text_bf[...], preferred_element_type=F32)
        for place in range(low, high):
            project(place)

    index = {}
    for side, most in Z_SIDES:
        for far in range(most, 0, -1):
            index[side, far] = len(index)
    flying = {}

    def part(step):
        return halves[ORDER.index(step % ZLO), peers.z_of(step) // ZLO]

    def gathered(side, most, to, value):
        for far in range(to + 1, min(to + STRIDE, most) + 1):
            flying[side, far].wait_recv()
            value = value + z_land[index[side, far]].astype(F32)
        return value

    def z_start(far):
        for side, most in Z_SIDES:
            if far > most:
                continue
            value = part(side * far)
            if far % STRIDE == 0:
                value = gathered(side, most, far, value)
            at = index[side, far]
            z_send[at] = value.astype(BF16)
            flying[side, far] = copies.start(
                z_send.at[at], z_land.at[at], peers.along_z(side * hop(far))
            )

    scalar = {"stage": 0, "slot": 0, "value": None}

    def scalar_send(value, to):
        stage = scalar["stage"]
        scalar["value"] = value
        s_send[stage] = value
        made = []
        for peer in to:
            slot = scalar["slot"]
            made.append((copies.start(s_send.at[stage], s_land.at[slot], peer), slot))
            scalar["slot"] += 1
        scalar["stage"] += 1
        return made

    def scalar_sum(made):
        value = scalar["value"]
        for copy, slot in made:
            copy.wait_recv()
            value = value + s_land[slot]
        return value

    own_lanes, other_lanes = pl.ds(0, OWN), pl.ds(OWN, OWN)
    zero = jnp.zeros((1, OWN), F32)
    carry = weigh(0, NEAR, own_lanes, (zero, zero, zero))
    over_z[3].wait_recv()
    image_forward(3, 1)
    others_ready(2)
    carry = weigh(0, NEAR, other_lanes, carry)
    image_grads(0, NEAR)
    for far in (8, 7, 1):
        z_start(far)
    for place in (3, 4, 5):
        image_ready(place)
    over_z[5].wait_recv()
    image_ready(6)
    over_z[4].wait_recv()
    image_ready(7)
    wide_zero = jnp.zeros((1, COLUMNS), F32)
    late = weigh(NEAR, ZLO, pl.ds(0, COLUMNS), (wide_zero, wide_zero, wide_zero))

    row = lax.broadcasted_iota(jnp.int32, (8, LANES), 0)
    total = jnp.zeros((8, LANES), F32)
    for k in range(3):
        part_sum = jnp.sum(carry[k], axis=1, keepdims=True)
        part_sum = part_sum + jnp.sum(late[k], axis=1, keepdims=True)
        total = jnp.where(row == k, part_sum, total)
    made = scalar_send(total, [peers.other_core()])

    def text_product(lanes):
        text_part[lanes, :] = lax.dot_general(
            weights[:, lanes],
            image_bf[...],
            (((0,), (0,)), ((), ())),
            preferred_element_type=F32,
        )

    text_product(other_lanes)
    pairs = {}
    for b in (2, 1, 3, 0):
        core_send[b] = text_part[pl.ds(OWN + b * GROUP, GROUP), :].astype(BF16)
        pairs[b] = copies.start(core_send.at[b], core_land.at[b], peers.other_core())
    image_grads(NEAR, ZLO)
    for far in (6, 5, 3):
        z_start(far)
    made = scalar_send(scalar_sum(made), [peers.along_x(step) for step in range(1, NX)])
    text_product(own_lanes)
    made = scalar_send(scalar_sum(made), [peers.along_y(step) for step in range(1, NY)])

    ready = set()

    def pair_sum(b, half):
        if b not in ready:
            pairs[b].wait_recv()
            ready.add(b)
        first = half * (GROUP // 2)
        mine = text_part[pl.ds(b * GROUP + first, GROUP // 2), :]
        return mine + core_land[b, pl.ds(first, GROUP // 2), :].astype(F32)

    across = {}

    def b_start(at, value, step):
        b_send[at] = value.astype(BF16)
        across[at] = copies.start(b_send.at[at], b_land.at[at], peers.second_axis(step))

    def b_landed(at):
        across[at].wait_recv()
        return b_land[at].astype(F32)

    b_start(0, pair_sum(2, 0), 1)
    b_start(1, pair_sum(2, 1), 3)
    b_start(2, pair_sum(1, 1), 1)
    b_start(3, pair_sum(3, 0), 3)
    made = scalar_send(scalar_sum(made), [peers.along_z(step) for step in (4, 8, -4)])
    z_start(4)
    b_start(4, pair_sum(1, 0) + b_landed(0), 1)
    b_start(5, pair_sum(3, 1) + b_landed(1), 3)
    z_start(2)
    last = []

    def a_start(a, rows):
        a_send[a - 1] = pack(rows).astype(BF16)
        last.append((copies.start(a_send.at[a - 1], a_land.at[3 - a], peers.first_axis(a)), 3 - a))

    rows = pair_sum(0, 1) + b_landed(2) + b_landed(5)
    a_start(2, rows[:TEXTS])
    a_start(3, rows[TEXTS:])
    rows = pair_sum(0, 0) + b_landed(3) + b_landed(4)
    a_start(1, rows[TEXTS:])
    text_sum = pack(rows[:TEXTS])
    text_values = text[...].astype(F32)
    text_inverse = row_inverse(text_values)
    text_unit = text_values * text_inverse
    made = scalar_send(scalar_sum(made), [peers.along_z(step) for step in (1, 2, 3)])
    grad = part(0)
    for side, most in Z_SIDES:
        grad = gathered(side, most, 0, grad)
    for k in range(NY):
        y_send[k] = narrow(grad[:, k * SLOT : (k + 1) * SLOT])
    over_y = {}
    for step in (2, 1, 3):
        over_y[NY - step] = copies.start(
            y_send.at[(y + step) % NY], y_land.at[NY - step - 1], peers.along_y(step)
        )
    grad_image[quarters[0], :] = widen(y_send[y]) * inverses[0]
    copies.finish()

    for copy, slot in last:
        copy.wait_recv()
        text_sum = text_sum + a_land[slot].astype(F32)
    text_sum = unpack(text_sum)
    inner = jnp.sum(text_unit * text_sum, axis=1, keepdims=True)
    grad_text[...] = (text_sum - text_unit * inner) * text_inverse
    for k in range(1, NY):
        over_y[k].wait_recv()
        grad_image[quarters[k], :] = widen(y_land[k - 1]) * inverses[k]
    factor = jnp.where(row == 0, 1.0 / BATCH, jnp.where(row == 2, scale, 1.0))
    totals[...] = scalar_sum(made) * factor
    copies.finish()


def shards(image_emb, text_emb, log_temp, bias):
    vmem = pl.BlockSpec(memory_space=pltpu.VMEM)
    anywhere = pl.BlockSpec(memory_space=pl.ANY)
    grad_image, grad_text, totals = pl.pallas_call(
        kernel,
        out_shape=(
            jax.ShapeDtypeStruct((ROWS, SLOT), F32),
            jax.ShapeDtypeStruct((TEXTS, D), F32),
            jax.ShapeDtypeStruct((8, LANES), F32),
        ),
        in_specs=[anywhere] * 4,
        out_specs=(vmem,) * 3,
        scratch_shapes=[
            pltpu.SMEM((1,), F32),
            pltpu.SMEM((1,), F32),
            pltpu.VMEM((ROWS, D), BF16),
            pltpu.VMEM((TEXTS, D), BF16),
            pltpu.VMEM((ZLO, QUARTER, D), BF16),
            pltpu.VMEM((SLOTS, PACKED, LANES), BF16),
            pltpu.VMEM((SLOTS, PACKED, LANES), BF16),
            pltpu.VMEM((COLUMNS, D), BF16),
            pltpu.VMEM((IMAGES, D), BF16),
            pltpu.VMEM((IMAGES, COLUMNS), F32),
            pltpu.VMEM((IMAGES, COLUMNS), BF16),
            pltpu.VMEM((IMAGES, D), F32),
            pltpu.VMEM((ZLO, 2, QUARTER, WIDE), F32),
            pltpu.VMEM((COLUMNS, D), F32),
            pltpu.VMEM((4, GROUP, D), BF16),
            pltpu.VMEM((4, GROUP, D), BF16),
            pltpu.VMEM((6, GROUP // 2, D), BF16),
            pltpu.VMEM((6, GROUP // 2, D), BF16),
            pltpu.VMEM((3, PACKED, LANES), BF16),
            pltpu.VMEM((3, PACKED, LANES), BF16),
            pltpu.VMEM((15, QUARTER, WIDE), BF16),
            pltpu.VMEM((15, QUARTER, WIDE), BF16),
            pltpu.VMEM((NY, QUARTER + 8, LANES), F32),
            pltpu.VMEM((NY - 1, QUARTER + 8, LANES), F32),
            pltpu.VMEM((5, 8, LANES), F32),
            pltpu.VMEM((13, 8, LANES), F32),
            pltpu.SemaphoreType.DMA((COPIES,)),
            pltpu.SemaphoreType.DMA((COPIES,)),
            pltpu.SemaphoreType.DMA((4,)),
        ],
        compiler_params=pltpu.CompilerParams(
            collective_id=0, has_side_effects=True, vmem_limit_bytes=VMEM_LIMIT
        ),
    )(log_temp, bias, image_emb, text_emb)
    return (totals[0, :1], grad_image, grad_text, totals[2, :1], totals[1, :1])


def solution(mesh):
    return jax.shard_map(
        shards,
        mesh=mesh,
        in_specs=(P("grp", None), P(("blk", "grp"), None), P(), P()),
        out_specs=(P(), P("grp", "blk"), P(("blk", "grp"), None), P(), P()),
        check_vma=False,
    )
```
